32 devices in a mesh: fsdp: 8 (over y, x, core), tensor: 4 (over z).
Axes of the slice: x: 2, y: 2, z: 4, core: 2. Of those that a mesh axis runs over, the one named last changes fastest.
Arguments:
- normed: bfloat16 [8192, 8192], P('fsdp', 'tensor')
- tile_values: bfloat16 [4, 128, 128, 128], P('tensor', 'fsdp'), may hold values from -0.09375 to 0.09375
- tile_rows: int32 [4, 128], P('tensor', 'fsdp'), may hold values from -1 to 15, as said below
- tile_columns: int32 [4, 128], P('tensor', 'fsdp'), may hold values from -1 to 7, as said below
- cotangent: bfloat16 [8192, 1024], P('fsdp', 'tensor')
Outputs:
- values: bfloat16 [8192, 1024], P('fsdp', 'tensor')
- grad_input: bfloat16 [8192, 8192], P('fsdp', 'tensor')
- tile_update: bfloat16 [4, 128, 128, 128], P('tensor', 'fsdp')
The draws below stay inside these ranges and needn't reach their ends.
Inputs may be any that keep to these rules, and one draw needn't show every extreme that they name: tile_rows[q, s] is -1 exactly where tile_columns[q, s] is -1 (an empty slot). In every part q exactly 64 slots are filled, no (row block, column block) pair appears twice, and each column block holds exactly 8 of the 16 row blocks. The slots s with equal s // 16 belong to one owner; in every part some owner has all 16 of its slots filled. `tile_columns`: column block of the tile in each slot; -1 marks an empty slot, as in tile_rows.
All inputs are finite; a program needn't handle non-finite values.
Results may differ from the reference program's by a relative error of at most 0.001.
Values may be sent and summed in bfloat16 or wider, within the bound.
No kernel may reach another device: no remote copies, remote signals or barrier semaphores. Data moves between devices by JAX's collectives and lax.ppermute only.
A program may use at most 128 MiB of HBM per device.

```python
import jax
import jax.numpy as jnp
from jax import lax

D = 8192
KVW = 1024
TILE = 128
QUARTERS = 4
RB = 16
CB = 8
KEPT = 64
CAP = 16
SLOTS = 128
TOKENS = 8192


def feature_draw(key, row_total, feature_total):
    noise_key, scale_key = jax.random.split(key, 2)
    scales = jnp.exp(jax.random.uniform(scale_key, (feature_total,), jnp.float32, -1.15, 1.15))
    noise = jax.random.normal(noise_key, (row_total, feature_total), jnp.float32)
    return (noise * scales[None, :]).astype(jnp.bfloat16)


def draw_normed(key, part):
    return feature_draw(jax.random.fold_in(key, 3), TOKENS, D)


def draw_cotangent(key, part):
    return feature_draw(jax.random.fold_in(key, 5), TOKENS, KVW)


def quarter_layout(quarter_key):
    pick_key, shuffle_key, owner_key, spread_key = jax.random.split(quarter_key, 4)
    column_keys = jax.random.split(pick_key, CB)
    picked_rows = jax.vmap(lambda subkey: jax.random.permutation(subkey, RB)[:RB // 2])(column_keys)
    row_list = picked_rows.reshape(-1).astype(jnp.int32)
    column_list = jnp.repeat(jnp.arange(CB, dtype=jnp.int32), RB // 2)
    shuffle = jax.random.permutation(shuffle_key, KEPT)
    row_list = row_list[shuffle]
    column_list = column_list[shuffle]
    owner_total = SLOTS // CAP
    full_owner = jax.random.randint(owner_key, (), 0, owner_total)
    spread = jax.random.permutation(spread_key, (owner_total - 1) * CAP)
    inverse = jnp.argsort(spread).astype(jnp.int32)
    slot_ids = jnp.arange(SLOTS, dtype=jnp.int32)
    owners = slot_ids // CAP
    other_position = slot_ids - jnp.where(owners > full_owner, CAP, 0)
    other_rank = inverse[jnp.clip(other_position, 0, (owner_total - 1) * CAP - 1)]
    tile_index = jnp.where(owners == full_owner, slot_ids % CAP, CAP + other_rank)
    occupied = tile_index < KEPT
    safe_index = jnp.clip(tile_index, 0, KEPT - 1)
    slot_rows = jnp.where(occupied, row_list[safe_index], -1)
    slot_columns = jnp.where(occupied, column_list[safe_index], -1)
    return (slot_rows.astype(jnp.int32), slot_columns.astype(jnp.int32))


def tile_layout(key):
    base_key = jax.random.fold_in(key, 11)
    quarter_keys = jax.vmap(lambda index: jax.random.fold_in(base_key, index))(jnp.arange(QUARTERS))
    return jax.vmap(quarter_layout)(quarter_keys)


def draw_tile_rows(key, part):
    return tile_layout(key)[0]


def draw_tile_columns(key, part):
    return tile_layout(key)[1]


def shard_levels(rng, shape, shards, least, top_value):
    def one(position, blocks):
        draws = jax.random.uniform(jax.random.fold_in(jax.random.fold_in(rng, 6), position), (blocks,), jnp.float32, least / len(shards), top_value / len(shards))
        return jnp.repeat(jnp.exp(draws), shape[position] // blocks).reshape((-1,) + (1,) * (len(shape) - position - 1))

    factor_of = one(*shards[0])
    for cut in shards[1:]:
        factor_of = factor_of * one(*cut)
    return factor_of


def gaussian(key, extent, scale, reach, pieces=(), kind=jnp.bfloat16):
    entries = scale * jax.random.normal(key, extent, jnp.float32)
    if pieces:
        entries = entries * shard_levels(key, extent, pieces, -0.22, 0.18)
    return jnp.clip(entries, -reach, reach).astype(kind)


def setup_inputs(seed: int = 0) -> dict:
    arg_keys = jax.random.split(jax.random.key(seed), 6)
    normed = draw_normed(jax.random.fold_in(arg_keys[5], 71), 0)
    tile_values = gaussian(arg_keys[1], (QUARTERS, SLOTS, TILE, TILE), (D // 2) ** -0.5, 0.09375, ((0, 4), (1, 8)))
    tile_rows = draw_tile_rows(jax.random.fold_in(arg_keys[5], 71), 0)
    tile_columns = draw_tile_columns(jax.random.fold_in(arg_keys[5], 71), 0)
    cotangent = draw_cotangent(jax.random.fold_in(arg_keys[5], 71), 0)
    return {"normed": normed, "tile_values": tile_values, "tile_rows": tile_rows, "tile_columns": tile_columns, "cotangent": cotangent}


def reference(normed, tile_values, tile_rows, tile_columns, cotangent):
    occupied = tile_columns >= 0
    global_rows = jnp.arange(QUARTERS, dtype=jnp.int32)[:, None] * RB + jnp.maximum(tile_rows, 0)
    pair_index = (global_rows * CB + jnp.maximum(tile_columns, 0)).reshape(-1)
    masked = jnp.where(occupied[:, :, None, None], tile_values.astype(jnp.float32), 0.0).reshape(-1, TILE, TILE)
    blocks = jnp.zeros((D // TILE * CB, TILE, TILE), jnp.float32).at[pair_index].add(masked)
    weight = blocks.reshape(D // TILE, CB, TILE, TILE).transpose(0, 2, 1, 3).reshape(D, KVW).astype(jnp.bfloat16)
    values = jnp.dot(normed, weight, preferred_element_type=jnp.float32).astype(jnp.bfloat16)
    grad_input = jnp.dot(cotangent, weight.T, preferred_element_type=jnp.float32).astype(jnp.bfloat16)
    gradient = jnp.dot(normed.T, cotangent, preferred_element_type=jnp.float32)
    grad_blocks = gradient.reshape(D // TILE, TILE, CB, TILE).transpose(0, 2, 1, 3).reshape(-1, TILE, TILE)
    picked = jnp.where(occupied.reshape(-1)[:, None, None], jnp.take(grad_blocks, pair_index, axis=0), 0.0)
    inverse_rms = lax.rsqrt(lax.optimization_barrier(jnp.mean(picked * picked, axis=(1, 2), keepdims=True)) + 1e-06)
    tile_update = (picked * inverse_rms).astype(jnp.bfloat16).reshape(QUARTERS, SLOTS, TILE, TILE)
    return (values, grad_input, tile_update)
```

```python
import functools

import jax
import jax.numpy as jnp
from jax import lax
from jax.experimental import pallas as pl
from jax.experimental.pallas import tpu as pltpu
from jax.sharding import PartitionSpec as P

VMEM_BYTES = 48 * 1024 * 1024
GROUP = 128
PAD = 16


def encode(block):
    peak = jnp.max(jnp.abs(block), axis=0, keepdims=True)
    exponent = jnp.floor(jnp.log2(jnp.maximum(peak, 2.0**-100))) + 1.0
    exponent = jnp.clip(exponent, -100.0, 128.0)
    scaled = jnp.round(block * jnp.exp2(15.0 - exponent))
    codes = jnp.clip(scaled, -32767.0, 32767.0).astype(jnp.int32).astype(jnp.int16)
    return codes, exponent


def decode(codes, exponent):
    return codes.astype(jnp.int32).astype(jnp.float32) * jnp.exp2(exponent - 15.0)


def as_code(exponents):
    return exponents.astype(jnp.int32).astype(jnp.int16)


def exponent_rows(codes):
    return codes.astype(jnp.int32).astype(jnp.float32)


def params():
    return pltpu.CompilerParams(vmem_limit_bytes=VMEM_BYTES)


def whole(shape):
    zeros = (0,) * len(shape)
    return pl.BlockSpec(shape, lambda *_: zeros, pipeline_mode=pl.Buffered(1))


def aligned(index, size):
    return pl.ds(pl.multiple_of(index * size, size), size)


def write_message(message_ref, rows, blocks):
    place = lax.broadcasted_iota(jnp.int32, (PAD, message_ref.shape[1]), 0)
    exponents = jnp.zeros((PAD, message_ref.shape[1]), jnp.float32)
    for group in range(rows // GROUP):
        codes, exponent = encode(blocks(group))
        message_ref[group * GROUP : (group + 1) * GROUP, :] = codes
        exponents = jnp.where(place == group, exponent, exponents)
    message_ref[rows : rows + PAD, :] = as_code(exponents)


def read_message(message_ref, rows):
    exponents = exponent_rows(message_ref[rows : rows + PAD, :])

    def block(group):
        return decode(
            message_ref[group * GROUP : (group + 1) * GROUP, :], exponents[group : group + 1, :]
        )

    return block


def values_kernel(devices, column_blocks, codes_ref, place_ref, normed_ref, *refs):
    tile_refs = refs[:devices]
    partial_ref, first_ref, transposed_ref, weight = refs[devices:]
    step = pl.program_id(0)
    chunks, block, chunk_width = partial_ref.shape
    tile = tile_refs[0].shape[-1]

    @pl.when(step == 0)
    def _():
        weight[...] = jnp.zeros_like(weight)
        transposed_ref[...] = jnp.zeros_like(transposed_ref)
        for k in range(devices):

            @pl.loop(0, tile_refs[k].shape[0])
            def _(slot):
                code = codes_ref[k, slot]

                @pl.when(code >= 0)
                def _():
                    row = aligned(code // column_blocks, tile)
                    column = aligned(code % column_blocks, tile)
                    values = tile_refs[k][slot]
                    weight[row, column] = values
                    transposed_ref[column, row] = values.T

    left = normed_ref[...]
    for chunk in range(chunks):
        partial_ref[chunk] = jnp.dot(
            left,
            weight[:, chunk * chunk_width : (chunk + 1) * chunk_width],
            preferred_element_type=jnp.float32,
        )

    rows = first_ref.shape[0] - PAD
    far = chunks - 1 - place_ref[0]
    place = lax.broadcasted_iota(jnp.int32, (PAD, chunk_width), 0)
    old = exponent_rows(first_ref[rows : rows + PAD, :])
    exponents = jnp.where(step == 0, 0.0, old)
    for group in range(block // GROUP):
        codes, exponent = encode(partial_ref[far, group * GROUP : (group + 1) * GROUP, :])
        first_ref[aligned(step * (block // GROUP) + group, GROUP), :] = codes
        exponents = jnp.where(place == step * (block // GROUP) + group, exponent, exponents)
    first_ref[rows : rows + PAD, :] = as_code(exponents)


def partial_values(codes, place, normed, tiles, chunks, column_blocks):
    tokens, features = normed.shape
    tile = tiles[0].shape[-1]
    width = column_blocks * tile
    block = 256
    return pl.pallas_call(
        functools.partial(values_kernel, len(tiles), column_blocks),
        grid_spec=pltpu.PrefetchScalarGridSpec(
            num_scalar_prefetch=2,
            grid=(tokens // block,),
            in_specs=[pl.BlockSpec((block, features), lambda i, *_: (i, 0))]
            + [whole(t.shape) for t in tiles],
            out_specs=[
                pl.BlockSpec((chunks, block, width // chunks), lambda i, *_: (0, i, 0)),
                whole((tokens + PAD, width // chunks)),
                whole((width, features)),
            ],
            scratch_shapes=[pltpu.VMEM((features, width), jnp.bfloat16)],
        ),
        out_shape=[
            jax.ShapeDtypeStruct((chunks, tokens, width // chunks), jnp.float32),
            jax.ShapeDtypeStruct((tokens + PAD, width // chunks), jnp.int16),
            jax.ShapeDtypeStruct((width, features), jnp.bfloat16),
        ],
        compiler_params=params(),
        cost_estimate=pl.CostEstimate(
            flops=2 * tokens * features * width,
            bytes_accessed=20 * 1024 * 1024,
            transcendentals=0,
        ),
        name="partial_values",
    )(codes, place, normed, *tiles)


def hop_kernel(chunk_ref, partial_ref, arrived_ref, message_ref):
    rows = partial_ref.shape[1]
    arrived = read_message(arrived_ref, rows)

    def total(group):
        return partial_ref[0, group * GROUP : (group + 1) * GROUP, :] + arrived(group)

    write_message(message_ref, rows, total)


def hop(chunk, partial, arrived):
    _, tokens, width = partial.shape
    return pl.pallas_call(
        hop_kernel,
        grid_spec=pltpu.PrefetchScalarGridSpec(
            num_scalar_prefetch=1,
            grid=(1,),
            in_specs=[
                pl.BlockSpec((1, tokens, width), lambda i, c: (c[0], 0, 0)),
                whole(arrived.shape),
            ],
            out_specs=whole(arrived.shape),
        ),
        out_shape=jax.ShapeDtypeStruct(arrived.shape, jnp.int16),
        compiler_params=params(),
        cost_estimate=pl.CostEstimate(
            flops=8 * tokens * width, bytes_accessed=8 * tokens * width, transcendentals=0
        ),
        name="hop",
    )(chunk, partial, arrived)


def last_hop_kernel(chunk_ref, partial_ref, right_ref, left_ref, values_ref):
    rows = partial_ref.shape[1]
    right = read_message(right_ref, rows)
    left = read_message(left_ref, rows)
    for group in range(rows // GROUP):
        span = slice(group * GROUP, (group + 1) * GROUP)
        total = partial_ref[0, span, :] + right(group) + left(group)
        values_ref[span, :] = total.astype(values_ref.dtype)


def last_hop(chunk, partial, right, left):
    _, tokens, width = partial.shape
    return pl.pallas_call(
        last_hop_kernel,
        grid_spec=pltpu.PrefetchScalarGridSpec(
            num_scalar_prefetch=1,
            grid=(1,),
            in_specs=[
                pl.BlockSpec((1, tokens, width), lambda i, c: (c[0], 0, 0)),
                whole(right.shape),
                whole(left.shape),
            ],
            out_specs=whole((tokens, width)),
        ),
        out_shape=jax.ShapeDtypeStruct((tokens, width), jnp.bfloat16),
        compiler_params=params(),
        cost_estimate=pl.CostEstimate(
            flops=8 * tokens * width, bytes_accessed=10 * tokens * width, transcendentals=0
        ),
        name="last_hop",
    )(chunk, partial, right, left)


def gradient_kernel(
    chips, column_blocks, codes_ref, place_ref, normed_ref, own, r1, r2, r3, l1, l2, l3, *refs
):
    keep_refs = refs[:chips]
    send_refs = refs[chips : 2 * chips]
    cotangent_ref, turned, gradient = refs[2 * chips :]
    chunk_width = own.shape[1]
    chunks = cotangent_ref.shape[1] // chunk_width
    pieces = (own[...], l1[...] + r3[...], l2[...] + r2[...], r1[...] + l3[...])
    for r in range(chunks):
        span = aligned(lax.rem(place_ref[0] + r, chunks), chunk_width)
        cotangent_ref[:, span] = pieces[r]
        turned[span, :] = pieces[r].T
    step = 256
    for n in range(normed_ref.shape[1] // step):
        span = slice(n * step, (n + 1) * step)
        gradient[:, span] = jnp.dot(
            turned[...], normed_ref[:, span], preferred_element_type=jnp.float32
        )
    tile = 128
    capacity = codes_ref.shape[1]

    def term(k, slot):
        code = codes_ref[k, slot]
        safe = jnp.maximum(code, 0)
        block = gradient[aligned(safe % column_blocks, tile), aligned(safe // column_blocks, tile)]
        return jnp.where(code >= 0, block, 0.0)

    for chip in range(chips):
        for slot in range(capacity):
            keep_refs[chip][slot * tile : (slot + 1) * tile, :] = term(2 * chip, slot)
        write_message(
            send_refs[chip], capacity * tile, lambda slot: term(2 * chip + 1, slot)
        )


def gradient_terms(codes, place, normed, own, rights, lefts, column_blocks):
    tokens, features = normed.shape
    chips = codes.shape[0] // 2
    capacity = codes.shape[1]
    rows = capacity * GROUP
    width = column_blocks * GROUP
    inputs = (normed, own, *rights, *lefts)
    shapes = (
        [((rows, GROUP), jnp.float32)] * chips
        + [((rows + PAD, GROUP), jnp.int16)] * chips
        + [((tokens, width), jnp.bfloat16)]
    )
    outputs = pl.pallas_call(
        functools.partial(gradient_kernel, chips, column_blocks),
        grid_spec=pltpu.PrefetchScalarGridSpec(
            num_scalar_prefetch=2,
            grid=(1,),
            in_specs=[whole(a.shape) for a in inputs],
            out_specs=[whole(shape) for shape, _ in shapes],
            scratch_shapes=[
                pltpu.VMEM((width, tokens), jnp.bfloat16),
                pltpu.VMEM((width, features), jnp.float32),
            ],
        ),
        out_shape=[jax.ShapeDtypeStruct(shape, kind) for shape, kind in shapes],
        compiler_params=params(),
        cost_estimate=pl.CostEstimate(
            flops=2 * tokens * features * width,
            bytes_accessed=16 * 1024 * 1024,
            transcendentals=0,
        ),
        name="gradient_terms",
    )(codes, place, *inputs)
    return outputs[:chips], outputs[chips : 2 * chips], outputs[-1]


def combine_kernel(kept_ref, arrived_ref, out_ref):
    rows = kept_ref.shape[0]
    arrived = read_message(arrived_ref, rows)

    def total(group):
        return kept_ref[group * GROUP : (group + 1) * GROUP, :] + arrived(group)

    if out_ref.dtype == jnp.int16:
        write_message(out_ref, rows, total)
    else:
        for group in range(rows // GROUP):
            out_ref[group * GROUP : (group + 1) * GROUP, :] = total(group)


def combine(kept, arrived, kind):
    shape = arrived.shape if kind == jnp.int16 else kept.shape
    return pl.pallas_call(
        combine_kernel,
        grid=(1,),
        in_specs=[whole(kept.shape), whole(arrived.shape)],
        out_specs=whole(shape),
        out_shape=jax.ShapeDtypeStruct(shape, kind),
        compiler_params=params(),
        cost_estimate=pl.CostEstimate(
            flops=8 * kept.size, bytes_accessed=8 * kept.size, transcendentals=0
        ),
        name="combine",
    )(kept, arrived)


def update_kernel(count, *refs):
    kept_ref, out_ref = refs[0], refs[-1]
    tile = out_ref.shape[-1]
    arrived = [read_message(ref, kept_ref.shape[0]) for ref in refs[1 : 1 + count]]
    for slot in range(out_ref.shape[0]):
        total = kept_ref[slot * tile : (slot + 1) * tile, :]
        for block in arrived:
            total = total + block(slot)
        mean = jnp.sum(total * total) / (tile * tile)
        out_ref[slot] = (total * lax.rsqrt(mean + 1e-06)).T.astype(out_ref.dtype)


def normalized_update(kept, arrived, shape):
    return pl.pallas_call(
        functools.partial(update_kernel, len(arrived)),
        grid=(1,),
        in_specs=[whole(kept.shape)] + [whole(a.shape) for a in arrived],
        out_specs=whole(shape),
        out_shape=jax.ShapeDtypeStruct(shape, jnp.bfloat16),
        compiler_params=params(),
        cost_estimate=pl.CostEstimate(
            flops=16 * kept.size, bytes_accessed=12 * kept.size, transcendentals=0
        ),
        name="normalized_update",
    )(kept, *arrived)


def grad_input_kernel(cotangent_ref, transposed_ref, out_ref):
    step = 512
    for n in range(out_ref.shape[1] // step):
        span = slice(n * step, (n + 1) * step)
        out_ref[:, span] = jnp.dot(
            cotangent_ref[...], transposed_ref[:, span], preferred_element_type=jnp.float32
        ).astype(out_ref.dtype)


def grad_inputs(cotangent, transposed):
    tokens, width = cotangent.shape
    features = transposed.shape[1]
    block = 256
    return pl.pallas_call(
        grad_input_kernel,
        grid=(tokens // block,),
        in_specs=[
            pl.BlockSpec((block, width), lambda i: (i, 0)),
            whole(transposed.shape),
        ],
        out_specs=pl.BlockSpec((block, features), lambda i: (i, 0)),
        out_shape=jax.ShapeDtypeStruct((tokens, features), jnp.bfloat16),
        compiler_params=params(),
        cost_estimate=pl.CostEstimate(
            flops=2 * tokens * features * width,
            bytes_accessed=10 * 1024 * 1024,
            transcendentals=0,
        ),
        name="grad_inputs",
    )(cotangent, transposed)


def local(devices, parts, normed, tile_values, tile_rows, tile_columns, cotangent):
    tile = tile_values.shape[-1]
    tiles = tile_values[0]
    column_blocks = cotangent.shape[1] * parts // tile
    chips = devices // 2
    place = lax.axis_index("tensor").astype(jnp.int32).reshape(1)

    def swap(x, mask):
        return lax.ppermute(x, "fsdp", [(i, i ^ mask) for i in range(devices)])

    def right(x, *sources):
        return lax.ppermute(x, "tensor", [(i, i + 1) for i in sources])

    def left(x, *sources):
        return lax.ppermute(x, "tensor", [(i, i - 1) for i in sources])

    r1, l1 = right(cotangent, 0, 1, 2), left(cotangent, 3, 2, 1)
    same_core = [tiles] + [swap(tiles, 2 * chip) for chip in range(1, chips)]
    codes = jnp.where(tile_columns >= 0, tile_rows * column_blocks + tile_columns, -1)
    mask = 1
    while mask < devices:
        codes = jnp.concatenate([codes, swap(codes, mask)], axis=0)
        mask *= 2
    r2, l2 = right(r1, 1, 2), left(l1, 2, 1)
    r3, l3 = right(r2, 2), left(l2, 1)
    gathered = []
    for chip in range(chips):
        gathered += [same_core[chip], swap(same_core[chip], 1)]

    partial, first, transposed = partial_values(
        codes, place, normed, gathered, parts, column_blocks
    )
    keep, send, full_cotangent = gradient_terms(
        codes, place, normed, cotangent, (r1, r2, r3), (l1, l2, l3), column_blocks
    )

    arrived = lax.ppermute(first, "tensor", [(0, 1), (3, 2)])
    second = hop((place + 2) % parts, partial, arrived)
    from_left, from_right = right(second, 0, 1), left(second, 3, 2)
    from_left = right(hop((place + 1) % parts, partial, from_left), 0, 1, 2)
    from_right = left(hop((place + 3) % parts, partial, from_right), 3, 2, 1)
    values = last_hop(place, partial, from_left, from_right)

    other = [swap(message, 1) for message in send]
    terms = [
        swap(combine(keep[chip], other[chip], jnp.int16), 2 * chip)
        for chip in reversed(range(1, chips))
    ]
    own = combine(keep[0], other[0], jnp.float32)
    update = normalized_update(own, terms, tile_values.shape[1:])
    grad_input = grad_inputs(full_cotangent, transposed)
    return values, grad_input, update[None]


def solution(mesh):
    in_specs = (
        P("fsdp", "tensor"),
        P("tensor", "fsdp", None, None),
        P("tensor", "fsdp"),
        P("tensor", "fsdp"),
        P("fsdp", "tensor"),
    )
    out_specs = (P("fsdp", "tensor"), P("fsdp", "tensor"), P("tensor", "fsdp", None, None))
    return jax.shard_map(
        functools.partial(local, mesh.shape["fsdp"], mesh.shape["tensor"]),
        mesh=mesh,
        in_specs=in_specs,
        out_specs=out_specs,
        check_vma=False,
    )
```

```python
import functools

import jax
import jax.numpy as jnp
from jax import lax
from jax.experimental import pallas as pl
from jax.experimental.pallas import tpu as pltpu
from jax.sharding import PartitionSpec as P

VMEM_BYTES = 48 * 1024 * 1024
GROUP = 128
PAD = 16


def encode(block):
    peak = jnp.max(jnp.abs(block), axis=0, keepdims=True)
    exponent = jnp.floor(jnp.log2(jnp.maximum(peak, 2.0**-100))) + 1.0
    exponent = jnp.clip(exponent, -100.0, 128.0)
    scaled = jnp.round(block * jnp.exp2(15.0 - exponent))
    codes = jnp.clip(scaled, -32767.0, 32767.0).astype(jnp.int32).astype(jnp.int16)
    return codes, exponent


def decode(codes, exponent):
    return codes.astype(jnp.int32).astype(jnp.float32) * jnp.exp2(exponent - 15.0)


def as_code(exponents):
    return exponents.astype(jnp.int32).astype(jnp.int16)


def exponent_rows(codes):
    return codes.astype(jnp.int32).astype(jnp.float32)


def params():
    return pltpu.CompilerParams(vmem_limit_bytes=VMEM_BYTES)


def whole(shape):
    zeros = (0,) * len(shape)
    return pl.BlockSpec(shape, lambda *_: zeros, pipeline_mode=pl.Buffered(1))


def aligned(index, size):
    return pl.ds(pl.multiple_of(index * size, size), size)


def write_message(message_ref, rows, blocks):
    place = lax.broadcasted_iota(jnp.int32, (PAD, message_ref.shape[1]), 0)
    exponents = jnp.zeros((PAD, message_ref.shape[1]), jnp.float32)
    for group in range(rows // GROUP):
        codes, exponent = encode(blocks(group))
        message_ref[group * GROUP : (group + 1) * GROUP, :] = codes
        exponents = jnp.where(place == group, exponent, exponents)
    message_ref[rows : rows + PAD, :] = as_code(exponents)


def read_message(message_ref, rows):
    exponents = exponent_rows(message_ref[rows : rows + PAD, :])

    def block(group):
        return decode(
            message_ref[group * GROUP : (group + 1) * GROUP, :], exponents[group : group + 1, :]
        )

    return block


def first_kernel(column_blocks, codes_ref, place_ref, normed_ref, *refs):
    message_refs = refs[:-2]
    weight_ref, first_ref = refs[-2:]
    tokens = normed_ref.shape[0]
    chunk_width = first_ref.shape[1]
    chunks = weight_ref.shape[1] // chunk_width
    tile = message_refs[0].shape[1]
    weight_ref[...] = jnp.zeros_like(weight_ref)
    for k in range(len(message_refs)):
        for slot in range(codes_ref.shape[1]):
            code = codes_ref[k, slot]

            @pl.when(code >= 0)
            def _():
                row = aligned(code // column_blocks, tile)
                column = aligned(code % column_blocks, tile)
                weight_ref[row, column] = message_refs[k][slot * tile : (slot + 1) * tile, :]

    far = weight_ref[:, aligned(chunks - 1 - place_ref[0], chunk_width)]
    partial = jnp.dot(normed_ref[...], far, preferred_element_type=jnp.float32)
    write_message(
        first_ref, tokens, lambda group: partial[group * GROUP : (group + 1) * GROUP, :]
    )


def first_values(codes, place, normed, messages, chunks, column_blocks):
    tokens, features = normed.shape
    tile = messages[0].shape[1]
    width = column_blocks * tile
    return pl.pallas_call(
        functools.partial(first_kernel, column_blocks),
        grid_spec=pltpu.PrefetchScalarGridSpec(
            num_scalar_prefetch=2,
            grid=(1,),
            in_specs=[whole(normed.shape)] + [whole(m.shape) for m in messages],
            out_specs=[whole((features, width)), whole((tokens + PAD, width // chunks))],
        ),
        out_shape=[
            jax.ShapeDtypeStruct((features, width), jnp.bfloat16),
            jax.ShapeDtypeStruct((tokens + PAD, width // chunks), jnp.int16),
        ],
        compiler_params=params(),
        cost_estimate=pl.CostEstimate(flops=1, bytes_accessed=1, transcendentals=0),
        name="first_values",
    )(codes, place, normed, *messages)


def partial_kernel(normed_ref, weight_ref, partial_ref):
    partial_ref[0] = jnp.dot(
        normed_ref[...], weight_ref[...], preferred_element_type=jnp.float32
    )


def partial_values(normed, weight, chunks):
    tokens, features = normed.shape
    width = weight.shape[1] // chunks
    return pl.pallas_call(
        partial_kernel,
        grid=(chunks,),
        in_specs=[whole(normed.shape), pl.BlockSpec((features, width), lambda h: (0, h))],
        out_specs=pl.BlockSpec((1, tokens, width), lambda h: (h, 0, 0)),
        out_shape=jax.ShapeDtypeStruct((chunks, tokens, width), jnp.float32),
        compiler_params=params(),
        cost_estimate=pl.CostEstimate(flops=1, bytes_accessed=1, transcendentals=0),
        name="partial_values",
    )(normed, weight)


def hop_kernel(place_ref, partial_ref, arrived_ref, message_ref):
    rows = partial_ref.shape[1]
    arrived = read_message(arrived_ref, rows)

    def total(group):
        return partial_ref[0, group * GROUP : (group + 1) * GROUP, :] + arrived(group)

    write_message(message_ref, rows, total)


def hop(place, ahead, partial, arrived):
    chunks, tokens, width = partial.shape
    return pl.pallas_call(
        hop_kernel,
        grid_spec=pltpu.PrefetchScalarGridSpec(
            num_scalar_prefetch=1,
            grid=(1,),
            in_specs=[
                pl.BlockSpec((1, tokens, width), lambda i, p: ((p[0] + ahead) % chunks, 0, 0)),
                whole(arrived.shape),
            ],
            out_specs=whole(arrived.shape),
        ),
        out_shape=jax.ShapeDtypeStruct(arrived.shape, jnp.int16),
        compiler_params=params(),
        cost_estimate=pl.CostEstimate(
            flops=8 * tokens * width, bytes_accessed=8 * tokens * width, transcendentals=0
        ),
        name="hop",
    )(place, partial, arrived)


def last_hop_kernel(place_ref, partial_ref, right_ref, left_ref, values_ref):
    rows = partial_ref.shape[1]
    right = read_message(right_ref, rows)
    left = read_message(left_ref, rows)
    for group in range(rows // GROUP):
        span = slice(group * GROUP, (group + 1) * GROUP)
        total = partial_ref[0, span, :] + right(group) + left(group)
        values_ref[span, :] = total.astype(values_ref.dtype)


def last_hop(place, partial, right, left):
    _, tokens, width = partial.shape
    return pl.pallas_call(
        last_hop_kernel,
        grid_spec=pltpu.PrefetchScalarGridSpec(
            num_scalar_prefetch=1,
            grid=(1,),
            in_specs=[
                pl.BlockSpec((1, tokens, width), lambda i, p: (p[0], 0, 0)),
                whole(right.shape),
                whole(left.shape),
            ],
            out_specs=whole((tokens, width)),
        ),
        out_shape=jax.ShapeDtypeStruct((tokens, width), jnp.bfloat16),
        compiler_params=params(),
        cost_estimate=pl.CostEstimate(
            flops=8 * tokens * width, bytes_accessed=10 * tokens * width, transcendentals=0
        ),
        name="last_hop",
    )(place, partial, right, left)


def chunk_order(place):
    return (
        place,
        jnp.where(place == 3, 2, place + 1),
        jnp.where(place == 0, 2, jnp.where(place == 1, 0, 1)),
        jnp.where(place < 2, 3, 0),
    )


def second_chunk(place, r1, l1):
    return jnp.where(place == 3, r1, l1)


def third_chunk(place, r1, r2, l2):
    return jnp.where((place == 1) | (place == 2), r1, r2 + l2)


def fourth_chunk(place, r2, l2, r3, l3):
    return jnp.where((place == 1) | (place == 2), r2 + l2, r3 + l3)


def product(turned, normed_ref, out_ref):
    step = 512
    for n in range(normed_ref.shape[1] // step):
        span = slice(n * step, (n + 1) * step)
        out_ref[:, span] = jnp.dot(turned, normed_ref[:, span], preferred_element_type=jnp.float32)


def chunk_kernel(pick, place_ref, normed_ref, *refs):
    tokens = normed_ref.shape[0]
    chunk = pick(place_ref[0], *[ref[:tokens, :] for ref in refs[:-1]])
    product(chunk.T, normed_ref, refs[-1])


def chunk_gradient(pick, place, normed, *chunks):
    tokens, features = normed.shape
    width = chunks[0].shape[1]
    return pl.pallas_call(
        functools.partial(chunk_kernel, pick),
        grid_spec=pltpu.PrefetchScalarGridSpec(
            num_scalar_prefetch=1,
            grid=(1,),
            in_specs=[whole(a.shape) for a in (normed, *chunks)],
            out_specs=whole((width, features)),
        ),
        out_shape=jax.ShapeDtypeStruct((width, features), jnp.float32),
        compiler_params=params(),
        cost_estimate=pl.CostEstimate(flops=1, bytes_accessed=1, transcendentals=0),
        name="chunk_gradient",
    )(place, normed, *chunks)


def slots_kernel(
    chips, column_blocks, codes_ref, place_ref, normed_ref, r2, l2, r3, l3, g1, g2, g3, *refs
):
    keep_refs = refs[:chips]
    send_refs = refs[chips : 2 * chips]
    gradient, sems = refs[2 * chips :]
    place = place_ref[0]
    copies = [
        pltpu.make_async_copy(g, gradient.at[i], sems.at[i]) for i, g in enumerate((g1, g2, g3))
    ]
    for copy in copies:
        copy.start()
    tokens = normed_ref.shape[0]
    chunk = fourth_chunk(place, *[ref[:tokens, :] for ref in (r2, l2, r3, l3)])
    product(chunk.T, normed_ref, gradient.at[3])
    for copy in copies:
        copy.wait()
    order = chunk_order(place)
    tile = GROUP
    capacity = codes_ref.shape[1]
    chunk_blocks = gradient.shape[1] // tile

    def term(k, slot):
        code = codes_ref[k, slot]
        safe = jnp.maximum(code, 0)
        row, column = safe // column_blocks, safe % column_blocks
        chunk = column // chunk_blocks
        stage = jnp.where(
            chunk == order[0],
            0,
            jnp.where(chunk == order[1], 1, jnp.where(chunk == order[2], 2, 3)),
        )
        block = gradient[stage, aligned(column % chunk_blocks, tile), aligned(row, tile)]
        return jnp.where(code >= 0, block, 0.0)

    for chip in reversed(range(chips)):
        write_message(send_refs[chip], capacity * tile, lambda slot: term(2 * chip + 1, slot))
        for slot in range(capacity):
            keep_refs[chip][slot * tile : (slot + 1) * tile, :] = term(2 * chip, slot)


def slot_terms(codes, place, normed, late, early, column_blocks):
    tokens, features = normed.shape
    chips = codes.shape[0] // 2
    rows = codes.shape[1] * GROUP
    width = early[0].shape[0]
    shapes = [((rows, GROUP), jnp.float32)] * chips + [((rows + PAD, GROUP), jnp.int16)] * chips
    outputs = pl.pallas_call(
        functools.partial(slots_kernel, chips, column_blocks),
        grid_spec=pltpu.PrefetchScalarGridSpec(
            num_scalar_prefetch=2,
            grid=(1,),
            in_specs=[whole(a.shape) for a in (normed, *late)]
            + [pl.BlockSpec(memory_space=pl.ANY)] * len(early),
            out_specs=[whole(shape) for shape, _ in shapes],
            scratch_shapes=[
                pltpu.VMEM((len(early) + 1, width, features), jnp.float32),
                pltpu.SemaphoreType.DMA((len(early),)),
            ],
        ),
        out_shape=[jax.ShapeDtypeStruct(shape, kind) for shape, kind in shapes],
        compiler_params=params(),
        cost_estimate=pl.CostEstimate(
            flops=2 * tokens * features * width,
            bytes_accessed=18 * 1024 * 1024,
            transcendentals=0,
        ),
        name="slot_terms",
    )(codes, place, normed, *late, *early)
    return outputs[:chips], outputs[chips:]


def combine_kernel(kept_ref, arrived_ref, out_ref):
    rows = kept_ref.shape[0]
    arrived = read_message(arrived_ref, rows)

    def total(group):
        return kept_ref[group * GROUP : (group + 1) * GROUP, :] + arrived(group)

    if out_ref.dtype == jnp.int16:
        write_message(out_ref, rows, total)
    else:
        for group in range(rows // GROUP):
            out_ref[group * GROUP : (group + 1) * GROUP, :] = total(group)


def combine(kept, arrived, kind):
    shape = arrived.shape if kind == jnp.int16 else kept.shape
    return pl.pallas_call(
        combine_kernel,
        grid=(1,),
        in_specs=[whole(kept.shape), whole(arrived.shape)],
        out_specs=whole(shape),
        out_shape=jax.ShapeDtypeStruct(shape, kind),
        compiler_params=params(),
        cost_estimate=pl.CostEstimate(
            flops=8 * kept.size, bytes_accessed=8 * kept.size, transcendentals=0
        ),
        name="combine",
    )(kept, arrived)


def update_kernel(count, *refs):
    kept_ref, out_ref = refs[0], refs[-1]
    tile = out_ref.shape[-1]
    arrived = [read_message(ref, kept_ref.shape[0]) for ref in refs[1 : 1 + count]]
    for slot in range(out_ref.shape[0]):
        total = kept_ref[slot * tile : (slot + 1) * tile, :]
        for block in arrived:
            total = total + block(slot)
        mean = jnp.sum(total * total) / (tile * tile)
        out_ref[slot] = (total * lax.rsqrt(mean + 1e-06)).T.astype(out_ref.dtype)


def normalized_update(kept, arrived, shape):
    return pl.pallas_call(
        functools.partial(update_kernel, len(arrived)),
        grid=(1,),
        in_specs=[whole(kept.shape)] + [whole(a.shape) for a in arrived],
        out_specs=whole(shape),
        out_shape=jax.ShapeDtypeStruct(shape, jnp.bfloat16),
        compiler_params=params(),
        cost_estimate=pl.CostEstimate(
            flops=16 * kept.size, bytes_accessed=12 * kept.size, transcendentals=0
        ),
        name="normalized_update",
    )(kept, *arrived)


def grad_input_kernel(place_ref, weight_ref, own, r1, r2, r3, l1, l2, l3, out_ref, cotangent):
    @pl.when(pl.program_id(0) == 0)
    def _():
        place = place_ref[0]
        order = chunk_order(place)
        width = own.shape[1]
        arrived = (r1, r2, r3, l1, l2, l3)
        v1, v2, v3, w1, w2, w3 = (ref[: own.shape[0], :] for ref in arrived)
        cotangent[:, aligned(order[0], width)] = own[...]
        cotangent[:, aligned(order[1], width)] = second_chunk(place, v1, w1)
        cotangent[:, aligned(order[2], width)] = third_chunk(place, v1, v2, w2)
        cotangent[:, aligned(order[3], width)] = fourth_chunk(place, v2, w2, v3, w3)

    out_ref[...] = lax.dot_general(
        cotangent[...],
        weight_ref[...],
        (((1,), (1,)), ((), ())),
        preferred_element_type=jnp.float32,
    ).astype(out_ref.dtype)


def grad_inputs(place, weight, *chunks):
    features, width = weight.shape
    tokens = chunks[0].shape[0]
    block = 256
    return pl.pallas_call(
        grad_input_kernel,
        grid_spec=pltpu.PrefetchScalarGridSpec(
            num_scalar_prefetch=1,
            grid=(features // block,),
            in_specs=[pl.BlockSpec((block, width), lambda i, p: (i, 0))]
            + [whole(chunk.shape) for chunk in chunks],
            out_specs=pl.BlockSpec((tokens, block), lambda i, p: (0, i)),
            scratch_shapes=[pltpu.VMEM((tokens, width), jnp.bfloat16)],
        ),
        out_shape=jax.ShapeDtypeStruct((tokens, features), jnp.bfloat16),
        compiler_params=params(),
        cost_estimate=pl.CostEstimate(
            flops=2 * tokens * features * width,
            bytes_accessed=12 * 1024 * 1024,
            transcendentals=0,
        ),
        name="grad_inputs",
    )(place, weight, *chunks)


def local(devices, parts, normed, tile_values, tile_rows, tile_columns, cotangent):
    capacity, tile = tile_values.shape[1], tile_values.shape[-1]
    column_blocks = cotangent.shape[1] * parts // tile
    chips = devices // 2
    rows = capacity * tile
    place = lax.axis_index("tensor").astype(jnp.int32).reshape(1)

    def swap(x, mask):
        return lax.ppermute(x, "fsdp", [(i, i ^ mask) for i in range(devices)])

    def right(x, *sources):
        return lax.ppermute(x, "tensor", [(i, i + 1) for i in sources])

    def left(x, *sources):
        return lax.ppermute(x, "tensor", [(i, i - 1) for i in sources])

    padded = jnp.pad(cotangent, ((0, PAD), (0, 0)))
    r1, l1 = right(padded, 0, 1, 2), left(padded, 3, 2, 1)
    positions = jnp.where(tile_columns >= 0, tile_rows * column_blocks + tile_columns + 1, 0)
    positions = jnp.pad(
        positions.astype(jnp.bfloat16), ((0, PAD - 1), (0, tile - capacity))
    )
    message = jnp.concatenate([tile_values.reshape(rows, tile), positions], axis=0)
    g1 = chunk_gradient(lambda place, own: own, place, normed, cotangent)
    direct = [1, 2] if chips == 4 else list(range(1, chips))
    same_core = [message] + [swap(message, 2 * chip) for chip in direct]
    beside = swap(message, 1)
    r1, l1, g1, beside, *same_core = lax.optimization_barrier((r1, l1, g1, beside, *same_core))

    r2, l2 = right(r1, 1, 2), left(l1, 2, 1)
    g2 = chunk_gradient(second_chunk, place, normed, r1, l1)
    if chips == 4:
        even = lax.axis_index("fsdp") % 2 == 0
        diagonal = lax.ppermute(
            jnp.where(even, same_core[2], same_core[1]),
            "fsdp",
            [(i, i ^ 2 if i % 2 == 0 else i ^ 4) for i in range(devices)],
        )
        across = [swap(m, 1) for m in same_core[1:]]
        diagonal, g2, *across = lax.optimization_barrier((diagonal, g2, *across))
        same_core.append(diagonal)
        across.append(swap(diagonal, 1))
    else:
        across = [swap(m, 1) for m in same_core[1:]]
    gathered = []
    for pair in zip(same_core, [beside] + across):
        gathered += pair
    r2, l2, *gathered = lax.optimization_barrier((r2, l2, *gathered))
    codes = jnp.stack([m[rows, :capacity] for m in gathered]).astype(jnp.int32) - 1

    r3, l3 = right(r2, 2), left(l2, 1)
    weight, first = first_values(codes, place, normed, gathered, parts, column_blocks)
    arrived = lax.ppermute(first, "tensor", [(0, 1), (3, 2)])
    partial = partial_values(normed, weight, parts)
    g3 = chunk_gradient(third_chunk, place, normed, r1, r2, l2)
    arrived, g3 = lax.optimization_barrier((arrived, g3))

    keep, send = slot_terms(
        codes, place, normed, (r2, l2, r3, l3), (g1, g2, g3), column_blocks
    )
    second = hop(place, 2, partial, arrived)
    from_left, from_right = right(second, 0, 1), left(second, 3, 2)
    other = [swap(m, 1) for m in send]
    terms = [
        swap(combine(keep[chip], other[chip], jnp.int16), 2 * chip)
        for chip in reversed(range(1, chips))
    ]
    own = combine(keep[0], other[0], jnp.float32)
    from_left = right(hop(place, 1, partial, from_left), 0, 1, 2)
    from_right = left(hop(place, 3, partial, from_right), 3, 2, 1)
    grad_input = grad_inputs(place, weight, cotangent, r1, r2, r3, l1, l2, l3)
    values = last_hop(place, partial, from_left, from_right)
    update = normalized_update(own, terms, tile_values.shape[1:])
    return values, grad_input, update[None]


def solution(mesh):
    in_specs = (
        P("fsdp", "tensor"),
        P("tensor", "fsdp", None, None),
        P("tensor", "fsdp"),
        P("tensor", "fsdp"),
        P("fsdp", "tensor"),
    )
    out_specs = (P("fsdp", "tensor"), P("fsdp", "tensor"), P("tensor", "fsdp", None, None))
    return jax.shard_map(
        functools.partial(local, mesh.shape["fsdp"], mesh.shape["tensor"]),
        mesh=mesh,
        in_specs=in_specs,
        out_specs=out_specs,
        check_vma=False,
    )
```

```python
import functools

import jax
import jax.numpy as jnp
from jax import lax
from jax.experimental import pallas as pl
from jax.experimental.pallas import tpu as pltpu
from jax.sharding import PartitionSpec as P

MIB = 1024 * 1024
GROUP = 128
PAD = 16
EXTRA = 16


def encode(block):
    peak = jnp.max(jnp.abs(block), axis=0, keepdims=True)
    exponent = jnp.floor(jnp.log2(jnp.maximum(peak, 2.0**-100))) + 1.0
    exponent = jnp.clip(exponent, -100.0, 128.0)
    scaled = jnp.round(block * jnp.exp2(15.0 - exponent))
    codes = jnp.clip(scaled, -32767.0, 32767.0).astype(jnp.int32).astype(jnp.int16)
    return codes, exponent


def decode(codes, exponent):
    return codes.astype(jnp.int32).astype(jnp.float32) * jnp.exp2(exponent - 15.0)


def as_code(exponents):
    return exponents.astype(jnp.int32).astype(jnp.int16)


def exponent_rows(codes):
    return codes.astype(jnp.int32).astype(jnp.float32)


def params(mib):
    return pltpu.CompilerParams(vmem_limit_bytes=mib * MIB)


VMEM = pl.BlockSpec(memory_space=pltpu.VMEM)
SMEM = pl.BlockSpec(memory_space=pltpu.SMEM)
LITTLE = pl.CostEstimate(flops=1, bytes_accessed=1, transcendentals=0)


def aligned(index, size):
    return pl.ds(pl.multiple_of(index * size, size), size)


def write_message(message_ref, rows, blocks):
    place = lax.broadcasted_iota(jnp.int32, (PAD, message_ref.shape[1]), 0)
    exponents = jnp.zeros((PAD, message_ref.shape[1]), jnp.float32)
    for group in range(rows // GROUP):
        codes, exponent = encode(blocks(group))
        message_ref[group * GROUP : (group + 1) * GROUP, :] = codes
        exponents = jnp.where(place == group, exponent, exponents)
    message_ref[rows : rows + PAD, :] = as_code(exponents)


def read_message(message_ref, rows):
    exponents = exponent_rows(message_ref[rows : rows + PAD, :])

    def block(group):
        return decode(
            message_ref[group * GROUP : (group + 1) * GROUP, :], exponents[group : group + 1, :]
        )

    return block


def pack_kernel(column_blocks, rows_ref, columns_ref, tiles_ref, chunk_ref, message_ref, padded_ref):
    rows = tiles_ref.shape[0]
    tokens = chunk_ref.shape[0]
    message_ref[:rows, :] = tiles_ref[...]
    lane = lax.broadcasted_iota(jnp.int32, (PAD, tiles_ref.shape[1]), 1)
    positions = jnp.zeros(lane.shape, jnp.int32)
    for slot in range(rows_ref.shape[1]):
        row, column = rows_ref[0, slot], columns_ref[0, slot]
        position = jnp.where(column >= 0, row * column_blocks + column + 1, 0)
        positions = jnp.where(lane == slot, position, positions)
    message_ref[rows:, :] = positions.astype(jnp.float32).astype(message_ref.dtype)
    padded_ref[:tokens, :] = chunk_ref[...]
    padded_ref[tokens:, :] = jnp.zeros((EXTRA, chunk_ref.shape[1]), padded_ref.dtype)


def pack(rows, columns, tiles, chunk, column_blocks):
    return pl.pallas_call(
        functools.partial(pack_kernel, column_blocks),
        in_specs=[SMEM, SMEM, VMEM, VMEM],
        out_specs=[VMEM, VMEM],
        out_shape=[
            jax.ShapeDtypeStruct((tiles.shape[0] + PAD, tiles.shape[1]), tiles.dtype),
            jax.ShapeDtypeStruct((chunk.shape[0] + EXTRA, chunk.shape[1]), chunk.dtype),
        ],
        compiler_params=params(8),
        cost_estimate=LITTLE,
        name="pack",
    )(rows, columns, tiles, chunk)


def first_kernel(column_blocks, place_ref, normed_ref, *refs):
    message_refs = refs[:-6]
    weight_ref, first_ref, codes_ref, partial, scalars, sem = refs[-6:]
    tokens = normed_ref.shape[0]
    chunk_width = first_ref.shape[1]
    chunks = weight_ref.shape[1] // chunk_width
    tile = message_refs[0].shape[1]
    capacity = message_refs[0].shape[0] // tile
    for k, message_ref in enumerate(message_refs):
        positions = message_ref[capacity * tile : capacity * tile + PAD, :]
        codes_ref[k : k + 1, :] = positions.astype(jnp.float32)[:1, :].astype(jnp.int32) - 1
    copy = pltpu.make_async_copy(codes_ref, scalars, sem)
    copy.start()
    weight_ref[...] = jnp.zeros_like(weight_ref)
    copy.wait()
    for k, message_ref in enumerate(message_refs):
        for slot in range(capacity):
            code = scalars[k, slot]

            @pl.when(code >= 0)
            def _():
                row = aligned(code // column_blocks, tile)
                column = aligned(code % column_blocks, tile)
                weight_ref[row, column] = message_ref[slot * tile : (slot + 1) * tile, :]

    far = weight_ref[:, aligned(chunks - 1 - place_ref[0], chunk_width)]
    partial[...] = jnp.dot(normed_ref[...], far, preferred_element_type=jnp.float32)
    write_message(
        first_ref, tokens, lambda group: partial[group * GROUP : (group + 1) * GROUP, :]
    )


def first_values(place, normed, messages, chunks, column_blocks):
    tokens, features = normed.shape
    tile = messages[0].shape[1]
    width = column_blocks * tile
    return pl.pallas_call(
        functools.partial(first_kernel, column_blocks),
        in_specs=[SMEM, VMEM] + [VMEM] * len(messages),
        out_specs=[VMEM, VMEM, VMEM],
        out_shape=[
            jax.ShapeDtypeStruct((features, width), jnp.bfloat16),
            jax.ShapeDtypeStruct((tokens + PAD, width // chunks), jnp.int16),
            jax.ShapeDtypeStruct((len(messages), tile), jnp.int32),
        ],
        scratch_shapes=[
            pltpu.VMEM((tokens, width // chunks), jnp.float32),
            pltpu.SMEM((len(messages), tile), jnp.int32),
            pltpu.SemaphoreType.DMA,
        ],
        compiler_params=params(22),
        cost_estimate=LITTLE,
        name="first_values",
    )(place, normed, *messages)


def partial_kernel(normed_ref, weight_ref, partial_ref):
    step = 512
    for n in range(partial_ref.shape[1] // step):
        span = slice(n * step, (n + 1) * step)
        partial_ref[:, span] = jnp.dot(
            normed_ref[...], weight_ref[:, span], preferred_element_type=jnp.float32
        )


def partial_values(normed, weight):
    return pl.pallas_call(
        partial_kernel,
        in_specs=[VMEM, VMEM],
        out_specs=VMEM,
        out_shape=jax.ShapeDtypeStruct((normed.shape[0], weight.shape[1]), jnp.float32),
        compiler_params=params(20),
        cost_estimate=LITTLE,
        name="partial_values",
    )(normed, weight)


def chunk_of(place_ref, ahead, partial_ref, width):
    return aligned(lax.rem(place_ref[0] + ahead, partial_ref.shape[1] // width), width)


def hop_kernel(ahead, place_ref, partial_ref, arrived_ref, message_ref):
    rows, width = partial_ref.shape[0], message_ref.shape[1]
    arrived = read_message(arrived_ref, rows)
    columns = chunk_of(place_ref, ahead, partial_ref, width)

    def total(group):
        return partial_ref[group * GROUP : (group + 1) * GROUP, columns] + arrived(group)

    write_message(message_ref, rows, total)


def hop(place, ahead, partial, arrived):
    return pl.pallas_call(
        functools.partial(hop_kernel, ahead),
        in_specs=[SMEM, VMEM, VMEM],
        out_specs=VMEM,
        out_shape=jax.ShapeDtypeStruct(arrived.shape, jnp.int16),
        compiler_params=params(12),
        cost_estimate=LITTLE,
        name="hop",
    )(place, partial, arrived)


def last_hop_kernel(place_ref, partial_ref, right_ref, left_ref, values_ref):
    rows, width = values_ref.shape
    right = read_message(right_ref, rows)
    left = read_message(left_ref, rows)
    columns = chunk_of(place_ref, 0, partial_ref, width)
    for group in range(rows // GROUP):
        span = slice(group * GROUP, (group + 1) * GROUP)
        total = partial_ref[span, columns] + right(group) + left(group)
        values_ref[span, :] = total.astype(values_ref.dtype)


def last_hop(place, partial, right, left):
    rows, width = right.shape[0] - PAD, right.shape[1]
    return pl.pallas_call(
        last_hop_kernel,
        in_specs=[SMEM, VMEM, VMEM, VMEM],
        out_specs=VMEM,
        out_shape=jax.ShapeDtypeStruct((rows, width), jnp.bfloat16),
        compiler_params=params(12),
        cost_estimate=LITTLE,
        name="last_hop",
    )(place, partial, right, left)


def chunk_order(place):
    return (
        place,
        jnp.where(place == 3, 2, place + 1),
        jnp.where(place == 0, 2, jnp.where(place == 1, 0, 1)),
        jnp.where(place < 2, 3, 0),
    )


def second_chunk(place, r1, l1):
    return jnp.where(place == 3, r1, l1)


def third_chunk(place, r1, r2, l2):
    return jnp.where((place == 1) | (place == 2), r1, r2 + l2)


def fourth_chunk(place, r2, l2, r3, l3):
    return jnp.where((place == 1) | (place == 2), r2 + l2, r3 + l3)


def product(turned, normed_ref, out_ref):
    step = 1024
    for n in range(normed_ref.shape[1] // step):
        span = slice(n * step, (n + 1) * step)
        out_ref[:, span] = jnp.dot(turned, normed_ref[:, span], preferred_element_type=jnp.float32)


def chunk_kernel(pick, place_ref, normed_ref, *refs):
    tokens = normed_ref.shape[0]
    chunk = pick(place_ref[0], *[ref[:tokens, :] for ref in refs[:-1]])
    product(chunk.T, normed_ref, refs[-1])


def chunk_gradient(pick, place, normed, *chunks):
    return pl.pallas_call(
        functools.partial(chunk_kernel, pick),
        in_specs=[SMEM, VMEM] + [VMEM] * len(chunks),
        out_specs=VMEM,
        out_shape=jax.ShapeDtypeStruct((chunks[0].shape[1], normed.shape[1]), jnp.float32),
        compiler_params=params(16),
        cost_estimate=LITTLE,
        name="chunk_gradient",
    )(place, normed, *chunks)


def slots_kernel(
    chips, column_blocks, codes_ref, place_ref, normed_ref, r2, l2, r3, l3, g1, g2, g3, *refs
):
    keep_refs = refs[:chips]
    send_refs = refs[chips : 2 * chips]
    gradient, sems = refs[2 * chips :]
    place = place_ref[0]
    copies = [
        pltpu.make_async_copy(g, gradient.at[i], sems.at[i]) for i, g in enumerate((g1, g2, g3))
    ]
    for copy in copies:
        copy.start()
    tokens = normed_ref.shape[0]
    chunk = fourth_chunk(place, *[ref[:tokens, :] for ref in (r2, l2, r3, l3)])
    product(chunk.T, normed_ref, gradient.at[3])
    for copy in copies:
        copy.wait()
    order = chunk_order(place)
    tile = GROUP
    capacity = keep_refs[0].shape[0] // tile
    chunk_blocks = gradient.shape[1] // tile

    def term(k, slot):
        code = codes_ref[k, slot]
        safe = jnp.maximum(code, 0)
        row, column = safe // column_blocks, safe % column_blocks
        chunk = column // chunk_blocks
        stage = jnp.where(
            chunk == order[0],
            0,
            jnp.where(chunk == order[1], 1, jnp.where(chunk == order[2], 2, 3)),
        )
        block = gradient[stage, aligned(column % chunk_blocks, tile), aligned(row, tile)]
        return jnp.where(code >= 0, block, 0.0)

    for chip in reversed(range(chips)):
        write_message(send_refs[chip], capacity * tile, lambda slot: term(2 * chip + 1, slot))
        for slot in range(capacity):
            keep_refs[chip][slot * tile : (slot + 1) * tile, :] = term(2 * chip, slot)


def slot_terms(codes, place, normed, late, early, capacity, column_blocks):
    features = normed.shape[1]
    chips = codes.shape[0] // 2
    rows = capacity * GROUP
    width = early[0].shape[0]
    shapes = [((rows, GROUP), jnp.float32)] * chips + [((rows + PAD, GROUP), jnp.int16)] * chips
    outputs = pl.pallas_call(
        functools.partial(slots_kernel, chips, column_blocks),
        in_specs=[SMEM, SMEM, VMEM]
        + [VMEM] * len(late)
        + [pl.BlockSpec(memory_space=pl.ANY)] * len(early),
        out_specs=[VMEM] * len(shapes),
        scratch_shapes=[
            pltpu.VMEM((len(early) + 1, width, features), jnp.float32),
            pltpu.SemaphoreType.DMA((len(early),)),
        ],
        out_shape=[jax.ShapeDtypeStruct(shape, kind) for shape, kind in shapes],
        compiler_params=params(30),
        cost_estimate=LITTLE,
        name="slot_terms",
    )(codes, place, normed, *late, *early)
    return outputs[:chips], outputs[chips:]


def combine_kernel(kept_ref, arrived_ref, out_ref):
    rows = kept_ref.shape[0]
    arrived = read_message(arrived_ref, rows)

    def total(group):
        return kept_ref[group * GROUP : (group + 1) * GROUP, :] + arrived(group)

    if out_ref.dtype == jnp.int16:
        write_message(out_ref, rows, total)
    else:
        for group in range(rows // GROUP):
            out_ref[group * GROUP : (group + 1) * GROUP, :] = total(group)


def combine(kept, arrived, kind):
    shape = arrived.shape if kind == jnp.int16 else kept.shape
    return pl.pallas_call(
        combine_kernel,
        in_specs=[VMEM, VMEM],
        out_specs=VMEM,
        out_shape=jax.ShapeDtypeStruct(shape, kind),
        compiler_params=params(8),
        cost_estimate=LITTLE,
        name="combine",
    )(kept, arrived)


def update_kernel(count, *refs):
    kept_ref, out_ref = refs[0], refs[-1]
    tile = out_ref.shape[-1]
    arrived = [read_message(ref, kept_ref.shape[0]) for ref in refs[1 : 1 + count]]
    for slot in range(out_ref.shape[0]):
        total = kept_ref[slot * tile : (slot + 1) * tile, :]
        for block in arrived:
            total = total + block(slot)
        mean = jnp.sum(total * total) / (tile * tile)
        out_ref[slot] = (total * lax.rsqrt(mean + 1e-06)).T.astype(out_ref.dtype)


def normalized_update(kept, arrived, shape):
    return pl.pallas_call(
        functools.partial(update_kernel, len(arrived)),
        in_specs=[VMEM] * (1 + len(arrived)),
        out_specs=VMEM,
        out_shape=jax.ShapeDtypeStruct(shape, jnp.bfloat16),
        compiler_params=params(12),
        cost_estimate=LITTLE,
        name="normalized_update",
    )(kept, *arrived)


def grad_input_kernel(place_ref, weight_ref, own, r1, r2, r3, l1, l2, l3, out_ref, cotangent):
    @pl.when(pl.program_id(0) == 0)
    def _():
        place = place_ref[0]
        order = chunk_order(place)
        width = own.shape[1]
        arrived = (r1, r2, r3, l1, l2, l3)
        v1, v2, v3, w1, w2, w3 = (ref[: own.shape[0], :] for ref in arrived)
        cotangent[:, aligned(order[0], width)] = own[...]
        cotangent[:, aligned(order[1], width)] = second_chunk(place, v1, w1)
        cotangent[:, aligned(order[2], width)] = third_chunk(place, v1, v2, w2)
        cotangent[:, aligned(order[3], width)] = fourth_chunk(place, v2, w2, v3, w3)

    out_ref[...] = lax.dot_general(
        cotangent[...],
        weight_ref[...],
        (((1,), (1,)), ((), ())),
        preferred_element_type=jnp.float32,
    ).astype(out_ref.dtype)


def grad_inputs(place, weight, *chunks):
    features, width = weight.shape
    tokens = chunks[0].shape[0]
    block = 512
    return pl.pallas_call(
        grad_input_kernel,
        grid_spec=pltpu.PrefetchScalarGridSpec(
            num_scalar_prefetch=1,
            grid=(features // block,),
            in_specs=[pl.BlockSpec((block, width), lambda i, p: (i, 0))]
            + [VMEM] * len(chunks),
            out_specs=pl.BlockSpec((tokens, block), lambda i, p: (0, i)),
            scratch_shapes=[pltpu.VMEM((tokens, width), jnp.bfloat16)],
        ),
        out_shape=jax.ShapeDtypeStruct((tokens, features), jnp.bfloat16),
        compiler_params=params(20),
        cost_estimate=pl.CostEstimate(
            flops=2 * tokens * features * width,
            bytes_accessed=12 * MIB,
            transcendentals=0,
        ),
        name="grad_inputs",
    )(place, weight, *chunks)


def local(devices, parts, normed, tile_values, tile_rows, tile_columns, cotangent):
    capacity, tile = tile_values.shape[1], tile_values.shape[-1]
    column_blocks = cotangent.shape[1] * parts // tile
    chips = devices // 2
    rows = capacity * tile
    place = lax.axis_index("tensor").astype(jnp.int32).reshape(1)

    def swap(x, mask):
        return lax.ppermute(x, "fsdp", [(i, i ^ mask) for i in range(devices)])

    def right(x, *sources):
        return lax.ppermute(x, "tensor", [(i, i + 1) for i in sources])

    def left(x, *sources):
        return lax.ppermute(x, "tensor", [(i, i - 1) for i in sources])

    message, padded = pack(
        tile_rows, tile_columns, tile_values.reshape(rows, tile), cotangent, column_blocks
    )
    r1, l1 = right(padded, 0, 1, 2), left(padded, 3, 2, 1)
    g1 = chunk_gradient(lambda place, own: own, place, normed, cotangent)
    direct = [1, 2] if chips == 4 else list(range(1, chips))
    same_core = [message] + [swap(message, 2 * chip) for chip in direct]
    beside = swap(message, 1)
    r1, l1, g1, beside, *same_core = lax.optimization_barrier((r1, l1, g1, beside, *same_core))

    r2, l2 = right(r1, 1, 2), left(l1, 2, 1)
    g2 = chunk_gradient(second_chunk, place, normed, r1, l1)
    if chips == 4:
        even = lax.axis_index("fsdp") % 2 == 0
        diagonal = lax.ppermute(
            jnp.where(even, same_core[2], same_core[1]),
            "fsdp",
            [(i, i ^ 2 if i % 2 == 0 else i ^ 4) for i in range(devices)],
        )
        across = [swap(m, 1) for m in same_core[1:]]
        diagonal, g2, *across = lax.optimization_barrier((diagonal, g2, *across))
        same_core.append(diagonal)
        across.append(swap(diagonal, 1))
    else:
        across = [swap(m, 1) for m in same_core[1:]]
    gathered = []
    for pair in zip(same_core, [beside] + across):
        gathered += pair
    r2, l2, *gathered = lax.optimization_barrier((r2, l2, *gathered))

    r3, l3 = right(r2, 2), left(l2, 1)
    weight, first, codes = first_values(place, normed, gathered, parts, column_blocks)
    arrived = lax.ppermute(first, "tensor", [(0, 1), (3, 2)])
    partial = partial_values(normed, weight)
    g3 = chunk_gradient(third_chunk, place, normed, r1, r2, l2)
    arrived, g3 = lax.optimization_barrier((arrived, g3))

    keep, send = slot_terms(
        codes, place, normed, (r2, l2, r3, l3), (g1, g2, g3), capacity, column_blocks
    )
    second = hop(place, 2, partial, arrived)
    from_left, from_right = right(second, 0, 1), left(second, 3, 2)
    other = [swap(m, 1) for m in send]
    terms = [
        swap(combine(keep[chip], other[chip], jnp.int16), 2 * chip)
        for chip in reversed(range(1, chips))
    ]
    own = combine(keep[0], other[0], jnp.float32)
    from_left = right(hop(place, 1, partial, from_left), 0, 1, 2)
    from_right = left(hop(place, 3, partial, from_right), 3, 2, 1)
    grad_input = grad_inputs(place, weight, cotangent, r1, r2, r3, l1, l2, l3)
    values = last_hop(place, partial, from_left, from_right)
    update = normalized_update(own, terms, tile_values.shape[1:])
    return values, grad_input, update[None]


def solution(mesh):
    in_specs = (
        P("fsdp", "tensor"),
        P("tensor", "fsdp", None, None),
        P("tensor", "fsdp"),
        P("tensor", "fsdp"),
        P("fsdp", "tensor"),
    )
    out_specs = (P("fsdp", "tensor"), P("fsdp", "tensor"), P("tensor", "fsdp", None, None))
    return jax.shard_map(
        functools.partial(local, mesh.shape["fsdp"], mesh.shape["tensor"]),
        mesh=mesh,
        in_specs=in_specs,
        out_specs=out_specs,
        check_vma=False,
    )
```

```python
import functools

import jax
import jax.numpy as jnp
from jax import lax
from jax.experimental import pallas as pl
from jax.experimental.pallas import tpu as pltpu
from jax.sharding import PartitionSpec as P

MIB = 1024 * 1024
GROUP = 128
PAD = 16
EXTRA = 16


def encode(block):
    peak = jnp.max(jnp.abs(block), axis=0, keepdims=True)
    exponent = jnp.floor(jnp.log2(jnp.maximum(peak, 2.0**-100))) + 1.0
    exponent = jnp.clip(exponent, -100.0, 128.0)
    scaled = jnp.round(block * jnp.exp2(15.0 - exponent))
    codes = jnp.clip(scaled, -32767.0, 32767.0).astype(jnp.int32).astype(jnp.int16)
    return codes, exponent


def decode(codes, exponent):
    return codes.astype(jnp.int32).astype(jnp.float32) * jnp.exp2(exponent - 15.0)


def as_code(exponents):
    return exponents.astype(jnp.int32).astype(jnp.int16)


def exponent_rows(codes):
    return codes.astype(jnp.int32).astype(jnp.float32)


def params(mib):
    return pltpu.CompilerParams(vmem_limit_bytes=mib * MIB)


VMEM = pl.BlockSpec(memory_space=pltpu.VMEM)
SMEM = pl.BlockSpec(memory_space=pltpu.SMEM)
LITTLE = pl.CostEstimate(flops=1, bytes_accessed=1, transcendentals=0)


def aligned(index, size):
    return pl.ds(pl.multiple_of(index * size, size), size)


def write_message(message_ref, rows, blocks):
    place = lax.broadcasted_iota(jnp.int32, (PAD, message_ref.shape[1]), 0)
    exponents = jnp.zeros((PAD, message_ref.shape[1]), jnp.float32)
    for group in range(rows // GROUP):
        codes, exponent = encode(blocks(group))
        message_ref[group * GROUP : (group + 1) * GROUP, :] = codes
        exponents = jnp.where(place == group, exponent, exponents)
    message_ref[rows : rows + PAD, :] = as_code(exponents)


def read_message(message_ref, rows):
    exponents = exponent_rows(message_ref[rows : rows + PAD, :])

    def block(group):
        return decode(
            message_ref[group * GROUP : (group + 1) * GROUP, :], exponents[group : group + 1, :]
        )

    return block


def pack_kernel(
    column_blocks, rows_ref, columns_ref, tiles_ref, chunk_ref, message_ref, padded_ref, slots, sems
):
    rows = tiles_ref.shape[0]
    tokens = chunk_ref.shape[0]
    copies = [
        pltpu.make_async_copy(rows_ref, slots.at[0], sems.at[0]),
        pltpu.make_async_copy(columns_ref, slots.at[1], sems.at[1]),
        pltpu.make_async_copy(chunk_ref, padded_ref.at[pl.ds(0, tokens)], sems.at[2]),
        pltpu.make_async_copy(tiles_ref, message_ref.at[pl.ds(0, rows)], sems.at[3]),
    ]
    for copy in copies:
        copy.start()
    padded_ref[tokens:, :] = jnp.zeros((EXTRA, chunk_ref.shape[1]), padded_ref.dtype)
    copies[0].wait()
    copies[1].wait()
    lane = lax.broadcasted_iota(jnp.int32, (PAD, tiles_ref.shape[1]), 1)
    positions = jnp.zeros(lane.shape, jnp.int32)
    for slot in range(rows_ref.shape[1]):
        row, column = slots[0, 0, slot], slots[1, 0, slot]
        position = jnp.where(column >= 0, row * column_blocks + column + 1, 0)
        positions = jnp.where(lane == slot, position, positions)
    message_ref[rows:, :] = positions.astype(jnp.float32).astype(message_ref.dtype)
    copies[2].wait()
    copies[3].wait()


def pack(rows, columns, tiles, chunk, column_blocks):
    return pl.pallas_call(
        functools.partial(pack_kernel, column_blocks),
        in_specs=[pl.BlockSpec(memory_space=pl.ANY)] * 4,
        out_specs=[VMEM, VMEM],
        out_shape=[
            jax.ShapeDtypeStruct((tiles.shape[0] + PAD, tiles.shape[1]), tiles.dtype),
            jax.ShapeDtypeStruct((chunk.shape[0] + EXTRA, chunk.shape[1]), chunk.dtype),
        ],
        scratch_shapes=[
            pltpu.SMEM((2,) + rows.shape, jnp.int32),
            pltpu.SemaphoreType.DMA((4,)),
        ],
        compiler_params=params(8),
        cost_estimate=LITTLE,
        name="pack",
    )(rows, columns, tiles, chunk)


def first_kernel(column_blocks, place_ref, normed_ref, *refs):
    message_refs = refs[:-6]
    weight_ref, first_ref, codes_ref, partial, scalars, sem = refs[-6:]
    tokens = normed_ref.shape[0]
    chunk_width = first_ref.shape[1]
    chunks = weight_ref.shape[1] // chunk_width
    tile = message_refs[0].shape[1]
    capacity = message_refs[0].shape[0] // tile
    for k, message_ref in enumerate(message_refs):
        positions = message_ref[capacity * tile : capacity * tile + PAD, :]
        codes_ref[k : k + 1, :] = positions.astype(jnp.float32)[:1, :].astype(jnp.int32) - 1
    copy = pltpu.make_async_copy(codes_ref, scalars, sem)
    copy.start()
    weight_ref[...] = jnp.zeros_like(weight_ref)
    copy.wait()
    for k, message_ref in enumerate(message_refs):
        for slot in range(capacity):
            code = scalars[k, slot]

            @pl.when(code >= 0)
            def _():
                row = aligned(code // column_blocks, tile)
                column = aligned(code % column_blocks, tile)
                weight_ref[row, column] = message_ref[slot * tile : (slot + 1) * tile, :]

    far = weight_ref[:, aligned(chunks - 1 - place_ref[0], chunk_width)]
    partial[...] = jnp.dot(normed_ref[...], far, preferred_element_type=jnp.float32)
    write_message(
        first_ref, tokens, lambda group: partial[group * GROUP : (group + 1) * GROUP, :]
    )


def first_values(place, normed, messages, chunks, column_blocks):
    tokens, features = normed.shape
    tile = messages[0].shape[1]
    width = column_blocks * tile
    return pl.pallas_call(
        functools.partial(first_kernel, column_blocks),
        in_specs=[SMEM, VMEM] + [VMEM] * len(messages),
        out_specs=[VMEM, VMEM, VMEM],
        out_shape=[
            jax.ShapeDtypeStruct((features, width), jnp.bfloat16),
            jax.ShapeDtypeStruct((tokens + PAD, width // chunks), jnp.int16),
            jax.ShapeDtypeStruct((len(messages), tile), jnp.int32),
        ],
        scratch_shapes=[
            pltpu.VMEM((tokens, width // chunks), jnp.float32),
            pltpu.SMEM((len(messages), tile), jnp.int32),
            pltpu.SemaphoreType.DMA,
        ],
        compiler_params=params(22),
        cost_estimate=LITTLE,
        name="first_values",
    )(place, normed, *messages)


def partial_kernel(normed_ref, weight_ref, partial_ref):
    step = 512
    for n in range(partial_ref.shape[1] // step):
        span = slice(n * step, (n + 1) * step)
        partial_ref[:, span] = jnp.dot(
            normed_ref[...], weight_ref[:, span], preferred_element_type=jnp.float32
        )


def partial_values(normed, weight):
    return pl.pallas_call(
        partial_kernel,
        in_specs=[VMEM, VMEM],
        out_specs=VMEM,
        out_shape=jax.ShapeDtypeStruct((normed.shape[0], weight.shape[1]), jnp.float32),
        compiler_params=params(20),
        cost_estimate=LITTLE,
        name="partial_values",
    )(normed, weight)


def chunk_of(place_ref, ahead, partial_ref, width):
    return aligned(lax.rem(place_ref[0] + ahead, partial_ref.shape[1] // width), width)


def hop_kernel(ahead, place_ref, partial_ref, arrived_ref, message_ref):
    rows, width = partial_ref.shape[0], message_ref.shape[1]
    arrived = read_message(arrived_ref, rows)
    columns = chunk_of(place_ref, ahead, partial_ref, width)

    def total(group):
        return partial_ref[group * GROUP : (group + 1) * GROUP, columns] + arrived(group)

    write_message(message_ref, rows, total)


def hop(place, ahead, partial, arrived):
    return pl.pallas_call(
        functools.partial(hop_kernel, ahead),
        in_specs=[SMEM, VMEM, VMEM],
        out_specs=VMEM,
        out_shape=jax.ShapeDtypeStruct(arrived.shape, jnp.int16),
        compiler_params=params(12),
        cost_estimate=LITTLE,
        name="hop",
    )(place, partial, arrived)


def last_hop_kernel(place_ref, partial_ref, right_ref, left_ref, values_ref):
    rows, width = values_ref.shape
    right = read_message(right_ref, rows)
    left = read_message(left_ref, rows)
    columns = chunk_of(place_ref, 0, partial_ref, width)
    for group in range(rows // GROUP):
        span = slice(group * GROUP, (group + 1) * GROUP)
        total = partial_ref[span, columns] + right(group) + left(group)
        values_ref[span, :] = total.astype(values_ref.dtype)


def last_hop(place, partial, right, left):
    rows, width = right.shape[0] - PAD, right.shape[1]
    return pl.pallas_call(
        last_hop_kernel,
        in_specs=[SMEM, VMEM, VMEM, VMEM],
        out_specs=VMEM,
        out_shape=jax.ShapeDtypeStruct((rows, width), jnp.bfloat16),
        compiler_params=params(12),
        cost_estimate=LITTLE,
        name="last_hop",
    )(place, partial, right, left)


def chunk_order(place):
    return (
        place,
        jnp.where(place == 3, 2, place + 1),
        jnp.where(place == 0, 2, jnp.where(place == 1, 0, 1)),
        jnp.where(place < 2, 3, 0),
    )


def second_chunk(place, r1, l1):
    return jnp.where(place == 3, r1, l1)


def third_chunk(place, r1, r2, l2):
    return jnp.where((place == 1) | (place == 2), r1, r2 + l2)


def fourth_chunk(place, r2, l2, r3, l3):
    return jnp.where((place == 1) | (place == 2), r2 + l2, r3 + l3)


def product(turned, normed_ref, out_ref):
    step = 1024
    for n in range(normed_ref.shape[1] // step):
        span = slice(n * step, (n + 1) * step)
        out_ref[:, span] = jnp.dot(turned, normed_ref[:, span], preferred_element_type=jnp.float32)


def chunk_kernel(pick, place_ref, normed_ref, *refs):
    tokens = normed_ref.shape[0]
    chunk = pick(place_ref[0], *[ref[:tokens, :] for ref in refs[:-1]])
    product(chunk.T, normed_ref, refs[-1])


def chunk_gradient(pick, place, normed, *chunks):
    return pl.pallas_call(
        functools.partial(chunk_kernel, pick),
        in_specs=[SMEM, VMEM] + [VMEM] * len(chunks),
        out_specs=VMEM,
        out_shape=jax.ShapeDtypeStruct((chunks[0].shape[1], normed.shape[1]), jnp.float32),
        compiler_params=params(16),
        cost_estimate=LITTLE,
        name="chunk_gradient",
    )(place, normed, *chunks)


def slots_kernel(
    chips, column_blocks, codes_ref, place_ref, normed_ref, r2, l2, r3, l3, g1, g2, g3, *refs
):
    keep_refs = refs[:chips]
    send_refs = refs[chips : 2 * chips]
    gradient, sems = refs[2 * chips :]
    place = place_ref[0]
    copies = [
        pltpu.make_async_copy(g, gradient.at[i], sems.at[i]) for i, g in enumerate((g1, g2, g3))
    ]
    for copy in copies:
        copy.start()
    tokens = normed_ref.shape[0]
    chunk = fourth_chunk(place, *[ref[:tokens, :] for ref in (r2, l2, r3, l3)])
    product(chunk.T, normed_ref, gradient.at[3])
    for copy in copies:
        copy.wait()
    order = chunk_order(place)
    tile = GROUP
    capacity = keep_refs[0].shape[0] // tile
    chunk_blocks = gradient.shape[1] // tile

    def term(k, slot):
        code = codes_ref[k, slot]
        safe = jnp.maximum(code, 0)
        row, column = safe // column_blocks, safe % column_blocks
        chunk = column // chunk_blocks
        stage = jnp.where(
            chunk == order[0],
            0,
            jnp.where(chunk == order[1], 1, jnp.where(chunk == order[2], 2, 3)),
        )
        block = gradient[stage, aligned(column % chunk_blocks, tile), aligned(row, tile)]
        return jnp.where(code >= 0, block, 0.0)

    for chip in reversed(range(chips)):
        write_message(send_refs[chip], capacity * tile, lambda slot: term(2 * chip + 1, slot))
        for slot in range(capacity):
            keep_refs[chip][slot * tile : (slot + 1) * tile, :] = term(2 * chip, slot)


def slot_terms(codes, place, normed, late, early, capacity, column_blocks):
    features = normed.shape[1]
    chips = codes.shape[0] // 2
    rows = capacity * GROUP
    width = early[0].shape[0]
    shapes = [((rows, GROUP), jnp.float32)] * chips + [((rows + 3 * PAD, GROUP), jnp.int16)] * chips
    outputs = pl.pallas_call(
        functools.partial(slots_kernel, chips, column_blocks),
        in_specs=[SMEM, SMEM, VMEM]
        + [VMEM] * len(late)
        + [pl.BlockSpec(memory_space=pl.ANY)] * len(early),
        out_specs=[VMEM] * len(shapes),
        scratch_shapes=[
            pltpu.VMEM((len(early) + 1, width, features), jnp.float32),
            pltpu.SemaphoreType.DMA((len(early),)),
        ],
        out_shape=[jax.ShapeDtypeStruct(shape, kind) for shape, kind in shapes],
        compiler_params=params(30),
        cost_estimate=LITTLE,
        name="slot_terms",
    )(codes, place, normed, *late, *early)
    return outputs[:chips], outputs[chips:]


def combine_kernel(kept_ref, arrived_ref, out_ref):
    rows = kept_ref.shape[0]
    arrived = read_message(arrived_ref, rows)

    def total(group):
        return kept_ref[group * GROUP : (group + 1) * GROUP, :] + arrived(group)

    if out_ref.dtype == jnp.int16:
        write_message(out_ref, rows, total)
    else:
        for group in range(rows // GROUP):
            out_ref[group * GROUP : (group + 1) * GROUP, :] = total(group)


def combine(kept, arrived, kind):
    shape = arrived.shape if kind == jnp.int16 else kept.shape
    return pl.pallas_call(
        combine_kernel,
        in_specs=[VMEM, VMEM],
        out_specs=VMEM,
        out_shape=jax.ShapeDtypeStruct(shape, kind),
        compiler_params=params(8),
        cost_estimate=LITTLE,
        name="combine",
    )(kept, arrived)


def update_kernel(count, *refs):
    kept_ref, out_ref = refs[0], refs[-1]
    tile = out_ref.shape[-1]
    arrived = [read_message(ref, kept_ref.shape[0]) for ref in refs[1 : 1 + count]]
    for slot in range(out_ref.shape[0]):
        total = kept_ref[slot * tile : (slot + 1) * tile, :]
        for block in arrived:
            total = total + block(slot)
        mean = jnp.sum(total * total) / (tile * tile)
        out_ref[slot] = (total * lax.rsqrt(mean + 1e-06)).T.astype(out_ref.dtype)


def normalized_update(kept, arrived, shape):
    return pl.pallas_call(
        functools.partial(update_kernel, len(arrived)),
        in_specs=[VMEM] * (1 + len(arrived)),
        out_specs=VMEM,
        out_shape=jax.ShapeDtypeStruct(shape, jnp.bfloat16),
        compiler_params=params(12),
        cost_estimate=LITTLE,
        name="normalized_update",
    )(kept, *arrived)


def grad_input_kernel(place_ref, weight_ref, own, r1, r2, r3, l1, l2, l3, out_ref, cotangent):
    @pl.when(pl.program_id(0) == 0)
    def _():
        place = place_ref[0]
        order = chunk_order(place)
        width = own.shape[1]
        arrived = (r1, r2, r3, l1, l2, l3)
        v1, v2, v3, w1, w2, w3 = (ref[: own.shape[0], :] for ref in arrived)
        cotangent[:, aligned(order[0], width)] = own[...]
        cotangent[:, aligned(order[1], width)] = second_chunk(place, v1, w1)
        cotangent[:, aligned(order[2], width)] = third_chunk(place, v1, v2, w2)
        cotangent[:, aligned(order[3], width)] = fourth_chunk(place, v2, w2, v3, w3)

    out_ref[...] = lax.dot_general(
        cotangent[...],
        weight_ref[...],
        (((1,), (1,)), ((), ())),
        preferred_element_type=jnp.float32,
    ).astype(out_ref.dtype)


def grad_inputs(place, weight, *chunks):
    features, width = weight.shape
    tokens = chunks[0].shape[0]
    block = 512
    return pl.pallas_call(
        grad_input_kernel,
        grid_spec=pltpu.PrefetchScalarGridSpec(
            num_scalar_prefetch=1,
            grid=(features // block,),
            in_specs=[pl.BlockSpec((block, width), lambda i, p: (i, 0))]
            + [VMEM] * len(chunks),
            out_specs=pl.BlockSpec((tokens, block), lambda i, p: (0, i)),
            scratch_shapes=[pltpu.VMEM((tokens, width), jnp.bfloat16)],
        ),
        out_shape=jax.ShapeDtypeStruct((tokens, features), jnp.bfloat16),
        compiler_params=params(20),
        cost_estimate=pl.CostEstimate(
            flops=2 * tokens * features * width,
            bytes_accessed=12 * MIB,
            transcendentals=0,
        ),
        name="grad_inputs",
    )(place, weight, *chunks)


def local(devices, parts, normed, tile_values, tile_rows, tile_columns, cotangent):
    capacity, tile = tile_values.shape[1], tile_values.shape[-1]
    column_blocks = cotangent.shape[1] * parts // tile
    chips = devices // 2
    rows = capacity * tile
    place = lax.axis_index("tensor").astype(jnp.int32).reshape(1)

    def swap(x, mask):
        return lax.ppermute(x, "fsdp", [(i, i ^ mask) for i in range(devices)])

    def right(x, *sources):
        return lax.ppermute(x, "tensor", [(i, i + 1) for i in sources])

    def left(x, *sources):
        return lax.ppermute(x, "tensor", [(i, i - 1) for i in sources])

    message, padded = pack(
        tile_rows, tile_columns, tile_values.reshape(rows, tile), cotangent, column_blocks
    )
    r1, l1 = right(padded, 0, 1, 2), left(padded, 3, 2, 1)
    g1 = chunk_gradient(lambda place, own: own, place, normed, cotangent)
    same_core = [message] + [swap(message, 2 * chip) for chip in range(1, chips)]
    beside = swap(message, 1)
    r1, l1, g1, beside = lax.optimization_barrier((r1, l1, g1, beside))
    r2, l2 = right(r1, 1, 2), left(l1, 2, 1)
    g2 = chunk_gradient(second_chunk, place, normed, r1, l1)
    *same_core, g2 = lax.optimization_barrier((*same_core, g2))
    gathered = [same_core[0], beside]
    for m in same_core[1:]:
        gathered += [m, swap(m, 1)]
    r2, l2, *gathered = lax.optimization_barrier((r2, l2, *gathered))
    r3, l3 = right(r2, 2), left(l2, 1)

    weight, first, codes = first_values(place, normed, gathered, parts, column_blocks)
    arrived = lax.ppermute(first, "tensor", [(0, 1), (3, 2)])
    partial = partial_values(normed, weight)
    g3 = chunk_gradient(third_chunk, place, normed, r1, r2, l2)
    g3, partial = lax.optimization_barrier((g3, partial))
    keep, send = slot_terms(
        codes, place, normed, (r2, l2, r3, l3), (g1, g2, g3), capacity, column_blocks
    )
    arrived, keep, send = lax.optimization_barrier((arrived, keep, send))

    second = hop(place, 2, partial, arrived)
    from_left, from_right = right(second, 0, 1), left(second, 3, 2)
    other = [swap(m, 1) for m in send]
    sums = [combine(keep[chip], other[chip], jnp.int16) for chip in range(1, chips)]
    from_left, from_right, _ = lax.optimization_barrier((from_left, from_right, sums))
    terms = [swap(m, 2 * chip) for chip, m in reversed(list(enumerate(sums, 1)))]
    own = combine(keep[0], other[0], jnp.float32)

    from_left = right(hop(place, 1, partial, from_left), 0, 1, 2)
    from_right = left(hop(place, 3, partial, from_right), 3, 2, 1)
    grad_input = grad_inputs(place, weight, cotangent, r1, r2, r3, l1, l2, l3)
    values = last_hop(place, partial, from_left, from_right)
    update = normalized_update(own, terms, tile_values.shape[1:])
    return values, grad_input, update[None]


def solution(mesh):
    in_specs = (
        P("fsdp", "tensor"),
        P("tensor", "fsdp", None, None),
        P("tensor", "fsdp"),
        P("tensor", "fsdp"),
        P("fsdp", "tensor"),
    )
    out_specs = (P("fsdp", "tensor"), P("fsdp", "tensor"), P("tensor", "fsdp", None, None))
    return jax.shard_map(
        functools.partial(local, mesh.shape["fsdp"], mesh.shape["tensor"]),
        mesh=mesh,
        in_specs=in_specs,
        out_specs=out_specs,
        check_vma=False,
    )
```

```python
import functools

import jax
import jax.numpy as jnp
from jax import lax
from jax.experimental import pallas as pl
from jax.experimental.pallas import tpu as pltpu
from jax.sharding import PartitionSpec as P

MIB = 1024 * 1024
GROUP = 128
PAD = 16
EXTRA = 16


def encode(block):
    peak = jnp.max(jnp.abs(block), axis=0, keepdims=True)
    exponent = jnp.floor(jnp.log2(jnp.maximum(peak, 2.0**-100))) + 1.0
    exponent = jnp.clip(exponent, -100.0, 128.0)
    scaled = jnp.round(block * jnp.exp2(15.0 - exponent))
    codes = jnp.clip(scaled, -32767.0, 32767.0).astype(jnp.int32).astype(jnp.int16)
    return codes, exponent


def decode(codes, exponent):
    return codes.astype(jnp.int32).astype(jnp.float32) * jnp.exp2(exponent - 15.0)


def as_code(exponents):
    return exponents.astype(jnp.int32).astype(jnp.int16)


def exponent_rows(codes):
    return codes.astype(jnp.int32).astype(jnp.float32)


def params(mib):
    return pltpu.CompilerParams(vmem_limit_bytes=mib * MIB)


VMEM = pl.BlockSpec(memory_space=pltpu.VMEM)
SMEM = pl.BlockSpec(memory_space=pltpu.SMEM)
LITTLE = pl.CostEstimate(flops=1, bytes_accessed=1, transcendentals=0)


def aligned(index, size):
    return pl.ds(pl.multiple_of(index * size, size), size)


def write_message(message_ref, rows, blocks):
    place = lax.broadcasted_iota(jnp.int32, (PAD, message_ref.shape[1]), 0)
    exponents = jnp.zeros((PAD, message_ref.shape[1]), jnp.float32)
    for group in range(rows // GROUP):
        codes, exponent = encode(blocks(group))
        message_ref[group * GROUP : (group + 1) * GROUP, :] = codes
        exponents = jnp.where(place == group, exponent, exponents)
    message_ref[rows : rows + PAD, :] = as_code(exponents)


def read_message(message_ref, rows):
    exponents = exponent_rows(message_ref[rows : rows + PAD, :])

    def block(group):
        return decode(
            message_ref[group * GROUP : (group + 1) * GROUP, :], exponents[group : group + 1, :]
        )

    return block


def pack_kernel(
    column_blocks, rows_ref, columns_ref, tiles_ref, chunk_ref, message_ref, padded_ref, slots, sems
):
    rows = tiles_ref.shape[0]
    tokens = chunk_ref.shape[0]
    copies = [
        pltpu.make_async_copy(rows_ref, slots.at[0], sems.at[0]),
        pltpu.make_async_copy(columns_ref, slots.at[1], sems.at[1]),
        pltpu.make_async_copy(chunk_ref, padded_ref.at[pl.ds(0, tokens)], sems.at[2]),
        pltpu.make_async_copy(tiles_ref, message_ref.at[pl.ds(0, rows)], sems.at[3]),
    ]
    for copy in copies:
        copy.start()
    padded_ref[tokens:, :] = jnp.zeros((EXTRA, chunk_ref.shape[1]), padded_ref.dtype)
    copies[0].wait()
    copies[1].wait()
    lane = lax.broadcasted_iota(jnp.int32, (PAD, tiles_ref.shape[1]), 1)
    positions = jnp.zeros(lane.shape, jnp.int32)
    for slot in range(rows_ref.shape[1]):
        row, column = slots[0, 0, slot], slots[1, 0, slot]
        position = jnp.where(column >= 0, row * column_blocks + column + 1, 0)
        positions = jnp.where(lane == slot, position, positions)
    message_ref[rows:, :] = positions.astype(jnp.float32).astype(message_ref.dtype)
    copies[2].wait()
    copies[3].wait()


def pack(rows, columns, tiles, chunk, column_blocks):
    return pl.pallas_call(
        functools.partial(pack_kernel, column_blocks),
        in_specs=[pl.BlockSpec(memory_space=pltpu.HBM)] * 4,
        out_specs=[VMEM, VMEM],
        out_shape=[
            jax.ShapeDtypeStruct((tiles.shape[0] + PAD, tiles.shape[1]), tiles.dtype),
            jax.ShapeDtypeStruct((chunk.shape[0] + EXTRA, chunk.shape[1]), chunk.dtype),
        ],
        scratch_shapes=[
            pltpu.SMEM((2,) + rows.shape, jnp.int32),
            pltpu.SemaphoreType.DMA((4,)),
        ],
        compiler_params=params(63),
        cost_estimate=LITTLE,
        name="pack",
    )(rows, columns, tiles, chunk)


def first_kernel(column_blocks, place_ref, normed_ref, *refs):
    message_refs = refs[:-6]
    weight_ref, first_ref, codes_ref, partial, scalars, sem = refs[-6:]
    tokens = normed_ref.shape[0]
    chunk_width = first_ref.shape[1]
    chunks = weight_ref.shape[1] // chunk_width
    tile = message_refs[0].shape[1]
    capacity = message_refs[0].shape[0] // tile
    for k, message_ref in enumerate(message_refs):
        positions = message_ref[capacity * tile : capacity * tile + PAD, :]
        codes_ref[k : k + 1, :] = positions.astype(jnp.float32)[:1, :].astype(jnp.int32) - 1
    copy = pltpu.make_async_copy(codes_ref, scalars, sem)
    copy.start()
    weight_ref[...] = jnp.zeros_like(weight_ref)
    copy.wait()
    for k, message_ref in enumerate(message_refs):
        for slot in range(capacity):
            code = scalars[k, slot]

            @pl.when(code >= 0)
            def _():
                row = aligned(code // column_blocks, tile)
                column = aligned(code % column_blocks, tile)
                weight_ref[row, column] = message_ref[slot * tile : (slot + 1) * tile, :]

    far = weight_ref[:, aligned(chunks - 1 - place_ref[0], chunk_width)]
    partial[...] = jnp.dot(normed_ref[...], far, preferred_element_type=jnp.float32)
    write_message(
        first_ref, tokens, lambda group: partial[group * GROUP : (group + 1) * GROUP, :]
    )


def first_values(place, normed, messages, chunks, column_blocks):
    tokens, features = normed.shape
    tile = messages[0].shape[1]
    width = column_blocks * tile
    return pl.pallas_call(
        functools.partial(first_kernel, column_blocks),
        in_specs=[SMEM, VMEM] + [VMEM] * len(messages),
        out_specs=[VMEM, VMEM, VMEM],
        out_shape=[
            jax.ShapeDtypeStruct((features, width), jnp.bfloat16),
            jax.ShapeDtypeStruct((tokens + PAD, width // chunks), jnp.int16),
            jax.ShapeDtypeStruct((len(messages), tile), jnp.int32),
        ],
        scratch_shapes=[
            pltpu.VMEM((tokens, width // chunks), jnp.float32),
            pltpu.SMEM((len(messages), tile), jnp.int32),
            pltpu.SemaphoreType.DMA,
        ],
        compiler_params=params(22),
        cost_estimate=LITTLE,
        name="first_values",
    )(place, normed, *messages)


def partial_kernel(place_ref, normed_ref, weight_ref, partial_ref, second_ref):
    rows, chunk_width = normed_ref.shape[0], second_ref.shape[1]
    step = 2 * chunk_width
    for n in range(partial_ref.shape[1] // step):
        span = slice(n * step, (n + 1) * step)
        partial_ref[:, span] = jnp.dot(
            normed_ref[...], weight_ref[:, span], preferred_element_type=jnp.float32
        )
    columns = aligned(place_ref[0] ^ 2, chunk_width)
    write_message(
        second_ref, rows, lambda group: partial_ref[group * GROUP : (group + 1) * GROUP, columns]
    )


def partial_values(place, normed, weight, message_shape):
    return pl.pallas_call(
        partial_kernel,
        in_specs=[SMEM, VMEM, VMEM],
        out_specs=[VMEM, VMEM],
        out_shape=[
            jax.ShapeDtypeStruct((normed.shape[0], weight.shape[1]), jnp.float32),
            jax.ShapeDtypeStruct(message_shape, jnp.int16),
        ],
        compiler_params=params(20),
        cost_estimate=LITTLE,
        name="partial_values",
    )(place, normed, weight)


def hop_kernel(pick, place_ref, partial_ref, arrived_ref, message_ref):
    rows, width = partial_ref.shape[0], message_ref.shape[1]
    arrived = read_message(arrived_ref, rows)
    columns = aligned(pick(place_ref[0]), width)

    def total(group):
        return partial_ref[group * GROUP : (group + 1) * GROUP, columns] + arrived(group)

    write_message(message_ref, rows, total)


def hop(pick, place, partial, arrived):
    return pl.pallas_call(
        functools.partial(hop_kernel, pick),
        in_specs=[SMEM, VMEM, VMEM],
        out_specs=VMEM,
        out_shape=jax.ShapeDtypeStruct(arrived.shape, jnp.int16),
        compiler_params=params(12),
        cost_estimate=LITTLE,
        name="hop",
    )(place, partial, arrived)


def last_hop_kernel(place_ref, partial_ref, right_ref, left_ref, values_ref):
    rows, width = values_ref.shape
    right = read_message(right_ref, rows)
    left = read_message(left_ref, rows)
    columns = aligned(place_ref[0], width)
    for group in range(rows // GROUP):
        span = slice(group * GROUP, (group + 1) * GROUP)
        total = partial_ref[span, columns] + right(group) + left(group)
        values_ref[span, :] = total.astype(values_ref.dtype)


def last_hop(place, partial, right, left):
    rows, width = right.shape[0] - PAD, right.shape[1]
    return pl.pallas_call(
        last_hop_kernel,
        in_specs=[SMEM, VMEM, VMEM, VMEM],
        out_specs=VMEM,
        out_shape=jax.ShapeDtypeStruct((rows, width), jnp.bfloat16),
        compiler_params=params(12),
        cost_estimate=LITTLE,
        name="last_hop",
    )(place, partial, right, left)


def chunk_order(place):
    return (
        place,
        place ^ 1,
        jnp.where(place < 2, 2, 1),
        jnp.where(place < 2, 3, 0),
    )


def product(turned, normed_ref, out_ref):
    step = 1024
    for n in range(normed_ref.shape[1] // step):
        span = slice(n * step, (n + 1) * step)
        out_ref[:, span] = jnp.dot(turned, normed_ref[:, span], preferred_element_type=jnp.float32)


def joined(tokens, refs):
    return functools.reduce(jnp.add, [ref[:tokens, :] for ref in refs])


def chunk_kernel(normed_ref, *refs):
    product(joined(normed_ref.shape[0], refs[:-1]).T, normed_ref, refs[-1])


def chunk_gradient(normed, *chunks):
    return pl.pallas_call(
        chunk_kernel,
        in_specs=[VMEM] + [VMEM] * len(chunks),
        out_specs=VMEM,
        out_shape=jax.ShapeDtypeStruct((chunks[0].shape[1], normed.shape[1]), jnp.float32),
        compiler_params=params(16),
        cost_estimate=LITTLE,
        name="chunk_gradient",
    )(normed, *chunks)


def slots_kernel(
    chips, column_blocks, codes_ref, place_ref, normed_ref, m2, d3, g1, g2, g3, *refs
):
    keep_refs = refs[:chips]
    send_refs = refs[chips : 2 * chips]
    gradient, sems = refs[2 * chips :]
    place = place_ref[0]
    copies = [
        pltpu.make_async_copy(g, gradient.at[i], sems.at[i]) for i, g in enumerate((g1, g2, g3))
    ]
    for copy in copies:
        copy.start()
    product(joined(normed_ref.shape[0], (m2, d3)).T, normed_ref, gradient.at[3])
    for copy in copies:
        copy.wait()
    order = chunk_order(place)
    tile = GROUP
    capacity = keep_refs[0].shape[0] // tile
    chunk_blocks = gradient.shape[1] // tile

    def term(k, slot):
        code = codes_ref[k, slot]
        safe = jnp.maximum(code, 0)
        row, column = safe // column_blocks, safe % column_blocks
        chunk = column // chunk_blocks
        stage = jnp.where(
            chunk == order[0],
            0,
            jnp.where(chunk == order[1], 1, jnp.where(chunk == order[2], 2, 3)),
        )
        block = gradient[stage, aligned(column % chunk_blocks, tile), aligned(row, tile)]
        return jnp.where(code >= 0, block, 0.0)

    for chip in reversed(range(chips)):
        write_message(send_refs[chip], capacity * tile, lambda slot: term(2 * chip + 1, slot))
        for slot in range(capacity):
            keep_refs[chip][slot * tile : (slot + 1) * tile, :] = term(2 * chip, slot)


def slot_terms(codes, place, normed, late, early, capacity, column_blocks):
    features = normed.shape[1]
    chips = codes.shape[0] // 2
    rows = capacity * GROUP
    width = early[0].shape[0]
    shapes = [((rows, GROUP), jnp.float32)] * chips + [((rows + 3 * PAD, GROUP), jnp.int16)] * chips
    outputs = pl.pallas_call(
        functools.partial(slots_kernel, chips, column_blocks),
        in_specs=[SMEM, SMEM, VMEM]
        + [VMEM] * len(late)
        + [pl.BlockSpec(memory_space=pl.ANY)] * len(early),
        out_specs=[VMEM] * len(shapes),
        scratch_shapes=[
            pltpu.VMEM((len(early) + 1, width, features), jnp.float32),
            pltpu.SemaphoreType.DMA((len(early),)),
        ],
        out_shape=[jax.ShapeDtypeStruct(shape, kind) for shape, kind in shapes],
        compiler_params=params(30),
        cost_estimate=LITTLE,
        name="slot_terms",
    )(codes, place, normed, *late, *early)
    return outputs[:chips], outputs[chips:]


def combine_kernel(kept_ref, arrived_ref, out_ref):
    rows = kept_ref.shape[0]
    arrived = read_message(arrived_ref, rows)

    def total(group):
        return kept_ref[group * GROUP : (group + 1) * GROUP, :] + arrived(group)

    if out_ref.dtype == jnp.int16:
        write_message(out_ref, rows, total)
    else:
        for group in range(rows // GROUP):
            out_ref[group * GROUP : (group + 1) * GROUP, :] = total(group)


def combine(kept, arrived, kind):
    shape = arrived.shape if kind == jnp.int16 else kept.shape
    return pl.pallas_call(
        combine_kernel,
        in_specs=[VMEM, VMEM],
        out_specs=VMEM,
        out_shape=jax.ShapeDtypeStruct(shape, kind),
        compiler_params=params(8),
        cost_estimate=LITTLE,
        name="combine",
    )(kept, arrived)


def update_kernel(count, *refs):
    kept_ref, out_ref = refs[0], refs[-1]
    tile = out_ref.shape[-1]
    arrived = [read_message(ref, kept_ref.shape[0]) for ref in refs[1 : 1 + count]]
    for slot in range(out_ref.shape[0]):
        total = kept_ref[slot * tile : (slot + 1) * tile, :]
        for block in arrived:
            total = total + block(slot)
        mean = jnp.sum(total * total) / (tile * tile)
        out_ref[slot] = (total * lax.rsqrt(mean + 1e-06)).T.astype(out_ref.dtype)


def normalized_update(kept, arrived, shape):
    return pl.pallas_call(
        functools.partial(update_kernel, len(arrived)),
        in_specs=[VMEM] * (1 + len(arrived)),
        out_specs=VMEM,
        out_shape=jax.ShapeDtypeStruct(shape, jnp.bfloat16),
        compiler_params=params(12),
        cost_estimate=LITTLE,
        name="normalized_update",
    )(kept, *arrived)


def grad_input_kernel(place_ref, weight_ref, own, a1, b1, e2, m2, d3, out_ref, cotangent):
    @pl.when(pl.program_id(0) == 0)
    def _():
        tokens, width = own.shape
        for chunk, refs in zip(chunk_order(place_ref[0]), ((own,), (a1,), (b1, e2), (m2, d3))):
            cotangent[:, aligned(chunk, width)] = joined(tokens, refs)

    out_ref[...] = lax.dot_general(
        cotangent[...],
        weight_ref[...],
        (((1,), (1,)), ((), ())),
        preferred_element_type=jnp.float32,
    ).astype(out_ref.dtype)


def grad_inputs(place, weight, *chunks):
    features, width = weight.shape
    tokens = chunks[0].shape[0]
    block = 512
    return pl.pallas_call(
        grad_input_kernel,
        grid_spec=pltpu.PrefetchScalarGridSpec(
            num_scalar_prefetch=1,
            grid=(features // block,),
            in_specs=[pl.BlockSpec((block, width), lambda i, p: (i, 0))]
            + [VMEM] * len(chunks),
            out_specs=pl.BlockSpec((tokens, block), lambda i, p: (0, i)),
            scratch_shapes=[pltpu.VMEM((tokens, width), jnp.bfloat16)],
        ),
        out_shape=jax.ShapeDtypeStruct((tokens, features), jnp.bfloat16),
        compiler_params=params(20),
        cost_estimate=pl.CostEstimate(
            flops=2 * tokens * features * width,
            bytes_accessed=12 * MIB,
            transcendentals=0,
        ),
        name="grad_inputs",
    )(place, weight, *chunks)


def local(devices, parts, normed, tile_values, tile_rows, tile_columns, cotangent):
    capacity, tile = tile_values.shape[1], tile_values.shape[-1]
    column_blocks = cotangent.shape[1] * parts // tile
    chips = devices // 2
    rows = capacity * tile
    place = lax.axis_index("tensor").astype(jnp.int32).reshape(1)

    def swap(x, mask):
        return lax.ppermute(x, "fsdp", [(i, i ^ mask) for i in range(devices)])

    def pairs(x):
        return lax.ppermute(x, "tensor", [(0, 1), (1, 0), (2, 3), (3, 2)])

    def middle(x):
        return lax.ppermute(x, "tensor", [(1, 2), (2, 1)])

    def outward(x):
        return lax.ppermute(x, "tensor", [(1, 0), (2, 3)])

    def inward(x):
        return lax.ppermute(x, "tensor", [(0, 1), (3, 2)])

    message, padded = pack(
        tile_rows, tile_columns, tile_values.reshape(rows, tile), cotangent, column_blocks
    )
    a1, b1 = pairs(padded), middle(padded)
    g1 = chunk_gradient(normed, cotangent)
    same_core = [message] + [swap(message, 2 * chip) for chip in range(1, chips)]
    beside = swap(message, 1)
    a1, b1, g1, beside = lax.optimization_barrier((a1, b1, g1, beside))
    m2, e2 = middle(a1), outward(b1)
    g2 = chunk_gradient(normed, a1)
    *same_core, g2 = lax.optimization_barrier((*same_core, g2))
    gathered = [same_core[0], beside]
    for m in same_core[1:]:
        gathered += [m, swap(m, 1)]
    d3 = outward(m2)

    weight, first, codes = first_values(place, normed, gathered, parts, column_blocks)
    arrived = inward(first)
    partial, second = partial_values(place, normed, weight, first.shape)
    g3 = chunk_gradient(normed, b1, e2)
    g3, partial, second = lax.optimization_barrier((g3, partial, second))
    keep, send = slot_terms(codes, place, normed, (m2, d3), (g1, g2, g3), capacity, column_blocks)
    arrived, keep, send = lax.optimization_barrier((arrived, keep, send))

    to_middle = inward(second)
    crossing = middle(hop(lambda p: p ^ 2, place, partial, arrived))
    other = [swap(m, 1) for m in send]
    sums = [combine(keep[chip], other[chip], jnp.int16) for chip in range(1, chips)]
    crossing, to_middle, _ = lax.optimization_barrier((crossing, to_middle, sums))
    terms = [swap(m, 2 * chip) for chip, m in reversed(list(enumerate(sums, 1)))]
    own = combine(keep[0], other[0], jnp.float32)

    by_pair = pairs(hop(lambda p: p ^ 1, place, partial, crossing))
    by_middle = middle(hop(lambda p: 3 - p, place, partial, to_middle))
    grad_input = grad_inputs(place, weight, cotangent, a1, b1, e2, m2, d3)
    update = normalized_update(own, terms, tile_values.shape[1:])
    by_pair, by_middle, update = lax.optimization_barrier((by_pair, by_middle, update))
    values = last_hop(place, partial, by_pair, by_middle)
    return values, grad_input, update[None]


def solution(mesh):
    in_specs = (
        P("fsdp", "tensor"),
        P("tensor", "fsdp", None, None),
        P("tensor", "fsdp"),
        P("tensor", "fsdp"),
        P("fsdp", "tensor"),
    )
    out_specs = (P("fsdp", "tensor"), P("fsdp", "tensor"), P("tensor", "fsdp", None, None))
    return jax.shard_map(
        functools.partial(local, mesh.shape["fsdp"], mesh.shape["tensor"]),
        mesh=mesh,
        in_specs=in_specs,
        out_specs=out_specs,
        check_vma=False,
    )
```

```python
import functools

import jax
import jax.numpy as jnp
from jax import lax
from jax.experimental import pallas as pl
from jax.experimental.pallas import tpu as pltpu
from jax.sharding import PartitionSpec as P

MIB = 1024 * 1024
GROUP = 128
PAD = 16
EXTRA = 16


def encode(block):
    peak = jnp.max(jnp.abs(block), axis=0, keepdims=True)
    exponent = jnp.floor(jnp.log2(jnp.maximum(peak, 2.0**-100))) + 1.0
    exponent = jnp.clip(exponent, -100.0, 128.0)
    scaled = jnp.round(block * jnp.exp2(15.0 - exponent))
    codes = jnp.clip(scaled, -32767.0, 32767.0).astype(jnp.int32).astype(jnp.int16)
    return codes, exponent


def decode(codes, exponent):
    return codes.astype(jnp.int32).astype(jnp.float32) * jnp.exp2(exponent - 15.0)


def as_code(exponents):
    return exponents.astype(jnp.int32).astype(jnp.int16)


def exponent_rows(codes):
    return codes.astype(jnp.int32).astype(jnp.float32)


def params(mib):
    return pltpu.CompilerParams(vmem_limit_bytes=mib * MIB)


VMEM = pl.BlockSpec(memory_space=pltpu.VMEM)
SMEM = pl.BlockSpec(memory_space=pltpu.SMEM)
LITTLE = pl.CostEstimate(flops=1, bytes_accessed=1, transcendentals=0)


def aligned(index, size):
    return pl.ds(pl.multiple_of(index * size, size), size)


def write_message(message_ref, rows, blocks):
    place = lax.broadcasted_iota(jnp.int32, (PAD, message_ref.shape[1]), 0)
    exponents = jnp.zeros((PAD, message_ref.shape[1]), jnp.float32)
    for group in range(rows // GROUP):
        codes, exponent = encode(blocks(group))
        message_ref[group * GROUP : (group + 1) * GROUP, :] = codes
        exponents = jnp.where(place == group, exponent, exponents)
    message_ref[rows : rows + PAD, :] = as_code(exponents)


def read_message(message_ref, rows):
    exponents = exponent_rows(message_ref[rows : rows + PAD, :])

    def block(group):
        return decode(
            message_ref[group * GROUP : (group + 1) * GROUP, :], exponents[group : group + 1, :]
        )

    return block


def pack_kernel(
    column_blocks, rows_ref, columns_ref, tiles_ref, chunk_ref, message_ref, padded_ref, slots, sems
):
    rows = tiles_ref.shape[0]
    tokens = chunk_ref.shape[0]
    copies = [
        pltpu.make_async_copy(rows_ref, slots.at[0], sems.at[0]),
        pltpu.make_async_copy(columns_ref, slots.at[1], sems.at[1]),
        pltpu.make_async_copy(chunk_ref, padded_ref.at[pl.ds(0, tokens)], sems.at[2]),
        pltpu.make_async_copy(tiles_ref, message_ref.at[pl.ds(0, rows)], sems.at[3]),
    ]
    for copy in copies:
        copy.start()
    padded_ref[tokens:, :] = jnp.zeros((EXTRA, chunk_ref.shape[1]), padded_ref.dtype)
    copies[0].wait()
    copies[1].wait()
    lane = lax.broadcasted_iota(jnp.int32, (PAD, tiles_ref.shape[1]), 1)
    positions = jnp.zeros(lane.shape, jnp.int32)
    for slot in range(rows_ref.shape[1]):
        row, column = slots[0, 0, slot], slots[1, 0, slot]
        position = jnp.where(column >= 0, row * column_blocks + column + 1, 0)
        positions = jnp.where(lane == slot, position, positions)
    message_ref[rows:, :] = positions.astype(jnp.float32).astype(message_ref.dtype)
    copies[2].wait()
    copies[3].wait()


def pack(rows, columns, tiles, chunk, column_blocks):
    return pl.pallas_call(
        functools.partial(pack_kernel, column_blocks),
        in_specs=[pl.BlockSpec(memory_space=pltpu.HBM)] * 4,
        out_specs=[VMEM, VMEM],
        out_shape=[
            jax.ShapeDtypeStruct((tiles.shape[0] + PAD, tiles.shape[1]), tiles.dtype),
            jax.ShapeDtypeStruct((chunk.shape[0] + EXTRA, chunk.shape[1]), chunk.dtype),
        ],
        scratch_shapes=[
            pltpu.SMEM((2,) + rows.shape, jnp.int32),
            pltpu.SemaphoreType.DMA((4,)),
        ],
        compiler_params=params(63),
        cost_estimate=LITTLE,
        name="pack",
    )(rows, columns, tiles, chunk)


def first_kernel(column_blocks, place_ref, normed_ref, *refs):
    message_refs = refs[:-6]
    weight_ref, first_ref, codes_ref, partial, scalars, sem = refs[-6:]
    tokens = normed_ref.shape[0]
    chunk_width = first_ref.shape[1]
    chunks = weight_ref.shape[1] // chunk_width
    tile = message_refs[0].shape[1]
    capacity = message_refs[0].shape[0] // tile
    for k, message_ref in enumerate(message_refs):
        positions = message_ref[capacity * tile : capacity * tile + PAD, :]
        codes_ref[k : k + 1, :] = positions.astype(jnp.float32)[:1, :].astype(jnp.int32) - 1
    copy = pltpu.make_async_copy(codes_ref, scalars, sem)
    copy.start()
    weight_ref[...] = jnp.zeros_like(weight_ref)
    copy.wait()
    for k, message_ref in enumerate(message_refs):
        for slot in range(capacity):
            code = scalars[k, slot]

            @pl.when(code >= 0)
            def _():
                row = aligned(code // column_blocks, tile)
                column = aligned(code % column_blocks, tile)
                weight_ref[row, column] = message_ref[slot * tile : (slot + 1) * tile, :]

    far = weight_ref[:, aligned(chunks - 1 - place_ref[0], chunk_width)]
    partial[...] = jnp.dot(normed_ref[...], far, preferred_element_type=jnp.float32)
    write_message(
        first_ref, tokens, lambda group: partial[group * GROUP : (group + 1) * GROUP, :]
    )


def first_values(place, normed, messages, chunks, column_blocks):
    tokens, features = normed.shape
    tile = messages[0].shape[1]
    width = column_blocks * tile
    return pl.pallas_call(
        functools.partial(first_kernel, column_blocks),
        in_specs=[SMEM, VMEM] + [VMEM] * len(messages),
        out_specs=[VMEM, VMEM, VMEM],
        out_shape=[
            jax.ShapeDtypeStruct((features, width), jnp.bfloat16),
            jax.ShapeDtypeStruct((tokens + PAD, width // chunks), jnp.int16),
            jax.ShapeDtypeStruct((len(messages), tile), jnp.int32),
        ],
        scratch_shapes=[
            pltpu.VMEM((tokens, width // chunks), jnp.float32),
            pltpu.SMEM((len(messages), tile), jnp.int32),
            pltpu.SemaphoreType.DMA,
        ],
        compiler_params=params(22),
        cost_estimate=LITTLE,
        name="first_values",
    )(place, normed, *messages)


def partial_kernel(place_ref, normed_ref, weight_ref, partial_ref, second_ref):
    rows, chunk_width = normed_ref.shape[0], second_ref.shape[1]
    step = 2 * chunk_width
    for n in range(partial_ref.shape[1] // step):
        span = slice(n * step, (n + 1) * step)
        partial_ref[:, span] = jnp.dot(
            normed_ref[...], weight_ref[:, span], preferred_element_type=jnp.float32
        )
    columns = aligned(place_ref[0] ^ 2, chunk_width)
    write_message(
        second_ref, rows, lambda group: partial_ref[group * GROUP : (group + 1) * GROUP, columns]
    )


def partial_values(place, normed, weight, message_shape):
    return pl.pallas_call(
        partial_kernel,
        in_specs=[SMEM, VMEM, VMEM],
        out_specs=[VMEM, VMEM],
        out_shape=[
            jax.ShapeDtypeStruct((normed.shape[0], weight.shape[1]), jnp.float32),
            jax.ShapeDtypeStruct(message_shape, jnp.int16),
        ],
        compiler_params=params(20),
        cost_estimate=LITTLE,
        name="partial_values",
    )(place, normed, weight)


def hop_kernel(pick, place_ref, partial_ref, arrived_ref, message_ref):
    rows, width = partial_ref.shape[0], message_ref.shape[1]
    arrived = read_message(arrived_ref, rows)
    columns = aligned(pick(place_ref[0]), width)

    def total(group):
        return partial_ref[group * GROUP : (group + 1) * GROUP, columns] + arrived(group)

    write_message(message_ref, rows, total)


def hop(pick, place, partial, arrived):
    return pl.pallas_call(
        functools.partial(hop_kernel, pick),
        in_specs=[SMEM, VMEM, VMEM],
        out_specs=VMEM,
        out_shape=jax.ShapeDtypeStruct(arrived.shape, jnp.int16),
        compiler_params=params(12),
        cost_estimate=LITTLE,
        name="hop",
    )(place, partial, arrived)


def last_hop_kernel(place_ref, partial_ref, right_ref, left_ref, values_ref):
    rows, width = values_ref.shape
    right = read_message(right_ref, rows)
    left = read_message(left_ref, rows)
    columns = aligned(place_ref[0], width)
    for group in range(rows // GROUP):
        span = slice(group * GROUP, (group + 1) * GROUP)
        total = partial_ref[span, columns] + right(group) + left(group)
        values_ref[span, :] = total.astype(values_ref.dtype)


def last_hop(place, partial, right, left):
    rows, width = right.shape[0] - PAD, right.shape[1]
    return pl.pallas_call(
        last_hop_kernel,
        in_specs=[SMEM, VMEM, VMEM, VMEM],
        out_specs=VMEM,
        out_shape=jax.ShapeDtypeStruct((rows, width), jnp.bfloat16),
        compiler_params=params(12),
        cost_estimate=LITTLE,
        name="last_hop",
    )(place, partial, right, left)


def chunk_order(place):
    return (
        place,
        place ^ 1,
        jnp.where(place < 2, 2, 1),
        jnp.where(place < 2, 3, 0),
    )


def product(turned, normed_ref, out_ref):
    step = 1024
    for n in range(normed_ref.shape[1] // step):
        span = slice(n * step, (n + 1) * step)
        out_ref[:, span] = jnp.dot(turned, normed_ref[:, span], preferred_element_type=jnp.float32)


def joined(tokens, refs):
    return functools.reduce(jnp.add, [ref[:tokens, :] for ref in refs])


def chunk_kernel(normed_ref, *refs):
    product(joined(normed_ref.shape[0], refs[:-1]).T, normed_ref, refs[-1])


def own_kernel(normed_ref, chunk_ref, held_ref, out_ref, sem):
    copy = pltpu.make_async_copy(normed_ref, held_ref, sem)
    copy.start()
    turned = chunk_ref[...].T
    copy.wait()
    product(turned, held_ref, out_ref)


def own_gradient(normed, chunk):
    return pl.pallas_call(
        own_kernel,
        in_specs=[pl.BlockSpec(memory_space=pl.ANY), VMEM],
        out_specs=[VMEM, VMEM],
        out_shape=[
            jax.ShapeDtypeStruct(normed.shape, normed.dtype),
            jax.ShapeDtypeStruct((chunk.shape[1], normed.shape[1]), jnp.float32),
        ],
        scratch_shapes=[pltpu.SemaphoreType.DMA],
        compiler_params=params(16),
        cost_estimate=LITTLE,
        name="own_gradient",
    )(normed, chunk)


def chunk_gradient(normed, *chunks):
    return pl.pallas_call(
        chunk_kernel,
        in_specs=[VMEM] + [VMEM] * len(chunks),
        out_specs=VMEM,
        out_shape=jax.ShapeDtypeStruct((chunks[0].shape[1], normed.shape[1]), jnp.float32),
        compiler_params=params(16),
        cost_estimate=LITTLE,
        name="chunk_gradient",
    )(normed, *chunks)


def slots_kernel(
    chips, column_blocks, codes_ref, place_ref, normed_ref, m2, d3, g1, g2, g3, *refs
):
    keep_refs = refs[:chips]
    send_refs = refs[chips : 2 * chips]
    gradient, sems = refs[2 * chips :]
    place = place_ref[0]
    copies = [
        pltpu.make_async_copy(g, gradient.at[i], sems.at[i]) for i, g in enumerate((g1, g2, g3))
    ]
    for copy in copies:
        copy.start()
    product(joined(normed_ref.shape[0], (m2, d3)).T, normed_ref, gradient.at[3])
    for copy in copies:
        copy.wait()
    order = chunk_order(place)
    tile = GROUP
    capacity = keep_refs[0].shape[0] // tile
    chunk_blocks = gradient.shape[1] // tile

    def term(k, slot):
        code = codes_ref[k, slot]
        safe = jnp.maximum(code, 0)
        row, column = safe // column_blocks, safe % column_blocks
        chunk = column // chunk_blocks
        stage = jnp.where(
            chunk == order[0],
            0,
            jnp.where(chunk == order[1], 1, jnp.where(chunk == order[2], 2, 3)),
        )
        block = gradient[stage, aligned(column % chunk_blocks, tile), aligned(row, tile)]
        return jnp.where(code >= 0, block, 0.0)

    for chip in reversed(range(chips)):
        write_message(send_refs[chip], capacity * tile, lambda slot: term(2 * chip + 1, slot))
        for slot in range(capacity):
            keep_refs[chip][slot * tile : (slot + 1) * tile, :] = term(2 * chip, slot)


def slot_terms(codes, place, normed, late, early, capacity, column_blocks):
    features = normed.shape[1]
    chips = codes.shape[0] // 2
    rows = capacity * GROUP
    width = early[0].shape[0]
    shapes = [((rows, GROUP), jnp.float32)] * chips + [((rows + 3 * PAD, GROUP), jnp.int16)] * chips
    outputs = pl.pallas_call(
        functools.partial(slots_kernel, chips, column_blocks),
        in_specs=[SMEM, SMEM, VMEM]
        + [VMEM] * len(late)
        + [pl.BlockSpec(memory_space=pl.ANY)] * len(early),
        out_specs=[VMEM] * len(shapes),
        scratch_shapes=[
            pltpu.VMEM((len(early) + 1, width, features), jnp.float32),
            pltpu.SemaphoreType.DMA((len(early),)),
        ],
        out_shape=[jax.ShapeDtypeStruct(shape, kind) for shape, kind in shapes],
        compiler_params=params(30),
        cost_estimate=LITTLE,
        name="slot_terms",
    )(codes, place, normed, *late, *early)
    return outputs[:chips], outputs[chips:]


def combine_kernel(kept_ref, arrived_ref, out_ref):
    rows = kept_ref.shape[0]
    arrived = read_message(arrived_ref, rows)

    def total(group):
        return kept_ref[group * GROUP : (group + 1) * GROUP, :] + arrived(group)

    if out_ref.dtype == jnp.int16:
        write_message(out_ref, rows, total)
    else:
        for group in range(rows // GROUP):
            out_ref[group * GROUP : (group + 1) * GROUP, :] = total(group)


def combine(kept, arrived, kind):
    shape = arrived.shape if kind == jnp.int16 else kept.shape
    return pl.pallas_call(
        combine_kernel,
        in_specs=[VMEM, VMEM],
        out_specs=VMEM,
        out_shape=jax.ShapeDtypeStruct(shape, kind),
        compiler_params=params(8),
        cost_estimate=LITTLE,
        name="combine",
    )(kept, arrived)


def update_kernel(count, *refs):
    kept_ref, out_ref = refs[0], refs[-1]
    tile = out_ref.shape[-1]
    arrived = [read_message(ref, kept_ref.shape[0]) for ref in refs[1 : 1 + count]]
    for slot in range(out_ref.shape[0]):
        total = kept_ref[slot * tile : (slot + 1) * tile, :]
        for block in arrived:
            total = total + block(slot)
        mean = jnp.sum(total * total) / (tile * tile)
        out_ref[slot] = (total * lax.rsqrt(mean + 1e-06)).T.astype(out_ref.dtype)


def normalized_update(kept, arrived, shape):
    return pl.pallas_call(
        functools.partial(update_kernel, len(arrived)),
        in_specs=[VMEM] * (1 + len(arrived)),
        out_specs=VMEM,
        out_shape=jax.ShapeDtypeStruct(shape, jnp.bfloat16),
        compiler_params=params(12),
        cost_estimate=LITTLE,
        name="normalized_update",
    )(kept, *arrived)


def grad_input_kernel(place_ref, weight_ref, own, a1, b1, e2, m2, d3, out_ref, cotangent):
    @pl.when(pl.program_id(0) == 0)
    def _():
        tokens, width = own.shape
        for chunk, refs in zip(chunk_order(place_ref[0]), ((own,), (a1,), (b1, e2), (m2, d3))):
            cotangent[:, aligned(chunk, width)] = joined(tokens, refs)

    out_ref[...] = lax.dot_general(
        cotangent[...],
        weight_ref[...],
        (((1,), (1,)), ((), ())),
        preferred_element_type=jnp.float32,
    ).astype(out_ref.dtype)


def grad_inputs(place, weight, *chunks):
    features, width = weight.shape
    tokens = chunks[0].shape[0]
    block = 512
    return pl.pallas_call(
        grad_input_kernel,
        grid_spec=pltpu.PrefetchScalarGridSpec(
            num_scalar_prefetch=1,
            grid=(features // block,),
            in_specs=[pl.BlockSpec((block, width), lambda i, p: (i, 0))]
            + [VMEM] * len(chunks),
            out_specs=pl.BlockSpec((tokens, block), lambda i, p: (0, i)),
            scratch_shapes=[pltpu.VMEM((tokens, width), jnp.bfloat16)],
        ),
        out_shape=jax.ShapeDtypeStruct((tokens, features), jnp.bfloat16),
        compiler_params=params(20),
        cost_estimate=pl.CostEstimate(
            flops=2 * tokens * features * width,
            bytes_accessed=12 * MIB,
            transcendentals=0,
        ),
        name="grad_inputs",
    )(place, weight, *chunks)


def local(devices, parts, normed, tile_values, tile_rows, tile_columns, cotangent):
    capacity, tile = tile_values.shape[1], tile_values.shape[-1]
    column_blocks = cotangent.shape[1] * parts // tile
    chips = devices // 2
    rows = capacity * tile
    place = lax.axis_index("tensor").astype(jnp.int32).reshape(1)

    def swap(x, mask):
        return lax.ppermute(x, "fsdp", [(i, i ^ mask) for i in range(devices)])

    def pairs(x):
        return lax.ppermute(x, "tensor", [(0, 1), (1, 0), (2, 3), (3, 2)])

    def middle(x):
        return lax.ppermute(x, "tensor", [(1, 2), (2, 1)])

    def outward(x):
        return lax.ppermute(x, "tensor", [(1, 0), (2, 3)])

    def inward(x):
        return lax.ppermute(x, "tensor", [(0, 1), (3, 2)])

    message, padded = pack(
        tile_rows, tile_columns, tile_values.reshape(rows, tile), cotangent, column_blocks
    )
    a1, b1 = pairs(padded), middle(padded)
    normed, g1 = own_gradient(normed, cotangent)
    same_core = [message] + [swap(message, 2 * chip) for chip in range(1, chips)]
    beside = swap(message, 1)
    a1, b1, g1, beside = lax.optimization_barrier((a1, b1, g1, beside))
    m2, e2 = middle(a1), outward(b1)
    g2 = chunk_gradient(normed, a1)
    *same_core, g2 = lax.optimization_barrier((*same_core, g2))
    gathered = [same_core[0], beside]
    for m in same_core[1:]:
        gathered += [m, swap(m, 1)]
    m2, e2, *gathered = lax.optimization_barrier((m2, e2, *gathered))
    d3 = outward(m2)

    weight, first, codes = first_values(place, normed, gathered, parts, column_blocks)
    arrived = inward(first)
    partial, second = partial_values(place, normed, weight, first.shape)
    g3 = chunk_gradient(normed, b1, e2)
    g3, partial, second = lax.optimization_barrier((g3, partial, second))
    keep, send = slot_terms(codes, place, normed, (m2, d3), (g1, g2, g3), capacity, column_blocks)
    arrived, keep, send = lax.optimization_barrier((arrived, keep, send))

    to_middle = inward(second)
    crossing = middle(hop(lambda p: p ^ 2, place, partial, arrived))
    other = [swap(m, 1) for m in send]
    sums = [combine(keep[chip], other[chip], jnp.int16) for chip in range(1, chips)]
    own = combine(keep[0], other[0], jnp.float32)
    crossing, to_middle, own, _ = lax.optimization_barrier((crossing, to_middle, own, sums))
    terms = [swap(m, 2 * chip) for chip, m in reversed(list(enumerate(sums, 1)))]

    by_pair = pairs(hop(lambda p: p ^ 1, place, partial, crossing))
    by_middle = middle(hop(lambda p: 3 - p, place, partial, to_middle))
    grad_input = grad_inputs(place, weight, cotangent, a1, b1, e2, m2, d3)
    update = normalized_update(own, terms, tile_values.shape[1:])
    by_pair, by_middle, update = lax.optimization_barrier((by_pair, by_middle, update))
    values = last_hop(place, partial, by_pair, by_middle)
    return values, grad_input, update[None]


def solution(mesh):
    in_specs = (
        P("fsdp", "tensor"),
        P("tensor", "fsdp", None, None),
        P("tensor", "fsdp"),
        P("tensor", "fsdp"),
        P("fsdp", "tensor"),
    )
    out_specs = (P("fsdp", "tensor"), P("fsdp", "tensor"), P("tensor", "fsdp", None, None))
    return jax.shard_map(
        functools.partial(local, mesh.shape["fsdp"], mesh.shape["tensor"]),
        mesh=mesh,
        in_specs=in_specs,
        out_specs=out_specs,
        check_vma=False,
    )
```

```python
import functools

import jax
import jax.numpy as jnp
from jax import lax
from jax.experimental import pallas as pl
from jax.experimental.pallas import tpu as pltpu
from jax.sharding import PartitionSpec as P

MIB = 1024 * 1024
GROUP = 128
PAD = 16


def encode(block):
    peak = jnp.max(jnp.abs(block), axis=0, keepdims=True)
    exponent = jnp.floor(jnp.log2(jnp.maximum(peak, 2.0**-100))) + 1.0
    exponent = jnp.clip(exponent, -100.0, 128.0)
    scaled = jnp.round(block * jnp.exp2(15.0 - exponent))
    codes = jnp.clip(scaled, -32767.0, 32767.0).astype(jnp.int32).astype(jnp.int16)
    return codes, exponent


def decode(codes, exponent):
    return codes.astype(jnp.int32).astype(jnp.float32) * jnp.exp2(exponent - 15.0)


def as_code(exponents):
    return exponents.astype(jnp.int32).astype(jnp.int16)


def exponent_rows(codes):
    return codes.astype(jnp.int32).astype(jnp.float32)


def params(mib):
    return pltpu.CompilerParams(vmem_limit_bytes=mib * MIB)


VMEM = pl.BlockSpec(memory_space=pltpu.VMEM)
SMEM = pl.BlockSpec(memory_space=pltpu.SMEM)
LITTLE = pl.CostEstimate(flops=1, bytes_accessed=1, transcendentals=0)


def aligned(index, size):
    return pl.ds(pl.multiple_of(index * size, size), size)


def write_message(message_ref, rows, blocks):
    place = lax.broadcasted_iota(jnp.int32, (PAD, message_ref.shape[1]), 0)
    exponents = jnp.zeros((PAD, message_ref.shape[1]), jnp.float32)
    for group in range(rows // GROUP):
        codes, exponent = encode(blocks(group))
        message_ref[group * GROUP : (group + 1) * GROUP, :] = codes
        exponents = jnp.where(place == group, exponent, exponents)
    message_ref[rows : rows + PAD, :] = as_code(exponents)


def read_message(message_ref, rows):
    exponents = exponent_rows(message_ref[rows : rows + PAD, :])

    def block(group):
        return decode(
            message_ref[group * GROUP : (group + 1) * GROUP, :], exponents[group : group + 1, :]
        )

    return block


def first_kernel(column_blocks, place_ref, normed_ref, *refs):
    message_refs = refs[:-6]
    weight_ref, first_ref, codes_ref, partial, scalars, sem = refs[-6:]
    tokens = normed_ref.shape[0]
    chunk_width = first_ref.shape[1]
    chunks = weight_ref.shape[1] // chunk_width
    tile = message_refs[0].shape[1]
    capacity = message_refs[0].shape[0] // tile
    for k, message_ref in enumerate(message_refs):
        positions = message_ref[capacity * tile : capacity * tile + PAD, :]
        codes_ref[k : k + 1, :] = positions.astype(jnp.float32)[:1, :].astype(jnp.int32) - 1
    copy = pltpu.make_async_copy(codes_ref, scalars, sem)
    copy.start()
    weight_ref[...] = jnp.zeros_like(weight_ref)
    copy.wait()
    features = normed_ref.shape[1]
    for k, message_ref in enumerate(message_refs):
        for slot in range(capacity):
            code = scalars[k, slot]
            filled = code >= 0
            row = jnp.where(filled, code // column_blocks, features // tile)
            column = jnp.where(filled, code % column_blocks, 0)
            weight_ref[aligned(row, tile), aligned(column, tile)] = message_ref[
                slot * tile : (slot + 1) * tile, :
            ]
    far = weight_ref[:features, aligned(chunks - 1 - place_ref[0], chunk_width)]
    partial[...] = jnp.dot(normed_ref[...], far, preferred_element_type=jnp.float32)
    write_message(
        first_ref, tokens, lambda group: partial[group * GROUP : (group + 1) * GROUP, :]
    )


def first_values(place, normed, messages, chunks, column_blocks):
    tokens, features = normed.shape
    tile = messages[0].shape[1]
    width = column_blocks * tile
    return pl.pallas_call(
        functools.partial(first_kernel, column_blocks),
        in_specs=[SMEM, VMEM] + [VMEM] * len(messages),
        out_specs=[VMEM, VMEM, VMEM],
        out_shape=[
            jax.ShapeDtypeStruct((features + tile, width), jnp.bfloat16),
            jax.ShapeDtypeStruct((tokens + PAD, width // chunks), jnp.int16),
            jax.ShapeDtypeStruct((len(messages), tile), jnp.int32),
        ],
        scratch_shapes=[
            pltpu.VMEM((tokens, width // chunks), jnp.float32),
            pltpu.SMEM((len(messages), tile), jnp.int32),
            pltpu.SemaphoreType.DMA,
        ],
        compiler_params=params(22),
        cost_estimate=LITTLE,
        name="first_values",
    )(place, normed, *messages)


def partial_kernel(place_ref, normed_ref, weight_ref, partial_ref, second_ref):
    rows, chunk_width = normed_ref.shape[0], second_ref.shape[1]
    step = 2 * chunk_width
    for n in range(partial_ref.shape[1] // step):
        span = slice(n * step, (n + 1) * step)
        partial_ref[:, span] = jnp.dot(
            normed_ref[...],
            weight_ref[: normed_ref.shape[1], span],
            preferred_element_type=jnp.float32,
        )
    columns = aligned(place_ref[0] ^ 2, chunk_width)
    write_message(
        second_ref, rows, lambda group: partial_ref[group * GROUP : (group + 1) * GROUP, columns]
    )


def partial_values(place, normed, weight, message_shape):
    return pl.pallas_call(
        partial_kernel,
        in_specs=[SMEM, VMEM, VMEM],
        out_specs=[VMEM, VMEM],
        out_shape=[
            jax.ShapeDtypeStruct((normed.shape[0], weight.shape[1]), jnp.float32),
            jax.ShapeDtypeStruct(message_shape, jnp.int16),
        ],
        compiler_params=params(20),
        cost_estimate=LITTLE,
        name="partial_values",
    )(place, normed, weight)


def hop_kernel(pick, place_ref, partial_ref, arrived_ref, message_ref):
    rows, width = partial_ref.shape[0], message_ref.shape[1]
    arrived = read_message(arrived_ref, rows)
    columns = aligned(pick(place_ref[0]), width)

    def total(group):
        return partial_ref[group * GROUP : (group + 1) * GROUP, columns] + arrived(group)

    write_message(message_ref, rows, total)


def hop(pick, place, partial, arrived):
    return pl.pallas_call(
        functools.partial(hop_kernel, pick),
        in_specs=[SMEM, VMEM, VMEM],
        out_specs=VMEM,
        out_shape=jax.ShapeDtypeStruct(arrived.shape, jnp.int16),
        compiler_params=params(12),
        cost_estimate=LITTLE,
        name="hop",
    )(place, partial, arrived)


def last_hop_kernel(place_ref, partial_ref, right_ref, left_ref, values_ref):
    rows, width = values_ref.shape
    right = read_message(right_ref, rows)
    left = read_message(left_ref, rows)
    columns = aligned(place_ref[0], width)
    for group in range(rows // GROUP):
        span = slice(group * GROUP, (group + 1) * GROUP)
        total = partial_ref[span, columns] + right(group) + left(group)
        values_ref[span, :] = total.astype(values_ref.dtype)


def last_hop(place, partial, right, left):
    rows, width = right.shape[0] - PAD, right.shape[1]
    return pl.pallas_call(
        last_hop_kernel,
        in_specs=[SMEM, VMEM, VMEM, VMEM],
        out_specs=VMEM,
        out_shape=jax.ShapeDtypeStruct((rows, width), jnp.bfloat16),
        compiler_params=params(12),
        cost_estimate=LITTLE,
        name="last_hop",
    )(place, partial, right, left)


def chunk_order(place):
    return (
        place,
        place ^ 1,
        jnp.where(place < 2, 2, 1),
        jnp.where(place < 2, 3, 0),
    )


def widen_kernel(chunk_ref, wide_ref):
    tokens = chunk_ref.shape[0]
    wide_ref[:tokens, :] = chunk_ref[...]
    wide_ref[tokens:, :] = jnp.zeros((PAD, chunk_ref.shape[1]), chunk_ref.dtype)


def widen(chunk):
    return pl.pallas_call(
        widen_kernel,
        in_specs=[VMEM],
        out_specs=VMEM,
        out_shape=jax.ShapeDtypeStruct((chunk.shape[0] + PAD, chunk.shape[1]), chunk.dtype),
        compiler_params=params(4),
        cost_estimate=LITTLE,
        name="widen",
    )(chunk)


def product(turned, normed_ref, out_ref):
    step = 1024
    for n in range(normed_ref.shape[1] // step):
        span = slice(n * step, (n + 1) * step)
        out_ref[:, span] = jnp.dot(turned, normed_ref[:, span], preferred_element_type=jnp.float32)


def joined(tokens, refs):
    return functools.reduce(jnp.add, [ref[:tokens, :] for ref in refs])


def chunk_kernel(normed_ref, *refs):
    product(joined(normed_ref.shape[0], refs[:-1]).T, normed_ref, refs[-1])


def own_kernel(normed_ref, chunk_ref, held_ref, out_ref, sem):
    copy = pltpu.make_async_copy(normed_ref, held_ref, sem)
    copy.start()
    turned = chunk_ref[...].T
    copy.wait()
    product(turned, held_ref, out_ref)


def own_gradient(normed, chunk):
    return pl.pallas_call(
        own_kernel,
        in_specs=[pl.BlockSpec(memory_space=pl.ANY), VMEM],
        out_specs=[VMEM, VMEM],
        out_shape=[
            jax.ShapeDtypeStruct(normed.shape, normed.dtype),
            jax.ShapeDtypeStruct((chunk.shape[1], normed.shape[1]), jnp.float32),
        ],
        scratch_shapes=[pltpu.SemaphoreType.DMA],
        compiler_params=params(16),
        cost_estimate=LITTLE,
        name="own_gradient",
    )(normed, chunk)


def chunk_gradient(normed, *chunks):
    return pl.pallas_call(
        chunk_kernel,
        in_specs=[VMEM] + [VMEM] * len(chunks),
        out_specs=VMEM,
        out_shape=jax.ShapeDtypeStruct((chunks[0].shape[1], normed.shape[1]), jnp.float32),
        compiler_params=params(16),
        cost_estimate=LITTLE,
        name="chunk_gradient",
    )(normed, *chunks)


def slots_kernel(
    chips, column_blocks, codes_ref, place_ref, normed_ref, m2, d3, g1, g2, g3, *refs
):
    keep_refs = refs[:chips]
    send_refs = refs[chips : 2 * chips]
    gradient, sems = refs[2 * chips :]
    place = place_ref[0]
    copies = [
        pltpu.make_async_copy(g, gradient.at[i], sems.at[i]) for i, g in enumerate((g1, g2, g3))
    ]
    for copy in copies:
        copy.start()
    product(joined(normed_ref.shape[0], (m2, d3)).T, normed_ref, gradient.at[3])
    for copy in copies:
        copy.wait()
    order = chunk_order(place)
    tile = GROUP
    capacity = keep_refs[0].shape[0] // tile
    chunk_blocks = gradient.shape[1] // tile

    def term(k, slot):
        code = codes_ref[k, slot]
        safe = jnp.maximum(code, 0)
        row, column = safe // column_blocks, safe % column_blocks
        chunk = column // chunk_blocks
        stage = jnp.where(
            chunk == order[0],
            0,
            jnp.where(chunk == order[1], 1, jnp.where(chunk == order[2], 2, 3)),
        )
        block = gradient[stage, aligned(column % chunk_blocks, tile), aligned(row, tile)]
        return jnp.where(code >= 0, block, 0.0)

    for chip in reversed(range(chips)):
        write_message(send_refs[chip], capacity * tile, lambda slot: term(2 * chip + 1, slot))
        for slot in range(capacity):
            keep_refs[chip][slot * tile : (slot + 1) * tile, :] = term(2 * chip, slot)


def slot_terms(codes, place, normed, late, early, capacity, column_blocks):
    features = normed.shape[1]
    chips = codes.shape[0] // 2
    rows = capacity * GROUP
    width = early[0].shape[0]
    shapes = [((rows, GROUP), jnp.float32)] * chips + [((rows + 3 * PAD, GROUP), jnp.int16)] * chips
    outputs = pl.pallas_call(
        functools.partial(slots_kernel, chips, column_blocks),
        in_specs=[SMEM, SMEM, VMEM]
        + [VMEM] * len(late)
        + [pl.BlockSpec(memory_space=pl.ANY)] * len(early),
        out_specs=[VMEM] * len(shapes),
        scratch_shapes=[
            pltpu.VMEM((len(early) + 1, width, features), jnp.float32),
            pltpu.SemaphoreType.DMA((len(early),)),
        ],
        out_shape=[jax.ShapeDtypeStruct(shape, kind) for shape, kind in shapes],
        compiler_params=params(30),
        cost_estimate=LITTLE,
        name="slot_terms",
    )(codes, place, normed, *late, *early)
    return outputs[:chips], outputs[chips:]


def combine_kernel(kept_ref, arrived_ref, out_ref):
    rows = kept_ref.shape[0]
    arrived = read_message(arrived_ref, rows)

    def total(group):
        return kept_ref[group * GROUP : (group + 1) * GROUP, :] + arrived(group)

    if out_ref.dtype == jnp.int16:
        write_message(out_ref, rows, total)
    else:
        for group in range(rows // GROUP):
            out_ref[group * GROUP : (group + 1) * GROUP, :] = total(group)


def combine(kept, arrived, kind):
    shape = arrived.shape if kind == jnp.int16 else kept.shape
    return pl.pallas_call(
        combine_kernel,
        in_specs=[VMEM, VMEM],
        out_specs=VMEM,
        out_shape=jax.ShapeDtypeStruct(shape, kind),
        compiler_params=params(8),
        cost_estimate=LITTLE,
        name="combine",
    )(kept, arrived)


def update_kernel(count, *refs):
    kept_ref, out_ref = refs[0], refs[-1]
    tile = out_ref.shape[-1]
    arrived = [read_message(ref, kept_ref.shape[0]) for ref in refs[1 : 1 + count]]
    for slot in range(out_ref.shape[0]):
        total = kept_ref[slot * tile : (slot + 1) * tile, :]
        for block in arrived:
            total = total + block(slot)
        mean = jnp.sum(total * total) / (tile * tile)
        out_ref[slot] = (total * lax.rsqrt(mean + 1e-06)).T.astype(out_ref.dtype)


def normalized_update(kept, arrived, shape):
    return pl.pallas_call(
        functools.partial(update_kernel, len(arrived)),
        in_specs=[VMEM] * (1 + len(arrived)),
        out_specs=VMEM,
        out_shape=jax.ShapeDtypeStruct(shape, jnp.bfloat16),
        compiler_params=params(12),
        cost_estimate=LITTLE,
        name="normalized_update",
    )(kept, *arrived)


def grad_input_kernel(place_ref, weight_ref, own, a1, b1, e2, m2, d3, out_ref, cotangent):
    @pl.when(pl.program_id(0) == 0)
    def _():
        tokens, width = own.shape
        for chunk, refs in zip(chunk_order(place_ref[0]), ((own,), (a1,), (b1, e2), (m2, d3))):
            cotangent[:, aligned(chunk, width)] = joined(tokens, refs)

    out_ref[...] = lax.dot_general(
        cotangent[...],
        weight_ref[...],
        (((1,), (1,)), ((), ())),
        preferred_element_type=jnp.float32,
    ).astype(out_ref.dtype)


def grad_inputs(place, features, weight, *chunks):
    width = weight.shape[1]
    tokens = chunks[0].shape[0]
    block = 512
    return pl.pallas_call(
        grad_input_kernel,
        grid_spec=pltpu.PrefetchScalarGridSpec(
            num_scalar_prefetch=1,
            grid=(features // block,),
            in_specs=[pl.BlockSpec((block, width), lambda i, p: (i, 0))]
            + [VMEM] * len(chunks),
            out_specs=pl.BlockSpec((tokens, block), lambda i, p: (0, i)),
            scratch_shapes=[pltpu.VMEM((tokens, width), jnp.bfloat16)],
        ),
        out_shape=jax.ShapeDtypeStruct((tokens, features), jnp.bfloat16),
        compiler_params=params(20),
        cost_estimate=pl.CostEstimate(
            flops=2 * tokens * features * width,
            bytes_accessed=12 * MIB,
            transcendentals=0,
        ),
        name="grad_inputs",
    )(place, weight, *chunks)


def local(devices, parts, normed, tile_values, tile_rows, tile_columns, cotangent):
    capacity, tile = tile_values.shape[1], tile_values.shape[-1]
    column_blocks = cotangent.shape[1] * parts // tile
    chips = devices // 2
    rows = capacity * tile
    place = lax.axis_index("tensor").astype(jnp.int32).reshape(1)

    def swap(x, mask):
        return lax.ppermute(x, "fsdp", [(i, i ^ mask) for i in range(devices)])

    def pairs(x):
        return lax.ppermute(x, "tensor", [(0, 1), (1, 0), (2, 3), (3, 2)])

    def middle(x):
        return lax.ppermute(x, "tensor", [(1, 2), (2, 1)])

    def outward(x):
        return lax.ppermute(x, "tensor", [(1, 0), (2, 3)])

    def inward(x):
        return lax.ppermute(x, "tensor", [(0, 1), (3, 2)])

    positions = jnp.where(tile_columns >= 0, tile_rows * column_blocks + tile_columns + 1, 0)
    positions = jnp.pad(positions.astype(jnp.bfloat16), ((0, PAD - 1), (0, tile - capacity)))
    message = jnp.concatenate([tile_values.reshape(rows, tile), positions], axis=0)
    wide = widen(cotangent)
    a1, b1 = pairs(wide), middle(wide)
    normed, g1 = own_gradient(normed, cotangent)
    same_core = [message] + [swap(message, 2 * chip) for chip in range(1, chips)]
    beside = swap(message, 1)
    a1, b1, g1, beside = lax.optimization_barrier((a1, b1, g1, beside))
    m2, e2 = middle(a1), outward(b1)
    g2 = chunk_gradient(normed, a1)
    *same_core, g2 = lax.optimization_barrier((*same_core, g2))
    gathered = [same_core[0], beside]
    for m in same_core[1:]:
        gathered += [m, swap(m, 1)]
    m2, e2, *gathered = lax.optimization_barrier((m2, e2, *gathered))
    d3 = outward(m2)

    weight, first, codes = first_values(place, normed, gathered, parts, column_blocks)
    arrived = inward(first)
    partial, second = partial_values(place, normed, weight, first.shape)
    g3 = chunk_gradient(normed, b1, e2)
    g3, partial, second = lax.optimization_barrier((g3, partial, second))
    keep, send = slot_terms(codes, place, normed, (m2, d3), (g1, g2, g3), capacity, column_blocks)
    arrived, keep, send = lax.optimization_barrier((arrived, keep, send))

    to_middle = inward(second)
    crossing = middle(hop(lambda p: p ^ 2, place, partial, arrived))
    other = [swap(m, 1) for m in send]
    sums = [combine(keep[chip], other[chip], jnp.int16) for chip in range(1, chips)]
    own = combine(keep[0], other[0], jnp.float32)
    crossing, to_middle, own, _ = lax.optimization_barrier((crossing, to_middle, own, sums))
    terms = [swap(m, 2 * chip) for chip, m in reversed(list(enumerate(sums, 1)))]

    by_pair = pairs(hop(lambda p: p ^ 1, place, partial, crossing))
    by_middle = middle(hop(lambda p: 3 - p, place, partial, to_middle))
    grad_input = grad_inputs(place, normed.shape[1], weight, cotangent, a1, b1, e2, m2, d3)
    update = normalized_update(own, terms, tile_values.shape[1:])
    by_pair, by_middle, update = lax.optimization_barrier((by_pair, by_middle, update))
    values = last_hop(place, partial, by_pair, by_middle)
    return values, grad_input, update[None]


def solution(mesh):
    in_specs = (
        P("fsdp", "tensor"),
        P("tensor", "fsdp", None, None),
        P("tensor", "fsdp"),
        P("tensor", "fsdp"),
        P("fsdp", "tensor"),
    )
    out_specs = (P("fsdp", "tensor"), P("fsdp", "tensor"), P("tensor", "fsdp", None, None))
    return jax.shard_map(
        functools.partial(local, mesh.shape["fsdp"], mesh.shape["tensor"]),
        mesh=mesh,
        in_specs=in_specs,
        out_specs=out_specs,
        check_vma=False,
    )
```

```python
import functools

import jax
import jax.numpy as jnp
from jax import lax
from jax.experimental import pallas as pl
from jax.experimental.pallas import tpu as pltpu
from jax.sharding import PartitionSpec as P

MIB = 1024 * 1024
GROUP = 128
PAD = 16


def encode(block):
    peak = jnp.max(jnp.abs(block), axis=0, keepdims=True)
    exponent = jnp.floor(jnp.log2(jnp.maximum(peak, 2.0**-100))) + 1.0
    exponent = jnp.clip(exponent, -100.0, 128.0)
    scaled = jnp.round(block * jnp.exp2(15.0 - exponent))
    codes = jnp.clip(scaled, -32767.0, 32767.0).astype(jnp.int32).astype(jnp.int16)
    return codes, exponent


def decode(codes, exponent):
    return codes.astype(jnp.int32).astype(jnp.float32) * jnp.exp2(exponent - 15.0)


def as_code(exponents):
    return exponents.astype(jnp.int32).astype(jnp.int16)


def exponent_rows(codes):
    return codes.astype(jnp.int32).astype(jnp.float32)


def params(mib):
    return pltpu.CompilerParams(vmem_limit_bytes=mib * MIB)


VMEM = pl.BlockSpec(memory_space=pltpu.VMEM)
SMEM = pl.BlockSpec(memory_space=pltpu.SMEM)
LITTLE = pl.CostEstimate(flops=1, bytes_accessed=1, transcendentals=0)


def aligned(index, size):
    return pl.ds(pl.multiple_of(index * size, size), size)


def write_message(message_ref, rows, blocks):
    place = lax.broadcasted_iota(jnp.int32, (PAD, message_ref.shape[1]), 0)
    exponents = jnp.zeros((PAD, message_ref.shape[1]), jnp.float32)
    for group in range(rows // GROUP):
        codes, exponent = encode(blocks(group))
        message_ref[group * GROUP : (group + 1) * GROUP, :] = codes
        exponents = jnp.where(place == group, exponent, exponents)
    message_ref[rows : rows + PAD, :] = as_code(exponents)


def read_message(message_ref, rows):
    exponents = exponent_rows(message_ref[rows : rows + PAD, :])

    def block(group):
        return decode(
            message_ref[group * GROUP : (group + 1) * GROUP, :], exponents[group : group + 1, :]
        )

    return block


def first_kernel(column_blocks, place_ref, normed_ref, *refs):
    message_refs = refs[:-6]
    weight_ref, first_ref, codes_ref, partial, scalars, sem = refs[-6:]
    tokens = normed_ref.shape[0]
    chunk_width = first_ref.shape[1]
    chunks = weight_ref.shape[1] // chunk_width
    tile = message_refs[0].shape[1]
    capacity = message_refs[0].shape[0] // tile
    for k, message_ref in enumerate(message_refs):
        positions = message_ref[capacity * tile : capacity * tile + PAD, :]
        codes_ref[k : k + 1, :] = positions.astype(jnp.float32)[:1, :].astype(jnp.int32) - 1
    copy = pltpu.make_async_copy(codes_ref, scalars, sem)
    copy.start()
    weight_ref[...] = jnp.zeros_like(weight_ref)
    copy.wait()
    features = normed_ref.shape[1]
    for k, message_ref in enumerate(message_refs):
        for slot in range(capacity):
            code = scalars[k, slot]
            filled = code >= 0
            row = jnp.where(filled, code // column_blocks, features // tile)
            column = jnp.where(filled, code % column_blocks, 0)
            weight_ref[aligned(row, tile), aligned(column, tile)] = message_ref[
                slot * tile : (slot + 1) * tile, :
            ]
    far = weight_ref[:features, aligned(chunks - 1 - place_ref[0], chunk_width)]
    partial[...] = jnp.dot(normed_ref[...], far, preferred_element_type=jnp.float32)
    write_message(
        first_ref, tokens, lambda group: partial[group * GROUP : (group + 1) * GROUP, :]
    )


def first_values(place, normed, messages, chunks, column_blocks):
    tokens, features = normed.shape
    tile = messages[0].shape[1]
    width = column_blocks * tile
    return pl.pallas_call(
        functools.partial(first_kernel, column_blocks),
        in_specs=[SMEM, VMEM] + [VMEM] * len(messages),
        out_specs=[VMEM, VMEM, VMEM],
        out_shape=[
            jax.ShapeDtypeStruct((features + tile, width), jnp.bfloat16),
            jax.ShapeDtypeStruct((tokens + PAD, width // chunks), jnp.int16),
            jax.ShapeDtypeStruct((len(messages), tile), jnp.int32),
        ],
        scratch_shapes=[
            pltpu.VMEM((tokens, width // chunks), jnp.float32),
            pltpu.SMEM((len(messages), tile), jnp.int32),
            pltpu.SemaphoreType.DMA,
        ],
        compiler_params=params(17),
        cost_estimate=LITTLE,
        name="first_values",
    )(place, normed, *messages)


def partial_kernel(place_ref, normed_ref, weight_ref, partial_ref, second_ref):
    rows, chunk_width = normed_ref.shape[0], second_ref.shape[1]
    step = 2 * chunk_width
    for n in range(partial_ref.shape[1] // step):
        span = slice(n * step, (n + 1) * step)
        partial_ref[:, span] = jnp.dot(
            normed_ref[...],
            weight_ref[: normed_ref.shape[1], span],
            preferred_element_type=jnp.float32,
        )
    columns = aligned(place_ref[0] ^ 2, chunk_width)
    write_message(
        second_ref, rows, lambda group: partial_ref[group * GROUP : (group + 1) * GROUP, columns]
    )


def partial_values(place, normed, weight, message_shape):
    return pl.pallas_call(
        partial_kernel,
        in_specs=[SMEM, VMEM, VMEM],
        out_specs=[VMEM, VMEM],
        out_shape=[
            jax.ShapeDtypeStruct((normed.shape[0], weight.shape[1]), jnp.float32),
            jax.ShapeDtypeStruct(message_shape, jnp.int16),
        ],
        compiler_params=params(16),
        cost_estimate=LITTLE,
        name="partial_values",
    )(place, normed, weight)


def hop_kernel(pick, place_ref, partial_ref, arrived_ref, message_ref):
    rows, width = partial_ref.shape[0], message_ref.shape[1]
    arrived = read_message(arrived_ref, rows)
    columns = aligned(pick(place_ref[0]), width)

    def total(group):
        return partial_ref[group * GROUP : (group + 1) * GROUP, columns] + arrived(group)

    write_message(message_ref, rows, total)


def hop(pick, place, partial, arrived):
    return pl.pallas_call(
        functools.partial(hop_kernel, pick),
        in_specs=[SMEM, VMEM, VMEM],
        out_specs=VMEM,
        out_shape=jax.ShapeDtypeStruct(arrived.shape, jnp.int16),
        compiler_params=params(8),
        cost_estimate=LITTLE,
        name="hop",
    )(place, partial, arrived)


def last_hop_kernel(place_ref, partial_ref, right_ref, left_ref, values_ref):
    rows, width = values_ref.shape
    right = read_message(right_ref, rows)
    left = read_message(left_ref, rows)
    columns = aligned(place_ref[0], width)
    for group in range(rows // GROUP):
        span = slice(group * GROUP, (group + 1) * GROUP)
        total = partial_ref[span, columns] + right(group) + left(group)
        values_ref[span, :] = total.astype(values_ref.dtype)


def last_hop(place, partial, right, left):
    rows, width = right.shape[0] - PAD, right.shape[1]
    return pl.pallas_call(
        last_hop_kernel,
        in_specs=[SMEM, VMEM, VMEM, VMEM],
        out_specs=VMEM,
        out_shape=jax.ShapeDtypeStruct((rows, width), jnp.bfloat16),
        compiler_params=params(8),
        cost_estimate=LITTLE,
        name="last_hop",
    )(place, partial, right, left)


def chunk_order(place):
    return (
        place,
        place ^ 1,
        jnp.where(place < 2, 2, 1),
        jnp.where(place < 2, 3, 0),
    )


def product(turned, normed_ref, out_ref):
    step = 1024
    for n in range(normed_ref.shape[1] // step):
        span = slice(n * step, (n + 1) * step)
        out_ref[:, span] = jnp.dot(turned, normed_ref[:, span], preferred_element_type=jnp.float32)


def joined(tokens, refs):
    return functools.reduce(jnp.add, [ref[:tokens, :] for ref in refs])


def chunk_kernel(normed_ref, *refs):
    product(joined(normed_ref.shape[0], refs[:-1]).T, normed_ref, refs[-1])


def own_kernel(normed_ref, chunk_ref, held_ref, out_ref, sem):
    copy = pltpu.make_async_copy(normed_ref, held_ref, sem)
    copy.start()
    turned = chunk_ref[...].T
    copy.wait()
    product(turned, held_ref, out_ref)


def own_gradient(normed, chunk):
    return pl.pallas_call(
        own_kernel,
        in_specs=[pl.BlockSpec(memory_space=pl.ANY), VMEM],
        out_specs=[VMEM, VMEM],
        out_shape=[
            jax.ShapeDtypeStruct(normed.shape, normed.dtype),
            jax.ShapeDtypeStruct((chunk.shape[1], normed.shape[1]), jnp.float32),
        ],
        scratch_shapes=[pltpu.SemaphoreType.DMA],
        compiler_params=params(10),
        cost_estimate=LITTLE,
        name="own_gradient",
    )(normed, chunk)


def chunk_gradient(normed, *chunks):
    return pl.pallas_call(
        chunk_kernel,
        in_specs=[VMEM] + [VMEM] * len(chunks),
        out_specs=VMEM,
        out_shape=jax.ShapeDtypeStruct((chunks[0].shape[1], normed.shape[1]), jnp.float32),
        compiler_params=params(10),
        cost_estimate=LITTLE,
        name="chunk_gradient",
    )(normed, *chunks)


def slots_kernel(
    chips, column_blocks, codes_ref, place_ref, normed_ref, m2, d3, g1, g2, g3, *refs
):
    keep_refs = refs[:chips]
    send_refs = refs[chips : 2 * chips]
    gradient, sems = refs[2 * chips :]
    place = place_ref[0]
    copies = [
        pltpu.make_async_copy(g, gradient.at[i], sems.at[i]) for i, g in enumerate((g1, g2, g3))
    ]
    for copy in copies:
        copy.start()
    product(joined(normed_ref.shape[0], (m2, d3)).T, normed_ref, gradient.at[3])
    for copy in copies:
        copy.wait()
    order = chunk_order(place)
    tile = GROUP
    capacity = keep_refs[0].shape[0] // tile
    chunk_blocks = gradient.shape[1] // tile

    def term(k, slot):
        code = codes_ref[k, slot]
        safe = jnp.maximum(code, 0)
        row, column = safe // column_blocks, safe % column_blocks
        chunk = column // chunk_blocks
        stage = jnp.where(
            chunk == order[0],
            0,
            jnp.where(chunk == order[1], 1, jnp.where(chunk == order[2], 2, 3)),
        )
        block = gradient[stage, aligned(column % chunk_blocks, tile), aligned(row, tile)]
        return jnp.where(code >= 0, block, 0.0)

    for chip in reversed(range(chips)):
        write_message(send_refs[chip], capacity * tile, lambda slot: term(2 * chip + 1, slot))
        for slot in range(capacity):
            keep_refs[chip][slot * tile : (slot + 1) * tile, :] = term(2 * chip, slot)


def slot_terms(codes, place, normed, late, early, capacity, column_blocks):
    features = normed.shape[1]
    chips = codes.shape[0] // 2
    rows = capacity * GROUP
    width = early[0].shape[0]
    shapes = [((rows, GROUP), jnp.float32)] * chips + [((rows + 3 * PAD, GROUP), jnp.int16)] * chips
    outputs = pl.pallas_call(
        functools.partial(slots_kernel, chips, column_blocks),
        in_specs=[SMEM, SMEM, VMEM]
        + [VMEM] * len(late)
        + [pl.BlockSpec(memory_space=pl.ANY)] * len(early),
        out_specs=[VMEM] * len(shapes),
        scratch_shapes=[
            pltpu.VMEM((len(early) + 1, width, features), jnp.float32),
            pltpu.SemaphoreType.DMA((len(early),)),
        ],
        out_shape=[jax.ShapeDtypeStruct(shape, kind) for shape, kind in shapes],
        compiler_params=params(22),
        cost_estimate=LITTLE,
        name="slot_terms",
    )(codes, place, normed, *late, *early)
    return outputs[:chips], outputs[chips:]


def combine_kernel(kept_ref, arrived_ref, out_ref):
    rows = kept_ref.shape[0]
    arrived = read_message(arrived_ref, rows)

    def total(group):
        return kept_ref[group * GROUP : (group + 1) * GROUP, :] + arrived(group)

    if out_ref.dtype == jnp.int16:
        write_message(out_ref, rows, total)
    else:
        for group in range(rows // GROUP):
            out_ref[group * GROUP : (group + 1) * GROUP, :] = total(group)


def combine(kept, arrived, kind):
    shape = arrived.shape if kind == jnp.int16 else kept.shape
    return pl.pallas_call(
        combine_kernel,
        in_specs=[VMEM, VMEM],
        out_specs=VMEM,
        out_shape=jax.ShapeDtypeStruct(shape, kind),
        compiler_params=params(5),
        cost_estimate=LITTLE,
        name="combine",
    )(kept, arrived)


def update_kernel(count, *refs):
    kept_ref, out_ref = refs[0], refs[-1]
    tile = out_ref.shape[-1]
    arrived = [read_message(ref, kept_ref.shape[0]) for ref in refs[1 : 1 + count]]
    for slot in range(out_ref.shape[0]):
        total = kept_ref[slot * tile : (slot + 1) * tile, :]
        for block in arrived:
            total = total + block(slot)
        mean = jnp.sum(total * total) / (tile * tile)
        out_ref[slot] = (total * lax.rsqrt(mean + 1e-06)).T.astype(out_ref.dtype)


def normalized_update(kept, arrived, shape):
    return pl.pallas_call(
        functools.partial(update_kernel, len(arrived)),
        in_specs=[VMEM] * (1 + len(arrived)),
        out_specs=VMEM,
        out_shape=jax.ShapeDtypeStruct(shape, jnp.bfloat16),
        compiler_params=params(6),
        cost_estimate=LITTLE,
        name="normalized_update",
    )(kept, *arrived)


def grad_input_kernel(place_ref, weight_ref, own, a1, b1, e2, m2, d3, out_ref, cotangent):
    @pl.when(pl.program_id(0) == 0)
    def _():
        tokens, width = own.shape
        for chunk, refs in zip(chunk_order(place_ref[0]), ((own,), (a1,), (b1, e2), (m2, d3))):
            cotangent[:, aligned(chunk, width)] = joined(tokens, refs)

    out_ref[...] = lax.dot_general(
        cotangent[...],
        weight_ref[...],
        (((1,), (1,)), ((), ())),
        preferred_element_type=jnp.float32,
    ).astype(out_ref.dtype)


def grad_inputs(place, features, weight, *chunks):
    width = weight.shape[1]
    tokens = chunks[0].shape[0]
    block = 512
    return pl.pallas_call(
        grad_input_kernel,
        grid_spec=pltpu.PrefetchScalarGridSpec(
            num_scalar_prefetch=1,
            grid=(features // block,),
            in_specs=[pl.BlockSpec((block, width), lambda i, p: (i, 0))]
            + [VMEM] * len(chunks),
            out_specs=pl.BlockSpec((tokens, block), lambda i, p: (0, i)),
            scratch_shapes=[pltpu.VMEM((tokens, width), jnp.bfloat16)],
        ),
        out_shape=jax.ShapeDtypeStruct((tokens, features), jnp.bfloat16),
        compiler_params=params(14),
        cost_estimate=pl.CostEstimate(
            flops=2 * tokens * features * width,
            bytes_accessed=12 * MIB,
            transcendentals=0,
        ),
        name="grad_inputs",
    )(place, weight, *chunks)


def local(devices, parts, normed, tile_values, tile_rows, tile_columns, cotangent):
    capacity, tile = tile_values.shape[1], tile_values.shape[-1]
    column_blocks = cotangent.shape[1] * parts // tile
    chips = devices // 2
    rows = capacity * tile
    place = lax.axis_index("tensor").astype(jnp.int32).reshape(1)

    def swap(x, mask):
        return lax.ppermute(x, "fsdp", [(i, i ^ mask) for i in range(devices)])

    def pairs(x):
        return lax.ppermute(x, "tensor", [(0, 1), (1, 0), (2, 3), (3, 2)])

    def middle(x):
        return lax.ppermute(x, "tensor", [(1, 2), (2, 1)])

    def outward(x):
        return lax.ppermute(x, "tensor", [(1, 0), (2, 3)])

    def inward(x):
        return lax.ppermute(x, "tensor", [(0, 1), (3, 2)])

    positions = jnp.where(tile_columns >= 0, tile_rows * column_blocks + tile_columns + 1, 0)
    positions = jnp.pad(positions.astype(jnp.bfloat16), ((0, PAD - 1), (0, tile - capacity)))
    message = jnp.concatenate([tile_values.reshape(rows, tile), positions], axis=0)
    same_core = [message] + [swap(message, 2 * chip) for chip in range(1, chips)]
    a1, b1 = pairs(cotangent), middle(cotangent)
    normed, g1 = own_gradient(normed, cotangent)
    a1, b1, g1, *same_core = lax.optimization_barrier((a1, b1, g1, *same_core))
    m2, e2 = middle(a1), outward(b1)
    gathered = []
    for m in same_core:
        gathered += [m, swap(m, 1)]

    weight, first, codes = first_values(place, normed, gathered, parts, column_blocks)
    arrived = inward(first)
    m2, e2, codes = lax.optimization_barrier((m2, e2, codes))
    d3 = outward(m2)
    g2 = chunk_gradient(normed, a1)
    g3 = chunk_gradient(normed, b1, e2)
    partial, second = partial_values(place, normed, weight, first.shape)
    arrived, d3, g2, g3, partial = lax.optimization_barrier((arrived, d3, g2, g3, partial))
    third = hop(lambda p: p ^ 2, place, partial, arrived)
    third, second, codes = lax.optimization_barrier((third, second, codes))
    keep, send = slot_terms(codes, place, normed, (m2, d3), (g1, g2, g3), capacity, column_blocks)

    to_middle = inward(second)
    crossing = middle(third)
    other = [swap(m, 1) for m in send]
    sums = [combine(keep[chip], other[chip], jnp.int16) for chip in range(1, chips)]
    own = combine(keep[0], other[0], jnp.float32)
    crossing, to_middle, own, _ = lax.optimization_barrier((crossing, to_middle, own, sums))
    terms = [swap(m, 2 * chip) for chip, m in reversed(list(enumerate(sums, 1)))]

    by_pair = pairs(hop(lambda p: p ^ 1, place, partial, crossing))
    by_middle = middle(hop(lambda p: 3 - p, place, partial, to_middle))
    grad_input = grad_inputs(place, normed.shape[1], weight, cotangent, a1, b1, e2, m2, d3)
    update = normalized_update(own, terms, tile_values.shape[1:])
    by_pair, by_middle, update = lax.optimization_barrier((by_pair, by_middle, update))
    values = last_hop(place, partial, by_pair, by_middle)
    return values, grad_input, update[None]


def solution(mesh):
    in_specs = (
        P("fsdp", "tensor"),
        P("tensor", "fsdp", None, None),
        P("tensor", "fsdp"),
        P("tensor", "fsdp"),
        P("fsdp", "tensor"),
    )
    out_specs = (P("fsdp", "tensor"), P("fsdp", "tensor"), P("tensor", "fsdp", None, None))
    return jax.shard_map(
        functools.partial(local, mesh.shape["fsdp"], mesh.shape["tensor"]),
        mesh=mesh,
        in_specs=in_specs,
        out_specs=out_specs,
        check_vma=False,
    )
```

```python
import functools

import jax
import jax.numpy as jnp
from jax import lax
from jax.experimental import pallas as pl
from jax.experimental.pallas import tpu as pltpu
from jax.sharding import PartitionSpec as P

MIB = 1024 * 1024
GROUP = 128
PAD = 16
WIDE = 48


def encode(block):
    peak = jnp.max(jnp.abs(block), axis=0, keepdims=True)
    exponent = jnp.floor(jnp.log2(jnp.maximum(peak, 2.0**-100))) + 1.0
    exponent = jnp.clip(exponent, -100.0, 128.0)
    scaled = jnp.round(block * jnp.exp2(15.0 - exponent))
    codes = jnp.clip(scaled, -32767.0, 32767.0).astype(jnp.int32).astype(jnp.int16)
    return codes, exponent


def decode(codes, exponent):
    return codes.astype(jnp.int32).astype(jnp.float32) * jnp.exp2(exponent - 15.0)


def as_code(exponents):
    return exponents.astype(jnp.int32).astype(jnp.int16)


def exponent_rows(codes):
    return codes.astype(jnp.int32).astype(jnp.float32)


def params(mib):
    return pltpu.CompilerParams(vmem_limit_bytes=mib * MIB)


VMEM = pl.BlockSpec(memory_space=pltpu.VMEM)
SMEM = pl.BlockSpec(memory_space=pltpu.SMEM)
LITTLE = pl.CostEstimate(flops=1, bytes_accessed=1, transcendentals=0)


def aligned(index, size):
    return pl.ds(pl.multiple_of(index * size, size), size)


def write_message(message_ref, rows, blocks):
    place = lax.broadcasted_iota(jnp.int32, (PAD, message_ref.shape[1]), 0)
    exponents = jnp.zeros((PAD, message_ref.shape[1]), jnp.float32)
    for group in range(rows // GROUP):
        codes, exponent = encode(blocks(group))
        message_ref[group * GROUP : (group + 1) * GROUP, :] = codes
        exponents = jnp.where(place == group, exponent, exponents)
    message_ref[rows : rows + PAD, :] = as_code(exponents)


def read_message(message_ref, rows):
    exponents = exponent_rows(message_ref[rows : rows + PAD, :])

    def block(group):
        return decode(
            message_ref[group * GROUP : (group + 1) * GROUP, :], exponents[group : group + 1, :]
        )

    return block


def assembly_kernel(column_blocks, features, *refs):
    message_refs = refs[:-4]
    weight_ref, codes_ref, scalars, sem = refs[-4:]
    tile = message_refs[0].shape[1]
    capacity = message_refs[0].shape[0] // tile
    for k, message_ref in enumerate(message_refs):
        positions = message_ref[capacity * tile : capacity * tile + PAD, :]
        codes_ref[k : k + 1, :] = positions.astype(jnp.float32)[:1, :].astype(jnp.int32) - 1
    copy = pltpu.make_async_copy(codes_ref, scalars, sem)
    copy.start()
    weight_ref[...] = jnp.zeros_like(weight_ref)
    copy.wait()
    for k, message_ref in enumerate(message_refs):
        for slot in range(capacity):
            code = scalars[k, slot]
            filled = code >= 0
            row = jnp.where(filled, code // column_blocks, features // tile)
            column = jnp.where(filled, code % column_blocks, 0)
            weight_ref[aligned(row, tile), aligned(column, tile)] = message_ref[
                slot * tile : (slot + 1) * tile, :
            ]


def assembled(messages, features, column_blocks):
    tile = messages[0].shape[1]
    count = len(messages)
    return pl.pallas_call(
        functools.partial(assembly_kernel, column_blocks, features),
        in_specs=[VMEM] * count,
        out_specs=[VMEM, VMEM],
        out_shape=[
            jax.ShapeDtypeStruct((features + tile, column_blocks * tile), jnp.bfloat16),
            jax.ShapeDtypeStruct((count, tile), jnp.int32),
        ],
        scratch_shapes=[
            pltpu.SMEM((count, tile), jnp.int32),
            pltpu.SemaphoreType.DMA,
        ],
        compiler_params=params(12),
        cost_estimate=LITTLE,
        name="assembled",
    )(*messages)


def first_kernel(place_ref, normed_ref, weight_ref, first_ref, partial):
    tokens, features = normed_ref.shape
    chunk_width = first_ref.shape[1]
    chunks = weight_ref.shape[1] // chunk_width
    far = weight_ref[:features, aligned(chunks - 1 - place_ref[0], chunk_width)]
    partial[...] = jnp.dot(normed_ref[...], far, preferred_element_type=jnp.float32)
    write_message(
        first_ref, tokens, lambda group: partial[group * GROUP : (group + 1) * GROUP, :]
    )


def first_values(place, normed, weight, chunks):
    tokens = normed.shape[0]
    width = weight.shape[1] // chunks
    return pl.pallas_call(
        first_kernel,
        in_specs=[SMEM, VMEM, VMEM],
        out_specs=VMEM,
        out_shape=jax.ShapeDtypeStruct((tokens + PAD, width), jnp.int16),
        scratch_shapes=[pltpu.VMEM((tokens, width), jnp.float32)],
        compiler_params=params(14),
        cost_estimate=LITTLE,
        name="first_values",
    )(place, normed, weight)


def partial_kernel(place_ref, normed_ref, weight_ref, partial_ref, second_ref):
    rows, chunk_width = normed_ref.shape[0], second_ref.shape[1]
    step = 2 * chunk_width
    for n in range(partial_ref.shape[1] // step):
        span = slice(n * step, (n + 1) * step)
        partial_ref[:, span] = jnp.dot(
            normed_ref[...],
            weight_ref[: normed_ref.shape[1], span],
            preferred_element_type=jnp.float32,
        )
    columns = aligned(place_ref[0] ^ 2, chunk_width)
    write_message(
        second_ref, rows, lambda group: partial_ref[group * GROUP : (group + 1) * GROUP, columns]
    )


def partial_values(place, normed, weight, message_shape):
    return pl.pallas_call(
        partial_kernel,
        in_specs=[SMEM, VMEM, VMEM],
        out_specs=[VMEM, VMEM],
        out_shape=[
            jax.ShapeDtypeStruct((normed.shape[0], weight.shape[1]), jnp.float32),
            jax.ShapeDtypeStruct(message_shape, jnp.int16),
        ],
        compiler_params=params(16),
        cost_estimate=LITTLE,
        name="partial_values",
    )(place, normed, weight)


def hop_kernel(pick, place_ref, partial_ref, arrived_ref, message_ref):
    rows, width = partial_ref.shape[0], message_ref.shape[1]
    arrived = read_message(arrived_ref, rows)
    columns = aligned(pick(place_ref[0]), width)

    def total(group):
        return partial_ref[group * GROUP : (group + 1) * GROUP, columns] + arrived(group)

    write_message(message_ref, rows, total)


def hop(pick, place, partial, arrived):
    return pl.pallas_call(
        functools.partial(hop_kernel, pick),
        in_specs=[SMEM, VMEM, VMEM],
        out_specs=VMEM,
        out_shape=jax.ShapeDtypeStruct(arrived.shape, jnp.int16),
        compiler_params=params(8),
        cost_estimate=LITTLE,
        name="hop",
    )(place, partial, arrived)


def last_hop_kernel(place_ref, partial_ref, right_ref, left_ref, values_ref):
    rows, width = values_ref.shape
    right = read_message(right_ref, rows)
    left = read_message(left_ref, rows)
    columns = aligned(place_ref[0], width)
    for group in range(rows // GROUP):
        span = slice(group * GROUP, (group + 1) * GROUP)
        total = partial_ref[span, columns] + right(group) + left(group)
        values_ref[span, :] = total.astype(values_ref.dtype)


def last_hop(place, partial, right, left):
    rows, width = right.shape[0] - PAD, right.shape[1]
    return pl.pallas_call(
        last_hop_kernel,
        in_specs=[SMEM, VMEM, VMEM, VMEM],
        out_specs=VMEM,
        out_shape=jax.ShapeDtypeStruct((rows, width), jnp.bfloat16),
        compiler_params=params(8),
        cost_estimate=LITTLE,
        name="last_hop",
    )(place, partial, right, left)


def chunk_order(place):
    return (
        place,
        place ^ 1,
        jnp.where(place < 2, 2, 1),
        jnp.where(place < 2, 3, 0),
    )


def widen_kernel(a_ref, b_ref, wide_a_ref, wide_b_ref):
    tokens = a_ref.shape[0]
    for ref, wide_ref in ((a_ref, wide_a_ref), (b_ref, wide_b_ref)):
        wide_ref[:tokens, :] = ref[...]
        wide_ref[tokens:, :] = jnp.zeros((WIDE, ref.shape[1]), ref.dtype)


def widen(a, b):
    shape = (a.shape[0] + WIDE, a.shape[1])
    return pl.pallas_call(
        widen_kernel,
        in_specs=[VMEM, VMEM],
        out_specs=[VMEM, VMEM],
        out_shape=[jax.ShapeDtypeStruct(shape, a.dtype)] * 2,
        compiler_params=params(5),
        cost_estimate=LITTLE,
        name="widen",
    )(a, b)


def product(turned, normed_ref, out_ref):
    step = 1024
    for n in range(normed_ref.shape[1] // step):
        span = slice(n * step, (n + 1) * step)
        out_ref[:, span] = jnp.dot(turned, normed_ref[:, span], preferred_element_type=jnp.float32)


def joined(tokens, refs):
    return functools.reduce(jnp.add, [ref[:tokens, :] for ref in refs])


def chunk_kernel(normed_ref, *refs):
    product(joined(normed_ref.shape[0], refs[:-1]).T, normed_ref, refs[-1])


def own_kernel(normed_ref, chunk_ref, held_ref, out_ref, sem):
    copy = pltpu.make_async_copy(normed_ref, held_ref, sem)
    copy.start()
    turned = chunk_ref[...].T
    copy.wait()
    product(turned, held_ref, out_ref)


def own_gradient(normed, chunk):
    return pl.pallas_call(
        own_kernel,
        in_specs=[pl.BlockSpec(memory_space=pl.ANY), VMEM],
        out_specs=[VMEM, VMEM],
        out_shape=[
            jax.ShapeDtypeStruct(normed.shape, normed.dtype),
            jax.ShapeDtypeStruct((chunk.shape[1], normed.shape[1]), jnp.float32),
        ],
        scratch_shapes=[pltpu.SemaphoreType.DMA],
        compiler_params=params(10),
        cost_estimate=LITTLE,
        name="own_gradient",
    )(normed, chunk)


def chunk_gradient(normed, *chunks):
    return pl.pallas_call(
        chunk_kernel,
        in_specs=[VMEM] + [VMEM] * len(chunks),
        out_specs=VMEM,
        out_shape=jax.ShapeDtypeStruct((chunks[0].shape[1], normed.shape[1]), jnp.float32),
        compiler_params=params(10),
        cost_estimate=LITTLE,
        name="chunk_gradient",
    )(normed, *chunks)


def slots_kernel(
    chips, column_blocks, codes_ref, place_ref, normed_ref, m2, d3, g1, g2, g3, *refs
):
    keep_refs = refs[:chips]
    send_refs = refs[chips : 2 * chips]
    gradient, sems = refs[2 * chips :]
    place = place_ref[0]
    copies = [
        pltpu.make_async_copy(g, gradient.at[i], sems.at[i]) for i, g in enumerate((g1, g2, g3))
    ]
    for copy in copies:
        copy.start()
    product(joined(normed_ref.shape[0], (m2, d3)).T, normed_ref, gradient.at[3])
    for copy in copies:
        copy.wait()
    order = chunk_order(place)
    tile = GROUP
    capacity = keep_refs[0].shape[0] // tile
    chunk_blocks = gradient.shape[1] // tile

    def term(k, slot):
        code = codes_ref[k, slot]
        safe = jnp.maximum(code, 0)
        row, column = safe // column_blocks, safe % column_blocks
        chunk = column // chunk_blocks
        stage = jnp.where(
            chunk == order[0],
            0,
            jnp.where(chunk == order[1], 1, jnp.where(chunk == order[2], 2, 3)),
        )
        block = gradient[stage, aligned(column % chunk_blocks, tile), aligned(row, tile)]
        return jnp.where(code >= 0, block, 0.0)

    for chip in reversed(range(chips)):
        write_message(send_refs[chip], capacity * tile, lambda slot: term(2 * chip + 1, slot))
        for slot in range(capacity):
            keep_refs[chip][slot * tile : (slot + 1) * tile, :] = term(2 * chip, slot)


def slot_terms(codes, place, normed, late, early, capacity, column_blocks):
    features = normed.shape[1]
    chips = codes.shape[0] // 2
    rows = capacity * GROUP
    width = early[0].shape[0]
    shapes = [((rows, GROUP), jnp.float32)] * chips + [((rows + 3 * PAD, GROUP), jnp.int16)] * chips
    outputs = pl.pallas_call(
        functools.partial(slots_kernel, chips, column_blocks),
        in_specs=[SMEM, SMEM, VMEM]
        + [VMEM] * len(late)
        + [pl.BlockSpec(memory_space=pl.ANY)] * len(early),
        out_specs=[VMEM] * len(shapes),
        scratch_shapes=[
            pltpu.VMEM((len(early) + 1, width, features), jnp.float32),
            pltpu.SemaphoreType.DMA((len(early),)),
        ],
        out_shape=[jax.ShapeDtypeStruct(shape, kind) for shape, kind in shapes],
        compiler_params=params(22),
        cost_estimate=LITTLE,
        name="slot_terms",
    )(codes, place, normed, *late, *early)
    return outputs[:chips], outputs[chips:]


def combine_kernel(kept_ref, arrived_ref, out_ref):
    rows = kept_ref.shape[0]
    arrived = read_message(arrived_ref, rows)

    def total(group):
        return kept_ref[group * GROUP : (group + 1) * GROUP, :] + arrived(group)

    if out_ref.dtype == jnp.int16:
        write_message(out_ref, rows, total)
    else:
        for group in range(rows // GROUP):
            out_ref[group * GROUP : (group + 1) * GROUP, :] = total(group)


def combine(kept, arrived, kind):
    shape = arrived.shape if kind == jnp.int16 else kept.shape
    return pl.pallas_call(
        combine_kernel,
        in_specs=[VMEM, VMEM],
        out_specs=VMEM,
        out_shape=jax.ShapeDtypeStruct(shape, kind),
        compiler_params=params(5),
        cost_estimate=LITTLE,
        name="combine",
    )(kept, arrived)


def update_kernel(count, *refs):
    kept_ref, out_ref = refs[0], refs[-1]
    tile = out_ref.shape[-1]
    arrived = [read_message(ref, kept_ref.shape[0]) for ref in refs[1 : 1 + count]]
    for slot in range(out_ref.shape[0]):
        total = kept_ref[slot * tile : (slot + 1) * tile, :]
        for block in arrived:
            total = total + block(slot)
        mean = jnp.sum(total * total) / (tile * tile)
        out_ref[slot] = (total * lax.rsqrt(mean + 1e-06)).T.astype(out_ref.dtype)


def normalized_update(kept, arrived, shape):
    return pl.pallas_call(
        functools.partial(update_kernel, len(arrived)),
        in_specs=[VMEM] * (1 + len(arrived)),
        out_specs=VMEM,
        out_shape=jax.ShapeDtypeStruct(shape, jnp.bfloat16),
        compiler_params=params(6),
        cost_estimate=LITTLE,
        name="normalized_update",
    )(kept, *arrived)


def grad_input_kernel(place_ref, weight_ref, own, a1, b1, e2, m2, d3, out_ref, cotangent):
    @pl.when(pl.program_id(0) == 0)
    def _():
        tokens, width = own.shape
        for chunk, refs in zip(chunk_order(place_ref[0]), ((own,), (a1,), (b1, e2), (m2, d3))):
            cotangent[:, aligned(chunk, width)] = joined(tokens, refs)

    out_ref[...] = lax.dot_general(
        cotangent[...],
        weight_ref[...],
        (((1,), (1,)), ((), ())),
        preferred_element_type=jnp.float32,
    ).astype(out_ref.dtype)


def grad_inputs(place, features, weight, *chunks):
    width = weight.shape[1]
    tokens = chunks[0].shape[0]
    block = 512
    return pl.pallas_call(
        grad_input_kernel,
        grid_spec=pltpu.PrefetchScalarGridSpec(
            num_scalar_prefetch=1,
            grid=(features // block,),
            in_specs=[pl.BlockSpec((block, width), lambda i, p: (i, 0))]
            + [VMEM] * len(chunks),
            out_specs=pl.BlockSpec((tokens, block), lambda i, p: (0, i)),
            scratch_shapes=[pltpu.VMEM((tokens, width), jnp.bfloat16)],
        ),
        out_shape=jax.ShapeDtypeStruct((tokens, features), jnp.bfloat16),
        compiler_params=params(14),
        cost_estimate=pl.CostEstimate(
            flops=2 * tokens * features * width,
            bytes_accessed=12 * MIB,
            transcendentals=0,
        ),
        name="grad_inputs",
    )(place, weight, *chunks)


def local(devices, parts, normed, tile_values, tile_rows, tile_columns, cotangent):
    capacity, tile = tile_values.shape[1], tile_values.shape[-1]
    column_blocks = cotangent.shape[1] * parts // tile
    chips = devices // 2
    rows = capacity * tile
    place = lax.axis_index("tensor").astype(jnp.int32).reshape(1)

    def swap(x, mask):
        return lax.ppermute(x, "fsdp", [(i, i ^ mask) for i in range(devices)])

    def pairs(x):
        return lax.ppermute(x, "tensor", [(0, 1), (1, 0), (2, 3), (3, 2)])

    def middle(x):
        return lax.ppermute(x, "tensor", [(1, 2), (2, 1)])

    def outward(x):
        return lax.ppermute(x, "tensor", [(1, 0), (2, 3)])

    def inward(x):
        return lax.ppermute(x, "tensor", [(0, 1), (3, 2)])

    positions = jnp.where(tile_columns >= 0, tile_rows * column_blocks + tile_columns + 1, 0)
    positions = jnp.pad(positions.astype(jnp.bfloat16), ((0, PAD - 1), (0, tile - capacity)))
    message = jnp.concatenate([tile_values.reshape(rows, tile), positions], axis=0)
    direct = [1, 2] if chips == 4 else list(range(1, chips))
    same_core = [message] + [swap(message, 2 * chip) for chip in direct]
    beside = swap(message, 1)
    a1, b1 = pairs(cotangent), middle(cotangent)
    normed, g1 = own_gradient(normed, cotangent)
    a1, b1, g1, beside, *same_core = lax.optimization_barrier((a1, b1, g1, beside, *same_core))
    wide_a, wide_b = widen(a1, b1)
    m2, e2 = middle(wide_a), outward(wide_b)
    g2 = chunk_gradient(normed, a1)
    across = [beside] + [swap(m, 1) for m in same_core[1:]]
    if chips == 4:
        even = lax.axis_index("fsdp") % 2 == 0
        diagonal = lax.ppermute(
            jnp.where(even, same_core[2], same_core[1]),
            "fsdp",
            [(i, i ^ 2 if i % 2 == 0 else i ^ 4) for i in range(devices)],
        )
        diagonal, g2 = lax.optimization_barrier((diagonal, g2))
        same_core.append(diagonal)
        across.append(swap(diagonal, 1))
    gathered = []
    for pair in zip(same_core, across):
        gathered += pair

    weight, codes = assembled(gathered, normed.shape[1], column_blocks)
    first = first_values(place, normed, weight, parts)
    arrived = inward(first)
    m2, e2, codes, _ = lax.optimization_barrier((m2, e2, codes, first))
    d3 = outward(m2)
    g3 = chunk_gradient(normed, b1, e2)
    partial, second = partial_values(place, normed, weight, first.shape)
    arrived, d3, g2, g3, partial = lax.optimization_barrier((arrived, d3, g2, g3, partial))
    third = hop(lambda p: p ^ 2, place, partial, arrived)
    third, second, codes = lax.optimization_barrier((third, second, codes))
    keep, send = slot_terms(codes, place, normed, (m2, d3), (g1, g2, g3), capacity, column_blocks)

    to_middle = inward(second)
    crossing = middle(third)
    other = [swap(m, 1) for m in send]
    sums = [combine(keep[chip], other[chip], jnp.int16) for chip in range(1, chips)]
    own = combine(keep[0], other[0], jnp.float32)
    crossing, to_middle, own, _ = lax.optimization_barrier((crossing, to_middle, own, sums))
    terms = [swap(m, 2 * chip) for chip, m in reversed(list(enumerate(sums, 1)))]

    by_pair = pairs(hop(lambda p: p ^ 1, place, partial, crossing))
    by_middle = middle(hop(lambda p: 3 - p, place, partial, to_middle))
    grad_input = grad_inputs(place, normed.shape[1], weight, cotangent, a1, b1, e2, m2, d3)
    update = normalized_update(own, terms, tile_values.shape[1:])
    by_pair, by_middle, update = lax.optimization_barrier((by_pair, by_middle, update))
    values = last_hop(place, partial, by_pair, by_middle)
    return values, grad_input, update[None]


def solution(mesh):
    in_specs = (
        P("fsdp", "tensor"),
        P("tensor", "fsdp", None, None),
        P("tensor", "fsdp"),
        P("tensor", "fsdp"),
        P("fsdp", "tensor"),
    )
    out_specs = (P("fsdp", "tensor"), P("fsdp", "tensor"), P("tensor", "fsdp", None, None))
    return jax.shard_map(
        functools.partial(local, mesh.shape["fsdp"], mesh.shape["tensor"]),
        mesh=mesh,
        in_specs=in_specs,
        out_specs=out_specs,
        check_vma=False,
    )
```

```python
import functools

import jax
import jax.numpy as jnp
from jax import lax
from jax.experimental import pallas as pl
from jax.experimental.pallas import tpu as pltpu
from jax.sharding import PartitionSpec as P

MIB = 1024 * 1024
GROUP = 128
PAD = 16


def encode(block):
    peak = jnp.max(jnp.abs(block), axis=0, keepdims=True)
    exponent = jnp.floor(jnp.log2(jnp.maximum(peak, 2.0**-100))) + 1.0
    exponent = jnp.clip(exponent, -100.0, 128.0)
    scaled = jnp.round(block * jnp.exp2(15.0 - exponent))
    codes = jnp.clip(scaled, -32767.0, 32767.0).astype(jnp.int32).astype(jnp.int16)
    return codes, exponent


def decode(codes, exponent):
    return codes.astype(jnp.int32).astype(jnp.float32) * jnp.exp2(exponent - 15.0)


def as_code(exponents):
    return exponents.astype(jnp.int32).astype(jnp.int16)


def exponent_rows(codes):
    return codes.astype(jnp.int32).astype(jnp.float32)


def params(mib):
    return pltpu.CompilerParams(vmem_limit_bytes=mib * MIB)


VMEM = pl.BlockSpec(memory_space=pltpu.VMEM)
SMEM = pl.BlockSpec(memory_space=pltpu.SMEM)
LITTLE = pl.CostEstimate(flops=1, bytes_accessed=1, transcendentals=0)


def aligned(index, size):
    return pl.ds(pl.multiple_of(index * size, size), size)


def write_message(message_ref, rows, blocks):
    place = lax.broadcasted_iota(jnp.int32, (PAD, message_ref.shape[1]), 0)
    exponents = jnp.zeros((PAD, message_ref.shape[1]), jnp.float32)
    for group in range(rows // GROUP):
        codes, exponent = encode(blocks(group))
        message_ref[group * GROUP : (group + 1) * GROUP, :] = codes
        exponents = jnp.where(place == group, exponent, exponents)
    message_ref[rows : rows + PAD, :] = as_code(exponents)


def read_message(message_ref, rows):
    exponents = exponent_rows(message_ref[rows : rows + PAD, :])

    def block(group):
        return decode(
            message_ref[group * GROUP : (group + 1) * GROUP, :], exponents[group : group + 1, :]
        )

    return block


def assembly_kernel(column_blocks, features, *refs):
    message_refs = refs[:-4]
    weight_ref, codes_ref, scalars, sem = refs[-4:]
    tile = message_refs[0].shape[1]
    capacity = message_refs[0].shape[0] // tile
    for k, message_ref in enumerate(message_refs):
        positions = message_ref[capacity * tile : capacity * tile + PAD, :]
        codes_ref[k : k + 1, :] = positions.astype(jnp.float32)[:1, :].astype(jnp.int32) - 1
    copy = pltpu.make_async_copy(codes_ref, scalars, sem)
    copy.start()
    weight_ref[...] = jnp.zeros_like(weight_ref)
    copy.wait()
    for k, message_ref in enumerate(message_refs):
        for slot in range(capacity):
            code = scalars[k, slot]
            filled = code >= 0
            row = jnp.where(filled, code // column_blocks, features // tile)
            column = jnp.where(filled, code % column_blocks, 0)
            weight_ref[aligned(row, tile), aligned(column, tile)] = message_ref[
                slot * tile : (slot + 1) * tile, :
            ]


def assembled(messages, features, column_blocks):
    tile = messages[0].shape[1]
    count = len(messages)
    return pl.pallas_call(
        functools.partial(assembly_kernel, column_blocks, features),
        in_specs=[VMEM] * count,
        out_specs=[VMEM, VMEM],
        out_shape=[
            jax.ShapeDtypeStruct((features + tile, column_blocks * tile), jnp.bfloat16),
            jax.ShapeDtypeStruct((count, tile), jnp.int32),
        ],
        scratch_shapes=[
            pltpu.SMEM((count, tile), jnp.int32),
            pltpu.SemaphoreType.DMA,
        ],
        compiler_params=params(12),
        cost_estimate=pl.CostEstimate(flops=0, bytes_accessed=8 * MIB, transcendentals=0),
        name="assembled",
    )(*messages)


def first_kernel(place_ref, normed_ref, weight_ref, first_ref, partial):
    tokens, features = normed_ref.shape
    chunk_width = first_ref.shape[1]
    chunks = weight_ref.shape[1] // chunk_width
    far = weight_ref[:features, aligned(chunks - 1 - place_ref[0], chunk_width)]
    partial[...] = jnp.dot(normed_ref[...], far, preferred_element_type=jnp.float32)
    write_message(
        first_ref, tokens, lambda group: partial[group * GROUP : (group + 1) * GROUP, :]
    )


def first_values(place, normed, weight, chunks):
    tokens = normed.shape[0]
    width = weight.shape[1] // chunks
    return pl.pallas_call(
        first_kernel,
        in_specs=[SMEM, VMEM, VMEM],
        out_specs=VMEM,
        out_shape=jax.ShapeDtypeStruct((tokens + PAD, width), jnp.int16),
        scratch_shapes=[pltpu.VMEM((tokens, width), jnp.float32)],
        compiler_params=params(14),
        cost_estimate=LITTLE,
        name="first_values",
    )(place, normed, weight)


def partial_kernel(place_ref, normed_ref, weight_ref, partial_ref, second_ref):
    rows, chunk_width = normed_ref.shape[0], second_ref.shape[1]
    step = 2 * chunk_width
    for n in range(partial_ref.shape[1] // step):
        span = slice(n * step, (n + 1) * step)
        partial_ref[:, span] = jnp.dot(
            normed_ref[...],
            weight_ref[: normed_ref.shape[1], span],
            preferred_element_type=jnp.float32,
        )
    columns = aligned(place_ref[0] ^ 2, chunk_width)
    write_message(
        second_ref, rows, lambda group: partial_ref[group * GROUP : (group + 1) * GROUP, columns]
    )


def partial_values(place, normed, weight, message_shape):
    return pl.pallas_call(
        partial_kernel,
        in_specs=[SMEM, VMEM, VMEM],
        out_specs=[VMEM, VMEM],
        out_shape=[
            jax.ShapeDtypeStruct((normed.shape[0], weight.shape[1]), jnp.float32),
            jax.ShapeDtypeStruct(message_shape, jnp.int16),
        ],
        compiler_params=params(16),
        cost_estimate=LITTLE,
        name="partial_values",
    )(place, normed, weight)


def hop_kernel(pick, place_ref, partial_ref, arrived_ref, message_ref):
    rows, width = partial_ref.shape[0], message_ref.shape[1]
    arrived = read_message(arrived_ref, rows)
    columns = aligned(pick(place_ref[0]), width)

    def total(group):
        return partial_ref[group * GROUP : (group + 1) * GROUP, columns] + arrived(group)

    write_message(message_ref, rows, total)


def hop(pick, place, partial, arrived):
    return pl.pallas_call(
        functools.partial(hop_kernel, pick),
        in_specs=[SMEM, VMEM, VMEM],
        out_specs=VMEM,
        out_shape=jax.ShapeDtypeStruct(arrived.shape, jnp.int16),
        compiler_params=params(8),
        cost_estimate=LITTLE,
        name="hop",
    )(place, partial, arrived)


def last_hop_kernel(place_ref, partial_ref, right_ref, left_ref, values_ref):
    rows, width = values_ref.shape
    right = read_message(right_ref, rows)
    left = read_message(left_ref, rows)
    columns = aligned(place_ref[0], width)
    for group in range(rows // GROUP):
        span = slice(group * GROUP, (group + 1) * GROUP)
        total = partial_ref[span, columns] + right(group) + left(group)
        values_ref[span, :] = total.astype(values_ref.dtype)


def last_hop(place, partial, right, left):
    rows, width = right.shape[0] - PAD, right.shape[1]
    return pl.pallas_call(
        last_hop_kernel,
        in_specs=[SMEM, VMEM, VMEM, VMEM],
        out_specs=VMEM,
        out_shape=jax.ShapeDtypeStruct((rows, width), jnp.bfloat16),
        compiler_params=params(8),
        cost_estimate=LITTLE,
        name="last_hop",
    )(place, partial, right, left)


def chunk_order(place):
    return (
        place,
        place ^ 1,
        jnp.where(place < 2, 2, 1),
        jnp.where(place < 2, 3, 0),
    )


def widen_kernel(chunk_ref, *wide_refs):
    tokens = chunk_ref.shape[0]
    for wide_ref in wide_refs:
        spare = wide_ref.shape[0] - tokens
        wide_ref[:tokens, :] = chunk_ref[...]
        wide_ref[tokens:, :] = jnp.zeros((spare, chunk_ref.shape[1]), chunk_ref.dtype)


def widen(chunk, *spares):
    tokens, width = chunk.shape
    return pl.pallas_call(
        widen_kernel,
        in_specs=[VMEM],
        out_specs=[VMEM] * len(spares),
        out_shape=[jax.ShapeDtypeStruct((tokens + spare, width), chunk.dtype) for spare in spares],
        compiler_params=params(5),
        cost_estimate=LITTLE,
        name="widen",
    )(chunk)


def product(turned, normed_ref, out_ref):
    step = 1024
    for n in range(normed_ref.shape[1] // step):
        span = slice(n * step, (n + 1) * step)
        out_ref[:, span] = jnp.dot(turned, normed_ref[:, span], preferred_element_type=jnp.float32)


def joined(tokens, refs):
    return functools.reduce(jnp.add, [ref[:tokens, :] for ref in refs])


def chunk_kernel(normed_ref, *refs):
    product(joined(normed_ref.shape[0], refs[:-1]).T, normed_ref, refs[-1])


def own_kernel(normed_ref, chunk_ref, held_ref, out_ref, sem):
    copy = pltpu.make_async_copy(normed_ref, held_ref, sem)
    copy.start()
    turned = chunk_ref[...].T
    copy.wait()
    product(turned, held_ref, out_ref)


def own_gradient(normed, chunk):
    return pl.pallas_call(
        own_kernel,
        in_specs=[pl.BlockSpec(memory_space=pl.ANY), VMEM],
        out_specs=[VMEM, VMEM],
        out_shape=[
            jax.ShapeDtypeStruct(normed.shape, normed.dtype),
            jax.ShapeDtypeStruct((chunk.shape[1], normed.shape[1]), jnp.float32),
        ],
        scratch_shapes=[pltpu.SemaphoreType.DMA],
        compiler_params=params(10),
        cost_estimate=LITTLE,
        name="own_gradient",
    )(normed, chunk)


def chunk_gradient(normed, *chunks):
    return pl.pallas_call(
        chunk_kernel,
        in_specs=[VMEM] + [VMEM] * len(chunks),
        out_specs=VMEM,
        out_shape=jax.ShapeDtypeStruct((chunks[0].shape[1], normed.shape[1]), jnp.float32),
        compiler_params=params(10),
        cost_estimate=LITTLE,
        name="chunk_gradient",
    )(normed, *chunks)


def slots_kernel(
    chips, column_blocks, codes_ref, place_ref, normed_ref, m2, d3, g1, g2, g3, *refs
):
    keep_refs = refs[:chips]
    send_refs = refs[chips : 2 * chips]
    gradient, sems = refs[2 * chips :]
    place = place_ref[0]
    copies = [
        pltpu.make_async_copy(g, gradient.at[i], sems.at[i]) for i, g in enumerate((g1, g2, g3))
    ]
    for copy in copies:
        copy.start()
    product(joined(normed_ref.shape[0], (m2, d3)).T, normed_ref, gradient.at[3])
    for copy in copies:
        copy.wait()
    order = chunk_order(place)
    tile = GROUP
    capacity = keep_refs[0].shape[0] // tile
    chunk_blocks = gradient.shape[1] // tile

    def term(k, slot):
        code = codes_ref[k, slot]
        safe = jnp.maximum(code, 0)
        row, column = safe // column_blocks, safe % column_blocks
        chunk = column // chunk_blocks
        stage = jnp.where(
            chunk == order[0],
            0,
            jnp.where(chunk == order[1], 1, jnp.where(chunk == order[2], 2, 3)),
        )
        block = gradient[stage, aligned(column % chunk_blocks, tile), aligned(row, tile)]
        return jnp.where(code >= 0, block, 0.0)

    for chip in reversed(range(chips)):
        write_message(send_refs[chip], capacity * tile, lambda slot: term(2 * chip + 1, slot))
        for slot in range(capacity):
            keep_refs[chip][slot * tile : (slot + 1) * tile, :] = term(2 * chip, slot)


def slot_terms(codes, place, normed, late, early, capacity, column_blocks):
    features = normed.shape[1]
    chips = codes.shape[0] // 2
    rows = capacity * GROUP
    width = early[0].shape[0]
    shapes = [((rows, GROUP), jnp.float32)] * chips + [((rows + 3 * PAD, GROUP), jnp.int16)] * chips
    outputs = pl.pallas_call(
        functools.partial(slots_kernel, chips, column_blocks),
        in_specs=[SMEM, SMEM, VMEM]
        + [VMEM] * len(late)
        + [pl.BlockSpec(memory_space=pl.ANY)] * len(early),
        out_specs=[VMEM] * len(shapes),
        scratch_shapes=[
            pltpu.VMEM((len(early) + 1, width, features), jnp.float32),
            pltpu.SemaphoreType.DMA((len(early),)),
        ],
        out_shape=[jax.ShapeDtypeStruct(shape, kind) for shape, kind in shapes],
        compiler_params=params(22),
        cost_estimate=LITTLE,
        name="slot_terms",
    )(codes, place, normed, *late, *early)
    return outputs[:chips], outputs[chips:]


def combine_kernel(kept_ref, arrived_ref, out_ref):
    rows = kept_ref.shape[0]
    arrived = read_message(arrived_ref, rows)

    def total(group):
        return kept_ref[group * GROUP : (group + 1) * GROUP, :] + arrived(group)

    if out_ref.dtype == jnp.int16:
        write_message(out_ref, rows, total)
    else:
        for group in range(rows // GROUP):
            out_ref[group * GROUP : (group + 1) * GROUP, :] = total(group)


def combine(kept, arrived, kind):
    shape = arrived.shape if kind == jnp.int16 else kept.shape
    return pl.pallas_call(
        combine_kernel,
        in_specs=[VMEM, VMEM],
        out_specs=VMEM,
        out_shape=jax.ShapeDtypeStruct(shape, kind),
        compiler_params=params(5),
        cost_estimate=LITTLE,
        name="combine",
    )(kept, arrived)


def update_kernel(count, *refs):
    kept_ref, out_ref = refs[0], refs[-1]
    tile = out_ref.shape[-1]
    arrived = [read_message(ref, kept_ref.shape[0]) for ref in refs[1 : 1 + count]]
    for slot in range(out_ref.shape[0]):
        total = kept_ref[slot * tile : (slot + 1) * tile, :]
        for block in arrived:
            total = total + block(slot)
        mean = jnp.sum(total * total) / (tile * tile)
        out_ref[slot] = (total * lax.rsqrt(mean + 1e-06)).T.astype(out_ref.dtype)


def normalized_update(kept, arrived, shape):
    return pl.pallas_call(
        functools.partial(update_kernel, len(arrived)),
        in_specs=[VMEM] * (1 + len(arrived)),
        out_specs=VMEM,
        out_shape=jax.ShapeDtypeStruct(shape, jnp.bfloat16),
        compiler_params=params(6),
        cost_estimate=LITTLE,
        name="normalized_update",
    )(kept, *arrived)


def grad_input_kernel(place_ref, weight_ref, own, a1, b1, e2, m2, d3, out_ref, cotangent):
    @pl.when(pl.program_id(0) == 0)
    def _():
        tokens, width = own.shape
        for chunk, refs in zip(chunk_order(place_ref[0]), ((own,), (a1,), (b1, e2), (m2, d3))):
            cotangent[:, aligned(chunk, width)] = joined(tokens, refs)

    out_ref[...] = lax.dot_general(
        cotangent[...],
        weight_ref[...],
        (((1,), (1,)), ((), ())),
        preferred_element_type=jnp.float32,
    ).astype(out_ref.dtype)


def grad_inputs(place, features, weight, *chunks):
    width = weight.shape[1]
    tokens = chunks[0].shape[0]
    block = 512
    return pl.pallas_call(
        grad_input_kernel,
        grid_spec=pltpu.PrefetchScalarGridSpec(
            num_scalar_prefetch=1,
            grid=(features // block,),
            in_specs=[pl.BlockSpec((block, width), lambda i, p: (i, 0))]
            + [VMEM] * len(chunks),
            out_specs=pl.BlockSpec((tokens, block), lambda i, p: (0, i)),
            scratch_shapes=[pltpu.VMEM((tokens, width), jnp.bfloat16)],
        ),
        out_shape=jax.ShapeDtypeStruct((tokens, features), jnp.bfloat16),
        compiler_params=params(14),
        cost_estimate=pl.CostEstimate(
            flops=2 * tokens * features * width,
            bytes_accessed=12 * MIB,
            transcendentals=0,
        ),
        name="grad_inputs",
    )(place, weight, *chunks)


def local(devices, parts, normed, tile_values, tile_rows, tile_columns, cotangent):
    capacity, tile = tile_values.shape[1], tile_values.shape[-1]
    column_blocks = cotangent.shape[1] * parts // tile
    chips = devices // 2
    rows = capacity * tile
    place = lax.axis_index("tensor").astype(jnp.int32).reshape(1)

    def swap(x, mask):
        return lax.ppermute(x, "fsdp", [(i, i ^ mask) for i in range(devices)])

    def pairs(x):
        return lax.ppermute(x, "tensor", [(0, 1), (1, 0), (2, 3), (3, 2)])

    def middle(x):
        return lax.ppermute(x, "tensor", [(1, 2), (2, 1)])

    def outward(x):
        return lax.ppermute(x, "tensor", [(1, 0), (2, 3)])

    def inward(x):
        return lax.ppermute(x, "tensor", [(0, 1), (3, 2)])

    positions = jnp.where(tile_columns >= 0, tile_rows * column_blocks + tile_columns + 1, 0)
    positions = jnp.pad(positions.astype(jnp.bfloat16), ((0, PAD - 1), (0, tile - capacity)))
    message = jnp.concatenate([tile_values.reshape(rows, tile), positions], axis=0)
    wider, wide = widen(cotangent, 2 * PAD, PAD)
    a1, b1 = pairs(wider), middle(wide)
    normed, g1 = own_gradient(normed, cotangent)
    same_core = [message] + [swap(message, 2 * chip) for chip in range(1, chips)]
    beside = swap(message, 1)
    a1, b1, g1, beside = lax.optimization_barrier((a1, b1, g1, beside))
    m2, e2 = middle(a1), outward(b1)
    g2 = chunk_gradient(normed, a1)
    *same_core, g2 = lax.optimization_barrier((*same_core, g2))
    gathered = [same_core[0], beside]
    for m in same_core[1:]:
        gathered += [m, swap(m, 1)]
    m2, e2, *gathered = lax.optimization_barrier((m2, e2, *gathered))
    d3 = outward(m2)

    weight, codes = assembled(gathered, normed.shape[1], column_blocks)
    first = first_values(place, normed, weight, parts)
    arrived = inward(first)
    weight, codes, _ = lax.optimization_barrier((weight, codes, first))
    partial, second = partial_values(place, normed, weight, first.shape)
    g3 = chunk_gradient(normed, b1, e2)
    g3, partial, second = lax.optimization_barrier((g3, partial, second))
    keep, send = slot_terms(codes, place, normed, (m2, d3), (g1, g2, g3), capacity, column_blocks)
    arrived, keep, send = lax.optimization_barrier((arrived, keep, send))

    to_middle = inward(second)
    crossing = middle(hop(lambda p: p ^ 2, place, partial, arrived))
    other = [swap(m, 1) for m in send]
    sums = [combine(keep[chip], other[chip], jnp.int16) for chip in range(1, chips)]
    own = combine(keep[0], other[0], jnp.float32)
    crossing, to_middle, own, _ = lax.optimization_barrier((crossing, to_middle, own, sums))
    terms = [swap(m, 2 * chip) for chip, m in reversed(list(enumerate(sums, 1)))]

    by_pair = pairs(hop(lambda p: p ^ 1, place, partial, crossing))
    by_middle = middle(hop(lambda p: 3 - p, place, partial, to_middle))
    grad_input = grad_inputs(place, normed.shape[1], weight, cotangent, a1, b1, e2, m2, d3)
    update = normalized_update(own, terms, tile_values.shape[1:])
    by_pair, by_middle, update = lax.optimization_barrier((by_pair, by_middle, update))
    values = last_hop(place, partial, by_pair, by_middle)
    return values, grad_input, update[None]


def solution(mesh):
    in_specs = (
        P("fsdp", "tensor"),
        P("tensor", "fsdp", None, None),
        P("tensor", "fsdp"),
        P("tensor", "fsdp"),
        P("fsdp", "tensor"),
    )
    out_specs = (P("fsdp", "tensor"), P("fsdp", "tensor"), P("tensor", "fsdp", None, None))
    return jax.shard_map(
        functools.partial(local, mesh.shape["fsdp"], mesh.shape["tensor"]),
        mesh=mesh,
        in_specs=in_specs,
        out_specs=out_specs,
        check_vma=False,
    )
```

```python
import functools

import jax
import jax.numpy as jnp
from jax import lax
from jax.experimental import pallas as pl
from jax.experimental.pallas import tpu as pltpu
from jax.sharding import PartitionSpec as P

MIB = 1024 * 1024
GROUP = 128
PAD = 16


def encode(block):
    peak = jnp.max(jnp.abs(block), axis=0, keepdims=True)
    exponent = jnp.floor(jnp.log2(jnp.maximum(peak, 2.0**-100))) + 1.0
    exponent = jnp.clip(exponent, -100.0, 128.0)
    scaled = jnp.round(block * jnp.exp2(15.0 - exponent))
    codes = jnp.clip(scaled, -32767.0, 32767.0).astype(jnp.int32).astype(jnp.int16)
    return codes, exponent


def decode(codes, exponent):
    return codes.astype(jnp.int32).astype(jnp.float32) * jnp.exp2(exponent - 15.0)


def as_code(exponents):
    return exponents.astype(jnp.int32).astype(jnp.int16)


def exponent_rows(codes):
    return codes.astype(jnp.int32).astype(jnp.float32)


def params(mib):
    return pltpu.CompilerParams(vmem_limit_bytes=mib * MIB)


VMEM = pl.BlockSpec(memory_space=pltpu.VMEM)
SMEM = pl.BlockSpec(memory_space=pltpu.SMEM)
LITTLE = pl.CostEstimate(flops=1, bytes_accessed=1, transcendentals=0)


def aligned(index, size):
    return pl.ds(pl.multiple_of(index * size, size), size)


def write_message(message_ref, rows, blocks):
    place = lax.broadcasted_iota(jnp.int32, (PAD, message_ref.shape[1]), 0)
    exponents = jnp.zeros((PAD, message_ref.shape[1]), jnp.float32)
    for group in range(rows // GROUP):
        codes, exponent = encode(blocks(group))
        message_ref[group * GROUP : (group + 1) * GROUP, :] = codes
        exponents = jnp.where(place == group, exponent, exponents)
    message_ref[rows : rows + PAD, :] = as_code(exponents)


def read_message(message_ref, rows):
    exponents = exponent_rows(message_ref[rows : rows + PAD, :])

    def block(group):
        return decode(
            message_ref[group * GROUP : (group + 1) * GROUP, :], exponents[group : group + 1, :]
        )

    return block


def first_kernel(column_blocks, place_ref, normed_ref, *refs):
    message_refs = refs[:-6]
    weight_ref, first_ref, codes_ref, partial, scalars, sem = refs[-6:]
    tokens = normed_ref.shape[0]
    chunk_width = first_ref.shape[1]
    chunks = weight_ref.shape[1] // chunk_width
    tile = message_refs[0].shape[1]
    capacity = message_refs[0].shape[0] // tile
    for k, message_ref in enumerate(message_refs):
        positions = message_ref[capacity * tile : capacity * tile + PAD, :]
        codes_ref[k : k + 1, :] = positions.astype(jnp.float32)[:1, :].astype(jnp.int32) - 1
    copy = pltpu.make_async_copy(codes_ref, scalars, sem)
    copy.start()
    weight_ref[...] = jnp.zeros_like(weight_ref)
    copy.wait()
    features = normed_ref.shape[1]
    for k, message_ref in enumerate(message_refs):
        for slot in range(capacity):
            code = scalars[k, slot]
            filled = code >= 0
            row = jnp.where(filled, code // column_blocks, features // tile)
            column = jnp.where(filled, code % column_blocks, 0)
            weight_ref[aligned(row, tile), aligned(column, tile)] = message_ref[
                slot * tile : (slot + 1) * tile, :
            ]
    far = weight_ref[:features, aligned(chunks - 1 - place_ref[0], chunk_width)]
    partial[...] = jnp.dot(normed_ref[...], far, preferred_element_type=jnp.float32)
    write_message(
        first_ref, tokens, lambda group: partial[group * GROUP : (group + 1) * GROUP, :]
    )


def first_values(place, normed, messages, chunks, column_blocks):
    tokens, features = normed.shape
    tile = messages[0].shape[1]
    width = column_blocks * tile
    return pl.pallas_call(
        functools.partial(first_kernel, column_blocks),
        in_specs=[SMEM, VMEM] + [VMEM] * len(messages),
        out_specs=[VMEM, VMEM, VMEM],
        out_shape=[
            jax.ShapeDtypeStruct((features + tile, width), jnp.bfloat16),
            jax.ShapeDtypeStruct((tokens + PAD, width // chunks), jnp.int16),
            jax.ShapeDtypeStruct((len(messages), tile), jnp.int32),
        ],
        scratch_shapes=[
            pltpu.VMEM((tokens, width // chunks), jnp.float32),
            pltpu.SMEM((len(messages), tile), jnp.int32),
            pltpu.SemaphoreType.DMA,
        ],
        compiler_params=params(22),
        cost_estimate=LITTLE,
        name="first_values",
    )(place, normed, *messages)


def partial_kernel(place_ref, normed_ref, weight_ref, partial_ref, second_ref):
    rows, chunk_width = normed_ref.shape[0], second_ref.shape[1]
    step = 2 * chunk_width
    for n in range(partial_ref.shape[1] // step):
        span = slice(n * step, (n + 1) * step)
        partial_ref[:, span] = jnp.dot(
            normed_ref[...],
            weight_ref[: normed_ref.shape[1], span],
            preferred_element_type=jnp.float32,
        )
    columns = aligned(place_ref[0] ^ 2, chunk_width)
    write_message(
        second_ref, rows, lambda group: partial_ref[group * GROUP : (group + 1) * GROUP, columns]
    )


def partial_values(place, normed, weight, message_shape):
    return pl.pallas_call(
        partial_kernel,
        in_specs=[SMEM, VMEM, VMEM],
        out_specs=[VMEM, VMEM],
        out_shape=[
            jax.ShapeDtypeStruct((normed.shape[0], weight.shape[1]), jnp.float32),
            jax.ShapeDtypeStruct(message_shape, jnp.int16),
        ],
        compiler_params=params(20),
        cost_estimate=LITTLE,
        name="partial_values",
    )(place, normed, weight)


def hop_kernel(pick, place_ref, partial_ref, arrived_ref, message_ref):
    rows, width = partial_ref.shape[0], message_ref.shape[1]
    arrived = read_message(arrived_ref, rows)
    columns = aligned(pick(place_ref[0]), width)

    def total(group):
        return partial_ref[group * GROUP : (group + 1) * GROUP, columns] + arrived(group)

    write_message(message_ref, rows, total)


def hop(pick, place, partial, arrived):
    return pl.pallas_call(
        functools.partial(hop_kernel, pick),
        in_specs=[SMEM, VMEM, VMEM],
        out_specs=VMEM,
        out_shape=jax.ShapeDtypeStruct(arrived.shape, jnp.int16),
        compiler_params=params(12),
        cost_estimate=LITTLE,
        name="hop",
    )(place, partial, arrived)


def last_hop_kernel(place_ref, partial_ref, right_ref, left_ref, values_ref):
    rows, width = values_ref.shape
    right = read_message(right_ref, rows)
    left = read_message(left_ref, rows)
    columns = aligned(place_ref[0], width)
    for group in range(rows // GROUP):
        span = slice(group * GROUP, (group + 1) * GROUP)
        total = partial_ref[span, columns] + right(group) + left(group)
        values_ref[span, :] = total.astype(values_ref.dtype)


def last_hop(place, partial, right, left):
    rows, width = right.shape[0] - PAD, right.shape[1]
    return pl.pallas_call(
        last_hop_kernel,
        in_specs=[SMEM, VMEM, VMEM, VMEM],
        out_specs=VMEM,
        out_shape=jax.ShapeDtypeStruct((rows, width), jnp.bfloat16),
        compiler_params=params(12),
        cost_estimate=LITTLE,
        name="last_hop",
    )(place, partial, right, left)


def chunk_order(place):
    return (
        place,
        place ^ 1,
        jnp.where(place < 2, 2, 1),
        jnp.where(place < 2, 3, 0),
    )


def widen_kernel(chunk_ref, *wide_refs):
    tokens = chunk_ref.shape[0]
    for wide_ref in wide_refs:
        spare = wide_ref.shape[0] - tokens
        wide_ref[:tokens, :] = chunk_ref[...]
        wide_ref[tokens:, :] = jnp.zeros((spare, chunk_ref.shape[1]), chunk_ref.dtype)


def widen(chunk, *spares):
    tokens, width = chunk.shape
    return pl.pallas_call(
        widen_kernel,
        in_specs=[VMEM],
        out_specs=[VMEM] * len(spares),
        out_shape=[jax.ShapeDtypeStruct((tokens + spare, width), chunk.dtype) for spare in spares],
        compiler_params=params(5),
        cost_estimate=LITTLE,
        name="widen",
    )(chunk)


def product(turned, normed_ref, out_ref):
    step = 1024
    for n in range(normed_ref.shape[1] // step):
        span = slice(n * step, (n + 1) * step)
        out_ref[:, span] = jnp.dot(turned, normed_ref[:, span], preferred_element_type=jnp.float32)


def joined(tokens, refs):
    return functools.reduce(jnp.add, [ref[:tokens, :] for ref in refs])


def chunk_kernel(normed_ref, *refs):
    product(joined(normed_ref.shape[0], refs[:-1]).T, normed_ref, refs[-1])


def chunk_gradient(normed, *chunks):
    return pl.pallas_call(
        chunk_kernel,
        in_specs=[VMEM] + [VMEM] * len(chunks),
        out_specs=VMEM,
        out_shape=jax.ShapeDtypeStruct((chunks[0].shape[1], normed.shape[1]), jnp.float32),
        compiler_params=params(16),
        cost_estimate=LITTLE,
        name="chunk_gradient",
    )(normed, *chunks)


def slots_kernel(
    chips, column_blocks, codes_ref, place_ref, normed_ref, b1, e2, m2, d3, g1, g2, *refs
):
    keep_refs = refs[:chips]
    send_refs = refs[chips : 2 * chips]
    gradient, turned, sems = refs[2 * chips :]
    place = place_ref[0]
    copies = [
        pltpu.make_async_copy(g, gradient.at[i], sems.at[i]) for i, g in enumerate((g1, g2))
    ]
    for copy in copies:
        copy.start()
    tokens, width = normed_ref.shape[0], gradient.shape[1]
    turned[:width, :] = joined(tokens, (b1, e2)).T
    turned[width:, :] = joined(tokens, (m2, d3)).T
    step = 512
    for n in range(normed_ref.shape[1] // step):
        span = slice(n * step, (n + 1) * step)
        both = jnp.dot(turned[...], normed_ref[:, span], preferred_element_type=jnp.float32)
        gradient[2, :, span] = both[:width, :]
        gradient[3, :, span] = both[width:, :]
    for copy in copies:
        copy.wait()
    order = chunk_order(place)
    tile = GROUP
    capacity = keep_refs[0].shape[0] // tile
    chunk_blocks = gradient.shape[1] // tile

    def term(k, slot):
        code = codes_ref[k, slot]
        safe = jnp.maximum(code, 0)
        row, column = safe // column_blocks, safe % column_blocks
        chunk = column // chunk_blocks
        stage = jnp.where(
            chunk == order[0],
            0,
            jnp.where(chunk == order[1], 1, jnp.where(chunk == order[2], 2, 3)),
        )
        block = gradient[stage, aligned(column % chunk_blocks, tile), aligned(row, tile)]
        return jnp.where(code >= 0, block, 0.0)

    for chip in reversed(range(chips)):
        write_message(send_refs[chip], capacity * tile, lambda slot: term(2 * chip + 1, slot))
        for slot in range(capacity):
            keep_refs[chip][slot * tile : (slot + 1) * tile, :] = term(2 * chip, slot)


def slot_terms(codes, place, normed, late, early, capacity, column_blocks):
    features = normed.shape[1]
    chips = codes.shape[0] // 2
    rows = capacity * GROUP
    width = early[0].shape[0]
    shapes = [((rows, GROUP), jnp.float32)] * chips + [((rows + 3 * PAD, GROUP), jnp.int16)] * chips
    outputs = pl.pallas_call(
        functools.partial(slots_kernel, chips, column_blocks),
        in_specs=[SMEM, SMEM, VMEM]
        + [VMEM] * len(late)
        + [pl.BlockSpec(memory_space=pl.ANY)] * len(early),
        out_specs=[VMEM] * len(shapes),
        scratch_shapes=[
            pltpu.VMEM((len(early) + 2, width, features), jnp.float32),
            pltpu.VMEM((2 * width, normed.shape[0]), jnp.bfloat16),
            pltpu.SemaphoreType.DMA((len(early),)),
        ],
        out_shape=[jax.ShapeDtypeStruct(shape, kind) for shape, kind in shapes],
        compiler_params=params(30),
        cost_estimate=LITTLE,
        name="slot_terms",
    )(codes, place, normed, *late, *early)
    return outputs[:chips], outputs[chips:]


def combine_kernel(kept_ref, arrived_ref, out_ref):
    rows = kept_ref.shape[0]
    arrived = read_message(arrived_ref, rows)

    def total(group):
        return kept_ref[group * GROUP : (group + 1) * GROUP, :] + arrived(group)

    if out_ref.dtype == jnp.int16:
        write_message(out_ref, rows, total)
    else:
        for group in range(rows // GROUP):
            out_ref[group * GROUP : (group + 1) * GROUP, :] = total(group)


def combine(kept, arrived, kind):
    shape = arrived.shape if kind == jnp.int16 else kept.shape
    return pl.pallas_call(
        combine_kernel,
        in_specs=[VMEM, VMEM],
        out_specs=VMEM,
        out_shape=jax.ShapeDtypeStruct(shape, kind),
        compiler_params=params(8),
        cost_estimate=LITTLE,
        name="combine",
    )(kept, arrived)


def update_kernel(count, *refs):
    kept_ref, out_ref = refs[0], refs[-1]
    tile = out_ref.shape[-1]
    arrived = [read_message(ref, kept_ref.shape[0]) for ref in refs[1 : 1 + count]]
    for slot in range(out_ref.shape[0]):
        total = kept_ref[slot * tile : (slot + 1) * tile, :]
        for block in arrived:
            total = total + block(slot)
        mean = jnp.sum(total * total) / (tile * tile)
        out_ref[slot] = (total * lax.rsqrt(mean + 1e-06)).T.astype(out_ref.dtype)


def normalized_update(kept, arrived, shape):
    return pl.pallas_call(
        functools.partial(update_kernel, len(arrived)),
        in_specs=[VMEM] * (1 + len(arrived)),
        out_specs=VMEM,
        out_shape=jax.ShapeDtypeStruct(shape, jnp.bfloat16),
        compiler_params=params(12),
        cost_estimate=LITTLE,
        name="normalized_update",
    )(kept, *arrived)


def grad_input_kernel(place_ref, weight_ref, own, a1, b1, e2, m2, d3, out_ref, cotangent):
    @pl.when(pl.program_id(0) == 0)
    def _():
        tokens, width = own.shape
        for chunk, refs in zip(chunk_order(place_ref[0]), ((own,), (a1,), (b1, e2), (m2, d3))):
            cotangent[:, aligned(chunk, width)] = joined(tokens, refs)

    out_ref[...] = lax.dot_general(
        cotangent[...],
        weight_ref[...],
        (((1,), (1,)), ((), ())),
        preferred_element_type=jnp.float32,
    ).astype(out_ref.dtype)


def grad_inputs(place, features, weight, *chunks):
    width = weight.shape[1]
    tokens = chunks[0].shape[0]
    block = 512
    return pl.pallas_call(
        grad_input_kernel,
        grid_spec=pltpu.PrefetchScalarGridSpec(
            num_scalar_prefetch=1,
            grid=(features // block,),
            in_specs=[pl.BlockSpec((block, width), lambda i, p: (i, 0))]
            + [VMEM] * len(chunks),
            out_specs=pl.BlockSpec((tokens, block), lambda i, p: (0, i)),
            scratch_shapes=[pltpu.VMEM((tokens, width), jnp.bfloat16)],
        ),
        out_shape=jax.ShapeDtypeStruct((tokens, features), jnp.bfloat16),
        compiler_params=params(20),
        cost_estimate=pl.CostEstimate(
            flops=2 * tokens * features * width,
            bytes_accessed=12 * MIB,
            transcendentals=0,
        ),
        name="grad_inputs",
    )(place, weight, *chunks)


def local(devices, parts, normed, tile_values, tile_rows, tile_columns, cotangent):
    capacity, tile = tile_values.shape[1], tile_values.shape[-1]
    column_blocks = cotangent.shape[1] * parts // tile
    chips = devices // 2
    rows = capacity * tile
    place = lax.axis_index("tensor").astype(jnp.int32).reshape(1)

    def swap(x, mask):
        return lax.ppermute(x, "fsdp", [(i, i ^ mask) for i in range(devices)])

    def pairs(x):
        return lax.ppermute(x, "tensor", [(0, 1), (1, 0), (2, 3), (3, 2)])

    def middle(x):
        return lax.ppermute(x, "tensor", [(1, 2), (2, 1)])

    def outward(x):
        return lax.ppermute(x, "tensor", [(1, 0), (2, 3)])

    def inward(x):
        return lax.ppermute(x, "tensor", [(0, 1), (3, 2)])

    positions = jnp.where(tile_columns >= 0, tile_rows * column_blocks + tile_columns + 1, 0)
    positions = jnp.pad(positions.astype(jnp.bfloat16), ((0, PAD - 1), (0, tile - capacity)))
    message = jnp.concatenate([tile_values.reshape(rows, tile), positions], axis=0)
    wider, wide = widen(cotangent, 2 * PAD, PAD)
    a1, b1 = pairs(wider), middle(wide)
    g1 = chunk_gradient(normed, cotangent)
    same_core = [message] + [swap(message, 2 * chip) for chip in range(1, chips)]
    beside = swap(message, 1)
    a1, b1, g1, beside = lax.optimization_barrier((a1, b1, g1, beside))
    m2, e2 = middle(a1), outward(b1)
    g2 = chunk_gradient(normed, a1)
    *same_core, g2 = lax.optimization_barrier((*same_core, g2))
    gathered = [same_core[0], beside]
    for m in same_core[1:]:
        gathered += [m, swap(m, 1)]
    m2, e2, *gathered = lax.optimization_barrier((m2, e2, *gathered))
    d3 = outward(m2)

    weight, first, codes = first_values(place, normed, gathered, parts, column_blocks)
    arrived = inward(first)
    partial, second = partial_values(place, normed, weight, first.shape)
    codes, partial, second = lax.optimization_barrier((codes, partial, second))
    late = (b1, e2, m2, d3)
    keep, send = slot_terms(codes, place, normed, late, (g1, g2), capacity, column_blocks)
    arrived, keep, send = lax.optimization_barrier((arrived, keep, send))

    to_middle = inward(second)
    crossing = middle(hop(lambda p: p ^ 2, place, partial, arrived))
    other = [swap(m, 1) for m in send]
    sums = [combine(keep[chip], other[chip], jnp.int16) for chip in range(1, chips)]
    own = combine(keep[0], other[0], jnp.float32)
    crossing, to_middle, own, _ = lax.optimization_barrier((crossing, to_middle, own, sums))
    terms = [swap(m, 2 * chip) for chip, m in reversed(list(enumerate(sums, 1)))]

    by_pair = pairs(hop(lambda p: p ^ 1, place, partial, crossing))
    by_middle = middle(hop(lambda p: 3 - p, place, partial, to_middle))
    grad_input = grad_inputs(place, normed.shape[1], weight, cotangent, a1, b1, e2, m2, d3)
    update = normalized_update(own, terms, tile_values.shape[1:])
    by_pair, by_middle, update = lax.optimization_barrier((by_pair, by_middle, update))
    values = last_hop(place, partial, by_pair, by_middle)
    return values, grad_input, update[None]


def solution(mesh):
    in_specs = (
        P("fsdp", "tensor"),
        P("tensor", "fsdp", None, None),
        P("tensor", "fsdp"),
        P("tensor", "fsdp"),
        P("fsdp", "tensor"),
    )
    out_specs = (P("fsdp", "tensor"), P("fsdp", "tensor"), P("tensor", "fsdp", None, None))
    return jax.shard_map(
        functools.partial(local, mesh.shape["fsdp"], mesh.shape["tensor"]),
        mesh=mesh,
        in_specs=in_specs,
        out_specs=out_specs,
        check_vma=False,
    )
```

```python
import functools

import jax
import jax.numpy as jnp
from jax import lax
from jax.experimental import pallas as pl
from jax.experimental.pallas import tpu as pltpu
from jax.sharding import PartitionSpec as P

MIB = 1024 * 1024
GROUP = 128
PAD = 16


def encode(block):
    peak = jnp.max(jnp.abs(block), axis=0, keepdims=True)
    exponent = jnp.floor(jnp.log2(jnp.maximum(peak, 2.0**-100))) + 1.0
    exponent = jnp.clip(exponent, -100.0, 128.0)
    scaled = jnp.round(block * jnp.exp2(15.0 - exponent))
    codes = jnp.clip(scaled, -32767.0, 32767.0).astype(jnp.int32).astype(jnp.int16)
    return codes, exponent


def decode(codes, exponent):
    return codes.astype(jnp.int32).astype(jnp.float32) * jnp.exp2(exponent - 15.0)


def as_code(exponents):
    return exponents.astype(jnp.int32).astype(jnp.int16)


def exponent_rows(codes):
    return codes.astype(jnp.int32).astype(jnp.float32)


def params(mib):
    return pltpu.CompilerParams(vmem_limit_bytes=mib * MIB)


VMEM = pl.BlockSpec(memory_space=pltpu.VMEM)
SMEM = pl.BlockSpec(memory_space=pltpu.SMEM)
LITTLE = pl.CostEstimate(flops=1, bytes_accessed=1, transcendentals=0)


def aligned(index, size):
    return pl.ds(pl.multiple_of(index * size, size), size)


def write_message(message_ref, rows, blocks):
    place = lax.broadcasted_iota(jnp.int32, (PAD, message_ref.shape[1]), 0)
    exponents = jnp.zeros((PAD, message_ref.shape[1]), jnp.float32)
    for group in range(rows // GROUP):
        codes, exponent = encode(blocks(group))
        message_ref[group * GROUP : (group + 1) * GROUP, :] = codes
        exponents = jnp.where(place == group, exponent, exponents)
    message_ref[rows : rows + PAD, :] = as_code(exponents)


def read_message(message_ref, rows):
    exponents = exponent_rows(message_ref[rows : rows + PAD, :])

    def block(group):
        return decode(
            message_ref[group * GROUP : (group + 1) * GROUP, :], exponents[group : group + 1, :]
        )

    return block


def assembly_kernel(column_blocks, features, *refs):
    message_refs = refs[:-4]
    weight_ref, codes_ref, scalars, sem = refs[-4:]
    tile = message_refs[0].shape[1]
    capacity = message_refs[0].shape[0] // tile
    for k, message_ref in enumerate(message_refs):
        positions = message_ref[capacity * tile : capacity * tile + PAD, :]
        codes_ref[k : k + 1, :] = positions.astype(jnp.float32)[:1, :].astype(jnp.int32) - 1
    copy = pltpu.make_async_copy(codes_ref, scalars, sem)
    copy.start()
    weight_ref[...] = jnp.zeros_like(weight_ref)
    copy.wait()
    for k, message_ref in enumerate(message_refs):
        for slot in range(capacity):
            code = scalars[k, slot]
            filled = code >= 0
            row = jnp.where(filled, code // column_blocks, features // tile)
            column = jnp.where(filled, code % column_blocks, 0)
            weight_ref[aligned(row, tile), aligned(column, tile)] = message_ref[
                slot * tile : (slot + 1) * tile, :
            ]


def assembled(messages, features, column_blocks):
    tile = messages[0].shape[1]
    count = len(messages)
    return pl.pallas_call(
        functools.partial(assembly_kernel, column_blocks, features),
        in_specs=[VMEM] * count,
        out_specs=[VMEM, VMEM],
        out_shape=[
            jax.ShapeDtypeStruct((features + tile, column_blocks * tile), jnp.bfloat16),
            jax.ShapeDtypeStruct((count, tile), jnp.int32),
        ],
        scratch_shapes=[
            pltpu.SMEM((count, tile), jnp.int32),
            pltpu.SemaphoreType.DMA,
        ],
        compiler_params=params(12),
        cost_estimate=LITTLE,
        name="assembled",
    )(*messages)


def first_kernel(place_ref, normed_ref, weight_ref, first_ref, partial):
    tokens, features = normed_ref.shape
    chunk_width = first_ref.shape[1]
    chunks = weight_ref.shape[1] // chunk_width
    far = weight_ref[:features, aligned(chunks - 1 - place_ref[0], chunk_width)]
    partial[...] = jnp.dot(normed_ref[...], far, preferred_element_type=jnp.float32)
    write_message(
        first_ref, tokens, lambda group: partial[group * GROUP : (group + 1) * GROUP, :]
    )


def first_values(place, normed, weight, chunks):
    tokens = normed.shape[0]
    width = weight.shape[1] // chunks
    return pl.pallas_call(
        first_kernel,
        in_specs=[SMEM, VMEM, VMEM],
        out_specs=VMEM,
        out_shape=jax.ShapeDtypeStruct((tokens + PAD, width), jnp.int16),
        scratch_shapes=[pltpu.VMEM((tokens, width), jnp.float32)],
        compiler_params=params(14),
        cost_estimate=LITTLE,
        name="first_values",
    )(place, normed, weight)


def partial_kernel(place_ref, normed_ref, weight_ref, partial_ref, second_ref):
    rows, chunk_width = normed_ref.shape[0], second_ref.shape[1]
    step = 2 * chunk_width
    for n in range(partial_ref.shape[1] // step):
        span = slice(n * step, (n + 1) * step)
        partial_ref[:, span] = jnp.dot(
            normed_ref[...],
            weight_ref[: normed_ref.shape[1], span],
            preferred_element_type=jnp.float32,
        )
    columns = aligned(place_ref[0] ^ 2, chunk_width)
    write_message(
        second_ref, rows, lambda group: partial_ref[group * GROUP : (group + 1) * GROUP, columns]
    )


def partial_values(place, normed, weight, message_shape):
    return pl.pallas_call(
        partial_kernel,
        in_specs=[SMEM, VMEM, VMEM],
        out_specs=[VMEM, VMEM],
        out_shape=[
            jax.ShapeDtypeStruct((normed.shape[0], weight.shape[1]), jnp.float32),
            jax.ShapeDtypeStruct(message_shape, jnp.int16),
        ],
        compiler_params=params(16),
        cost_estimate=LITTLE,
        name="partial_values",
    )(place, normed, weight)


def hop_kernel(pick, place_ref, partial_ref, arrived_ref, message_ref):
    rows, width = partial_ref.shape[0], message_ref.shape[1]
    arrived = read_message(arrived_ref, rows)
    columns = aligned(pick(place_ref[0]), width)

    def total(group):
        return partial_ref[group * GROUP : (group + 1) * GROUP, columns] + arrived(group)

    write_message(message_ref, rows, total)


def hop(pick, place, partial, arrived):
    return pl.pallas_call(
        functools.partial(hop_kernel, pick),
        in_specs=[SMEM, VMEM, VMEM],
        out_specs=VMEM,
        out_shape=jax.ShapeDtypeStruct(arrived.shape, jnp.int16),
        compiler_params=params(8),
        cost_estimate=LITTLE,
        name="hop",
    )(place, partial, arrived)


def last_hop_kernel(place_ref, partial_ref, right_ref, left_ref, values_ref):
    rows, width = values_ref.shape
    right = read_message(right_ref, rows)
    left = read_message(left_ref, rows)
    columns = aligned(place_ref[0], width)
    for group in range(rows // GROUP):
        span = slice(group * GROUP, (group + 1) * GROUP)
        total = partial_ref[span, columns] + right(group) + left(group)
        values_ref[span, :] = total.astype(values_ref.dtype)


def last_hop(place, partial, right, left):
    rows, width = right.shape[0] - PAD, right.shape[1]
    return pl.pallas_call(
        last_hop_kernel,
        in_specs=[SMEM, VMEM, VMEM, VMEM],
        out_specs=VMEM,
        out_shape=jax.ShapeDtypeStruct((rows, width), jnp.bfloat16),
        compiler_params=params(8),
        cost_estimate=LITTLE,
        name="last_hop",
    )(place, partial, right, left)


def chunk_order(place):
    return (
        place,
        place ^ 1,
        jnp.where(place < 2, 2, 1),
        jnp.where(place < 2, 3, 0),
    )


def widen_kernel(chunk_ref, *wide_refs):
    tokens = chunk_ref.shape[0]
    for wide_ref in wide_refs:
        spare = wide_ref.shape[0] - tokens
        wide_ref[:tokens, :] = chunk_ref[...]
        wide_ref[tokens:, :] = jnp.zeros((spare, chunk_ref.shape[1]), chunk_ref.dtype)


def widen(chunk, *spares):
    tokens, width = chunk.shape
    return pl.pallas_call(
        widen_kernel,
        in_specs=[VMEM],
        out_specs=[VMEM] * len(spares),
        out_shape=[jax.ShapeDtypeStruct((tokens + spare, width), chunk.dtype) for spare in spares],
        compiler_params=params(5),
        cost_estimate=LITTLE,
        name="widen",
    )(chunk)


def product(turned, normed_ref, out_ref):
    step = 1024
    for n in range(normed_ref.shape[1] // step):
        span = slice(n * step, (n + 1) * step)
        out_ref[:, span] = jnp.dot(turned, normed_ref[:, span], preferred_element_type=jnp.float32)


def joined(tokens, refs):
    return functools.reduce(jnp.add, [ref[:tokens, :] for ref in refs])


def chunk_kernel(normed_ref, *refs):
    product(joined(normed_ref.shape[0], refs[:-1]).T, normed_ref, refs[-1])


def own_kernel(normed_ref, chunk_ref, held_ref, out_ref, sem):
    copy = pltpu.make_async_copy(normed_ref, held_ref, sem)
    copy.start()
    turned = chunk_ref[...].T
    copy.wait()
    product(turned, held_ref, out_ref)


def own_gradient(normed, chunk):
    return pl.pallas_call(
        own_kernel,
        in_specs=[pl.BlockSpec(memory_space=pl.ANY), VMEM],
        out_specs=[VMEM, VMEM],
        out_shape=[
            jax.ShapeDtypeStruct(normed.shape, normed.dtype),
            jax.ShapeDtypeStruct((chunk.shape[1], normed.shape[1]), jnp.float32),
        ],
        scratch_shapes=[pltpu.SemaphoreType.DMA],
        compiler_params=params(10),
        cost_estimate=LITTLE,
        name="own_gradient",
    )(normed, chunk)


def chunk_gradient(normed, *chunks):
    return pl.pallas_call(
        chunk_kernel,
        in_specs=[VMEM] + [VMEM] * len(chunks),
        out_specs=VMEM,
        out_shape=jax.ShapeDtypeStruct((chunks[0].shape[1], normed.shape[1]), jnp.float32),
        compiler_params=params(10),
        cost_estimate=LITTLE,
        name="chunk_gradient",
    )(normed, *chunks)


def slots_kernel(
    chips, column_blocks, codes_ref, place_ref, normed_ref, m2, d3, g1, g2, g3, *refs
):
    keep_refs = refs[:chips]
    send_refs = refs[chips : 2 * chips]
    gradient, sems = refs[2 * chips :]
    place = place_ref[0]
    copies = [
        pltpu.make_async_copy(g, gradient.at[i], sems.at[i]) for i, g in enumerate((g1, g2, g3))
    ]
    for copy in copies:
        copy.start()
    product(joined(normed_ref.shape[0], (m2, d3)).T, normed_ref, gradient.at[3])
    for copy in copies:
        copy.wait()
    order = chunk_order(place)
    tile = GROUP
    capacity = keep_refs[0].shape[0] // tile
    chunk_blocks = gradient.shape[1] // tile

    def term(k, slot):
        code = codes_ref[k, slot]
        safe = jnp.maximum(code, 0)
        row, column = safe // column_blocks, safe % column_blocks
        chunk = column // chunk_blocks
        stage = jnp.where(
            chunk == order[0],
            0,
            jnp.where(chunk == order[1], 1, jnp.where(chunk == order[2], 2, 3)),
        )
        block = gradient[stage, aligned(column % chunk_blocks, tile), aligned(row, tile)]
        return jnp.where(code >= 0, block, 0.0)

    for chip in reversed(range(chips)):
        write_message(send_refs[chip], capacity * tile, lambda slot: term(2 * chip + 1, slot))
        for slot in range(capacity):
            keep_refs[chip][slot * tile : (slot + 1) * tile, :] = term(2 * chip, slot)


def slot_terms(codes, place, normed, late, early, capacity, column_blocks):
    features = normed.shape[1]
    chips = codes.shape[0] // 2
    rows = capacity * GROUP
    width = early[0].shape[0]
    shapes = [((rows, GROUP), jnp.float32)] * chips + [((rows + 3 * PAD, GROUP), jnp.int16)] * chips
    outputs = pl.pallas_call(
        functools.partial(slots_kernel, chips, column_blocks),
        in_specs=[SMEM, SMEM, VMEM]
        + [VMEM] * len(late)
        + [pl.BlockSpec(memory_space=pl.ANY)] * len(early),
        out_specs=[VMEM] * len(shapes),
        scratch_shapes=[
            pltpu.VMEM((len(early) + 1, width, features), jnp.float32),
            pltpu.SemaphoreType.DMA((len(early),)),
        ],
        out_shape=[jax.ShapeDtypeStruct(shape, kind) for shape, kind in shapes],
        compiler_params=params(22),
        cost_estimate=LITTLE,
        name="slot_terms",
    )(codes, place, normed, *late, *early)
    return outputs[:chips], outputs[chips:]


def combine_kernel(kept_ref, arrived_ref, out_ref):
    rows = kept_ref.shape[0]
    arrived = read_message(arrived_ref, rows)

    def total(group):
        return kept_ref[group * GROUP : (group + 1) * GROUP, :] + arrived(group)

    if out_ref.dtype == jnp.int16:
        write_message(out_ref, rows, total)
    else:
        for group in range(rows // GROUP):
            out_ref[group * GROUP : (group + 1) * GROUP, :] = total(group)


def combine(kept, arrived, kind):
    shape = arrived.shape if kind == jnp.int16 else kept.shape
    return pl.pallas_call(
        combine_kernel,
        in_specs=[VMEM, VMEM],
        out_specs=VMEM,
        out_shape=jax.ShapeDtypeStruct(shape, kind),
        compiler_params=params(5),
        cost_estimate=LITTLE,
        name="combine",
    )(kept, arrived)


def update_kernel(count, *refs):
    kept_ref, out_ref = refs[0], refs[-1]
    tile = out_ref.shape[-1]
    arrived = [read_message(ref, kept_ref.shape[0]) for ref in refs[1 : 1 + count]]
    for slot in range(out_ref.shape[0]):
        total = kept_ref[slot * tile : (slot + 1) * tile, :]
        for block in arrived:
            total = total + block(slot)
        mean = jnp.sum(total * total) / (tile * tile)
        out_ref[slot] = (total * lax.rsqrt(mean + 1e-06)).T.astype(out_ref.dtype)


def normalized_update(kept, arrived, shape):
    return pl.pallas_call(
        functools.partial(update_kernel, len(arrived)),
        in_specs=[VMEM] * (1 + len(arrived)),
        out_specs=VMEM,
        out_shape=jax.ShapeDtypeStruct(shape, jnp.bfloat16),
        compiler_params=params(6),
        cost_estimate=LITTLE,
        name="normalized_update",
    )(kept, *arrived)


def grad_input_kernel(place_ref, weight_ref, own, a1, b1, e2, m2, d3, out_ref, cotangent):
    @pl.when(pl.program_id(0) == 0)
    def _():
        tokens, width = own.shape
        for chunk, refs in zip(chunk_order(place_ref[0]), ((own,), (a1,), (b1, e2), (m2, d3))):
            cotangent[:, aligned(chunk, width)] = joined(tokens, refs)

    out_ref[...] = lax.dot_general(
        cotangent[...],
        weight_ref[...],
        (((1,), (1,)), ((), ())),
        preferred_element_type=jnp.float32,
    ).astype(out_ref.dtype)


def grad_inputs(place, features, weight, *chunks):
    width = weight.shape[1]
    tokens = chunks[0].shape[0]
    block = 512
    return pl.pallas_call(
        grad_input_kernel,
        grid_spec=pltpu.PrefetchScalarGridSpec(
            num_scalar_prefetch=1,
            grid=(features // block,),
            in_specs=[pl.BlockSpec((block, width), lambda i, p: (i, 0))]
            + [VMEM] * len(chunks),
            out_specs=pl.BlockSpec((tokens, block), lambda i, p: (0, i)),
            scratch_shapes=[pltpu.VMEM((tokens, width), jnp.bfloat16)],
        ),
        out_shape=jax.ShapeDtypeStruct((tokens, features), jnp.bfloat16),
        compiler_params=params(14),
        cost_estimate=pl.CostEstimate(
            flops=2 * tokens * features * width,
            bytes_accessed=12 * MIB,
            transcendentals=0,
        ),
        name="grad_inputs",
    )(place, weight, *chunks)


def local(devices, parts, normed, tile_values, tile_rows, tile_columns, cotangent):
    capacity, tile = tile_values.shape[1], tile_values.shape[-1]
    column_blocks = cotangent.shape[1] * parts // tile
    chips = devices // 2
    rows = capacity * tile
    place = lax.axis_index("tensor").astype(jnp.int32).reshape(1)

    def swap(x, mask):
        return lax.ppermute(x, "fsdp", [(i, i ^ mask) for i in range(devices)])

    def pairs(x):
        return lax.ppermute(x, "tensor", [(0, 1), (1, 0), (2, 3), (3, 2)])

    def middle(x):
        return lax.ppermute(x, "tensor", [(1, 2), (2, 1)])

    def outward(x):
        return lax.ppermute(x, "tensor", [(1, 0), (2, 3)])

    def inward(x):
        return lax.ppermute(x, "tensor", [(0, 1), (3, 2)])

    positions = jnp.where(tile_columns >= 0, tile_rows * column_blocks + tile_columns + 1, 0)
    positions = jnp.pad(positions.astype(jnp.bfloat16), ((0, PAD - 1), (0, tile - capacity)))
    message = jnp.concatenate([tile_values.reshape(rows, tile), positions], axis=0)
    wider, wide = widen(cotangent, 2 * PAD, PAD)
    a1, b1 = pairs(wider), middle(wide)
    normed, g1 = own_gradient(normed, cotangent)
    same_core = [message] + [swap(message, 2 * chip) for chip in range(1, chips)]
    beside = swap(message, 1)
    a1, b1, g1, beside = lax.optimization_barrier((a1, b1, g1, beside))
    m2, e2 = middle(a1), outward(b1)
    g2 = chunk_gradient(normed, a1)
    *same_core, g2 = lax.optimization_barrier((*same_core, g2))
    gathered = [same_core[0], beside]
    for m in same_core[1:]:
        gathered += [m, swap(m, 1)]

    weight, codes = assembled(gathered, normed.shape[1], column_blocks)
    m2, e2, weight, codes = lax.optimization_barrier((m2, e2, weight, codes))
    d3 = outward(m2)
    first = first_values(place, normed, weight, parts)
    arrived = inward(first)
    weight, codes, _ = lax.optimization_barrier((weight, codes, first))
    partial, second = partial_values(place, normed, weight, first.shape)
    g3 = chunk_gradient(normed, b1, e2)
    g3, partial, second = lax.optimization_barrier((g3, partial, second))
    keep, send = slot_terms(codes, place, normed, (m2, d3), (g1, g2, g3), capacity, column_blocks)
    arrived, keep, send = lax.optimization_barrier((arrived, keep, send))

    to_middle = inward(second)
    crossing = middle(hop(lambda p: p ^ 2, place, partial, arrived))
    other = [swap(m, 1) for m in send]
    sums = [combine(keep[chip], other[chip], jnp.int16) for chip in range(1, chips)]
    own = combine(keep[0], other[0], jnp.float32)
    crossing, to_middle, own, _ = lax.optimization_barrier((crossing, to_middle, own, sums))
    terms = [swap(m, 2 * chip) for chip, m in reversed(list(enumerate(sums, 1)))]

    by_pair = pairs(hop(lambda p: p ^ 1, place, partial, crossing))
    by_middle = middle(hop(lambda p: 3 - p, place, partial, to_middle))
    grad_input = grad_inputs(place, normed.shape[1], weight, cotangent, a1, b1, e2, m2, d3)
    update = normalized_update(own, terms, tile_values.shape[1:])
    by_pair, by_middle, update = lax.optimization_barrier((by_pair, by_middle, update))
    values = last_hop(place, partial, by_pair, by_middle)
    return values, grad_input, update[None]


def solution(mesh):
    in_specs = (
        P("fsdp", "tensor"),
        P("tensor", "fsdp", None, None),
        P("tensor", "fsdp"),
        P("tensor", "fsdp"),
        P("fsdp", "tensor"),
    )
    out_specs = (P("fsdp", "tensor"), P("fsdp", "tensor"), P("tensor", "fsdp", None, None))
    return jax.shard_map(
        functools.partial(local, mesh.shape["fsdp"], mesh.shape["tensor"]),
        mesh=mesh,
        in_specs=in_specs,
        out_specs=out_specs,
        check_vma=False,
    )
```

```python
import functools

import jax
import jax.numpy as jnp
from jax import lax
from jax.experimental import pallas as pl
from jax.experimental.pallas import tpu as pltpu
from jax.sharding import PartitionSpec as P

MIB = 1024 * 1024
GROUP = 128
PAD = 16


def encode(block):
    peak = jnp.max(jnp.abs(block), axis=0, keepdims=True)
    exponent = jnp.floor(jnp.log2(jnp.maximum(peak, 2.0**-100))) + 1.0
    exponent = jnp.clip(exponent, -100.0, 128.0)
    scaled = jnp.round(block * jnp.exp2(15.0 - exponent))
    codes = jnp.clip(scaled, -32767.0, 32767.0).astype(jnp.int32).astype(jnp.int16)
    return codes, exponent


def decode(codes, exponent):
    return codes.astype(jnp.int32).astype(jnp.float32) * jnp.exp2(exponent - 15.0)


def as_code(exponents):
    return exponents.astype(jnp.int32).astype(jnp.int16)


def exponent_rows(codes):
    return codes.astype(jnp.int32).astype(jnp.float32)


def params(mib):
    return pltpu.CompilerParams(vmem_limit_bytes=mib * MIB)


VMEM = pl.BlockSpec(memory_space=pltpu.VMEM)
SMEM = pl.BlockSpec(memory_space=pltpu.SMEM)
LITTLE = pl.CostEstimate(flops=1, bytes_accessed=1, transcendentals=0)


def aligned(index, size):
    return pl.ds(pl.multiple_of(index * size, size), size)


def write_message(message_ref, rows, blocks):
    place = lax.broadcasted_iota(jnp.int32, (PAD, message_ref.shape[1]), 0)
    exponents = jnp.zeros((PAD, message_ref.shape[1]), jnp.float32)
    for group in range(rows // GROUP):
        codes, exponent = encode(blocks(group))
        message_ref[group * GROUP : (group + 1) * GROUP, :] = codes
        exponents = jnp.where(place == group, exponent, exponents)
    message_ref[rows : rows + PAD, :] = as_code(exponents)


def read_message(message_ref, rows):
    exponents = exponent_rows(message_ref[rows : rows + PAD, :])

    def block(group):
        return decode(
            message_ref[group * GROUP : (group + 1) * GROUP, :], exponents[group : group + 1, :]
        )

    return block


def assembly_kernel(column_blocks, features, *refs):
    message_refs = refs[:-4]
    weight_ref, codes_ref, scalars, sem = refs[-4:]
    tile = message_refs[0].shape[1]
    capacity = message_refs[0].shape[0] // tile
    for k, message_ref in enumerate(message_refs):
        positions = message_ref[capacity * tile : capacity * tile + PAD, :]
        codes_ref[k : k + 1, :] = positions.astype(jnp.float32)[:1, :].astype(jnp.int32) - 1
    copy = pltpu.make_async_copy(codes_ref, scalars, sem)
    copy.start()
    weight_ref[...] = jnp.zeros_like(weight_ref)
    copy.wait()
    for k, message_ref in enumerate(message_refs):
        for slot in range(capacity):
            code = scalars[k, slot]
            filled = code >= 0
            row = jnp.where(filled, code // column_blocks, features // tile)
            column = jnp.where(filled, code % column_blocks, 0)
            weight_ref[aligned(row, tile), aligned(column, tile)] = message_ref[
                slot * tile : (slot + 1) * tile, :
            ]


def assembled(messages, features, column_blocks):
    tile = messages[0].shape[1]
    count = len(messages)
    return pl.pallas_call(
        functools.partial(assembly_kernel, column_blocks, features),
        in_specs=[VMEM] * count,
        out_specs=[VMEM, VMEM],
        out_shape=[
            jax.ShapeDtypeStruct((features + tile, column_blocks * tile), jnp.bfloat16),
            jax.ShapeDtypeStruct((count, tile), jnp.int32),
        ],
        scratch_shapes=[
            pltpu.SMEM((count, tile), jnp.int32),
            pltpu.SemaphoreType.DMA,
        ],
        compiler_params=params(12),
        cost_estimate=LITTLE,
        name="assembled",
    )(*messages)


def first_kernel(place_ref, normed_ref, weight_ref, first_ref, partial):
    tokens, features = normed_ref.shape
    chunk_width = first_ref.shape[1]
    chunks = weight_ref.shape[1] // chunk_width
    far = weight_ref[:features, aligned(chunks - 1 - place_ref[0], chunk_width)]
    partial[...] = jnp.dot(normed_ref[...], far, preferred_element_type=jnp.float32)
    write_message(
        first_ref, tokens, lambda group: partial[group * GROUP : (group + 1) * GROUP, :]
    )


def first_values(place, normed, weight, chunks):
    tokens = normed.shape[0]
    width = weight.shape[1] // chunks
    return pl.pallas_call(
        first_kernel,
        in_specs=[SMEM, VMEM, VMEM],
        out_specs=VMEM,
        out_shape=jax.ShapeDtypeStruct((tokens + PAD, width), jnp.int16),
        scratch_shapes=[pltpu.VMEM((tokens, width), jnp.float32)],
        compiler_params=params(14),
        cost_estimate=LITTLE,
        name="first_values",
    )(place, normed, weight)


def partial_kernel(place_ref, normed_ref, weight_ref, partial_ref, second_ref):
    rows, chunk_width = normed_ref.shape[0], second_ref.shape[1]
    step = 2 * chunk_width
    for n in range(partial_ref.shape[1] // step):
        span = slice(n * step, (n + 1) * step)
        partial_ref[:, span] = jnp.dot(
            normed_ref[...],
            weight_ref[: normed_ref.shape[1], span],
            preferred_element_type=jnp.float32,
        )
    columns = aligned(place_ref[0] ^ 2, chunk_width)
    write_message(
        second_ref, rows, lambda group: partial_ref[group * GROUP : (group + 1) * GROUP, columns]
    )


def partial_values(place, normed, weight, message_shape):
    return pl.pallas_call(
        partial_kernel,
        in_specs=[SMEM, VMEM, VMEM],
        out_specs=[VMEM, VMEM],
        out_shape=[
            jax.ShapeDtypeStruct((normed.shape[0], weight.shape[1]), jnp.float32),
            jax.ShapeDtypeStruct(message_shape, jnp.int16),
        ],
        compiler_params=params(16),
        cost_estimate=LITTLE,
        name="partial_values",
    )(place, normed, weight)


def hop_kernel(pick, place_ref, partial_ref, arrived_ref, message_ref):
    rows, width = partial_ref.shape[0], message_ref.shape[1]
    arrived = read_message(arrived_ref, rows)
    columns = aligned(pick(place_ref[0]), width)

    def total(group):
        return partial_ref[group * GROUP : (group + 1) * GROUP, columns] + arrived(group)

    write_message(message_ref, rows, total)


def hop(pick, place, partial, arrived):
    return pl.pallas_call(
        functools.partial(hop_kernel, pick),
        in_specs=[SMEM, VMEM, VMEM],
        out_specs=VMEM,
        out_shape=jax.ShapeDtypeStruct(arrived.shape, jnp.int16),
        compiler_params=params(8),
        cost_estimate=LITTLE,
        name="hop",
    )(place, partial, arrived)


def last_hop_kernel(place_ref, partial_ref, right_ref, left_ref, values_ref):
    rows, width = values_ref.shape
    right = read_message(right_ref, rows)
    left = read_message(left_ref, rows)
    columns = aligned(place_ref[0], width)
    for group in range(rows // GROUP):
        span = slice(group * GROUP, (group + 1) * GROUP)
        total = partial_ref[span, columns] + right(group) + left(group)
        values_ref[span, :] = total.astype(values_ref.dtype)


def last_hop(place, partial, right, left):
    rows, width = right.shape[0] - PAD, right.shape[1]
    return pl.pallas_call(
        last_hop_kernel,
        in_specs=[SMEM, VMEM, VMEM, VMEM],
        out_specs=VMEM,
        out_shape=jax.ShapeDtypeStruct((rows, width), jnp.bfloat16),
        compiler_params=params(8),
        cost_estimate=LITTLE,
        name="last_hop",
    )(place, partial, right, left)


def chunk_order(place):
    return (
        place,
        place ^ 1,
        jnp.where(place < 2, 2, 1),
        jnp.where(place < 2, 3, 0),
    )


def widen_kernel(chunk_ref, *wide_refs):
    tokens = chunk_ref.shape[0]
    for wide_ref in wide_refs:
        spare = wide_ref.shape[0] - tokens
        wide_ref[:tokens, :] = chunk_ref[...]
        wide_ref[tokens:, :] = jnp.zeros((spare, chunk_ref.shape[1]), chunk_ref.dtype)


def widen(chunk, *spares):
    tokens, width = chunk.shape
    return pl.pallas_call(
        widen_kernel,
        in_specs=[VMEM],
        out_specs=[VMEM] * len(spares),
        out_shape=[jax.ShapeDtypeStruct((tokens + spare, width), chunk.dtype) for spare in spares],
        compiler_params=params(5),
        cost_estimate=LITTLE,
        name="widen",
    )(chunk)


def product(turned, normed_ref, out_ref):
    step = 1024
    for n in range(normed_ref.shape[1] // step):
        span = slice(n * step, (n + 1) * step)
        out_ref[:, span] = jnp.dot(turned, normed_ref[:, span], preferred_element_type=jnp.float32)


def joined(tokens, refs):
    return functools.reduce(jnp.add, [ref[:tokens, :] for ref in refs])


def chunk_kernel(normed_ref, *refs):
    product(joined(normed_ref.shape[0], refs[:-1]).T, normed_ref, refs[-1])


def own_kernel(normed_ref, chunk_ref, held_ref, out_ref, sem):
    copy = pltpu.make_async_copy(normed_ref, held_ref, sem)
    copy.start()
    turned = chunk_ref[...].T
    copy.wait()
    product(turned, held_ref, out_ref)


def own_gradient(normed, chunk):
    return pl.pallas_call(
        own_kernel,
        in_specs=[pl.BlockSpec(memory_space=pl.ANY), VMEM],
        out_specs=[VMEM, VMEM],
        out_shape=[
            jax.ShapeDtypeStruct(normed.shape, normed.dtype),
            jax.ShapeDtypeStruct((chunk.shape[1], normed.shape[1]), jnp.float32),
        ],
        scratch_shapes=[pltpu.SemaphoreType.DMA],
        compiler_params=params(10),
        cost_estimate=LITTLE,
        name="own_gradient",
    )(normed, chunk)


def chunk_gradient(normed, *chunks):
    return pl.pallas_call(
        chunk_kernel,
        in_specs=[VMEM] + [VMEM] * len(chunks),
        out_specs=VMEM,
        out_shape=jax.ShapeDtypeStruct((chunks[0].shape[1], normed.shape[1]), jnp.float32),
        compiler_params=params(10),
        cost_estimate=LITTLE,
        name="chunk_gradient",
    )(normed, *chunks)


def slots_kernel(
    chips, column_blocks, codes_ref, place_ref, normed_ref, m2, d3, g1, g2, g3, *refs
):
    keep_refs = refs[:chips]
    send_refs = refs[chips : 2 * chips]
    gradient, sems = refs[2 * chips :]
    place = place_ref[0]
    copies = [
        pltpu.make_async_copy(g, gradient.at[i], sems.at[i]) for i, g in enumerate((g1, g2, g3))
    ]
    for copy in copies:
        copy.start()
    product(joined(normed_ref.shape[0], (m2, d3)).T, normed_ref, gradient.at[3])
    for copy in copies:
        copy.wait()
    order = chunk_order(place)
    tile = GROUP
    capacity = keep_refs[0].shape[0] // tile
    chunk_blocks = gradient.shape[1] // tile

    def term(k, slot):
        code = codes_ref[k, slot]
        safe = jnp.maximum(code, 0)
        row, column = safe // column_blocks, safe % column_blocks
        chunk = column // chunk_blocks
        stage = jnp.where(
            chunk == order[0],
            0,
            jnp.where(chunk == order[1], 1, jnp.where(chunk == order[2], 2, 3)),
        )
        block = gradient[stage, aligned(column % chunk_blocks, tile), aligned(row, tile)]
        return jnp.where(code >= 0, block, 0.0)

    for chip in reversed(range(chips)):
        write_message(send_refs[chip], capacity * tile, lambda slot: term(2 * chip + 1, slot))
        for slot in range(capacity):
            keep_refs[chip][slot * tile : (slot + 1) * tile, :] = term(2 * chip, slot)


def slot_terms(codes, place, normed, late, early, capacity, column_blocks):
    features = normed.shape[1]
    chips = codes.shape[0] // 2
    rows = capacity * GROUP
    width = early[0].shape[0]
    shapes = [((rows, GROUP), jnp.float32)] * chips + [((rows + 3 * PAD, GROUP), jnp.int16)] * chips
    outputs = pl.pallas_call(
        functools.partial(slots_kernel, chips, column_blocks),
        in_specs=[SMEM, SMEM, VMEM]
        + [VMEM] * len(late)
        + [pl.BlockSpec(memory_space=pl.ANY)] * len(early),
        out_specs=[VMEM] * len(shapes),
        scratch_shapes=[
            pltpu.VMEM((len(early) + 1, width, features), jnp.float32),
            pltpu.SemaphoreType.DMA((len(early),)),
        ],
        out_shape=[jax.ShapeDtypeStruct(shape, kind) for shape, kind in shapes],
        compiler_params=params(22),
        cost_estimate=LITTLE,
        name="slot_terms",
    )(codes, place, normed, *late, *early)
    return outputs[:chips], outputs[chips:]


def combine_kernel(kept_ref, arrived_ref, out_ref):
    rows = kept_ref.shape[0]
    arrived = read_message(arrived_ref, rows)

    def total(group):
        return kept_ref[group * GROUP : (group + 1) * GROUP, :] + arrived(group)

    if out_ref.dtype == jnp.int16:
        write_message(out_ref, rows, total)
    else:
        for group in range(rows // GROUP):
            out_ref[group * GROUP : (group + 1) * GROUP, :] = total(group)


def combine(kept, arrived, kind):
    shape = arrived.shape if kind == jnp.int16 else kept.shape
    return pl.pallas_call(
        combine_kernel,
        in_specs=[VMEM, VMEM],
        out_specs=VMEM,
        out_shape=jax.ShapeDtypeStruct(shape, kind),
        compiler_params=params(5),
        cost_estimate=LITTLE,
        name="combine",
    )(kept, arrived)


def update_kernel(count, *refs):
    kept_ref, out_ref = refs[0], refs[-1]
    tile = out_ref.shape[-1]
    arrived = [read_message(ref, kept_ref.shape[0]) for ref in refs[1 : 1 + count]]
    for slot in range(out_ref.shape[0]):
        total = kept_ref[slot * tile : (slot + 1) * tile, :]
        for block in arrived:
            total = total + block(slot)
        mean = jnp.sum(total * total) / (tile * tile)
        out_ref[slot] = (total * lax.rsqrt(mean + 1e-06)).T.astype(out_ref.dtype)


def normalized_update(kept, arrived, shape):
    return pl.pallas_call(
        functools.partial(update_kernel, len(arrived)),
        in_specs=[VMEM] * (1 + len(arrived)),
        out_specs=VMEM,
        out_shape=jax.ShapeDtypeStruct(shape, jnp.bfloat16),
        compiler_params=params(6),
        cost_estimate=LITTLE,
        name="normalized_update",
    )(kept, *arrived)


def grad_input_kernel(place_ref, weight_ref, own, a1, b1, e2, m2, d3, out_ref, cotangent):
    @pl.when(pl.program_id(0) == 0)
    def _():
        tokens, width = own.shape
        for chunk, refs in zip(chunk_order(place_ref[0]), ((own,), (a1,), (b1, e2), (m2, d3))):
            cotangent[:, aligned(chunk, width)] = joined(tokens, refs)

    out_ref[...] = lax.dot_general(
        cotangent[...],
        weight_ref[...],
        (((1,), (1,)), ((), ())),
        preferred_element_type=jnp.float32,
    ).astype(out_ref.dtype)


def grad_inputs(place, features, weight, *chunks):
    width = weight.shape[1]
    tokens = chunks[0].shape[0]
    block = 512
    return pl.pallas_call(
        grad_input_kernel,
        grid_spec=pltpu.PrefetchScalarGridSpec(
            num_scalar_prefetch=1,
            grid=(features // block,),
            in_specs=[pl.BlockSpec((block, width), lambda i, p: (i, 0))]
            + [VMEM] * len(chunks),
            out_specs=pl.BlockSpec((tokens, block), lambda i, p: (0, i)),
            scratch_shapes=[pltpu.VMEM((tokens, width), jnp.bfloat16)],
        ),
        out_shape=jax.ShapeDtypeStruct((tokens, features), jnp.bfloat16),
        compiler_params=params(14),
        cost_estimate=pl.CostEstimate(
            flops=2 * tokens * features * width,
            bytes_accessed=12 * MIB,
            transcendentals=0,
        ),
        name="grad_inputs",
    )(place, weight, *chunks)


def local(devices, parts, normed, tile_values, tile_rows, tile_columns, cotangent):
    capacity, tile = tile_values.shape[1], tile_values.shape[-1]
    column_blocks = cotangent.shape[1] * parts // tile
    chips = devices // 2
    rows = capacity * tile
    place = lax.axis_index("tensor").astype(jnp.int32).reshape(1)

    def swap(x, mask):
        return lax.ppermute(x, "fsdp", [(i, i ^ mask) for i in range(devices)])

    def pairs(x):
        return lax.ppermute(x, "tensor", [(0, 1), (1, 0), (2, 3), (3, 2)])

    def middle(x):
        return lax.ppermute(x, "tensor", [(1, 2), (2, 1)])

    def outward(x):
        return lax.ppermute(x, "tensor", [(1, 0), (2, 3)])

    def inward(x):
        return lax.ppermute(x, "tensor", [(0, 1), (3, 2)])

    positions = jnp.where(tile_columns >= 0, tile_rows * column_blocks + tile_columns + 1, 0)
    positions = jnp.pad(positions.astype(jnp.bfloat16), ((0, PAD - 1), (0, tile - capacity)))
    message = jnp.concatenate([tile_values.reshape(rows, tile), positions], axis=0)
    wider, wide = widen(cotangent, 2 * PAD, PAD)
    a1, b1 = pairs(wider), middle(wide)
    normed, g1 = own_gradient(normed, cotangent)
    same_core = [message] + [swap(message, 2 * chip) for chip in range(1, chips)]
    beside = swap(message, 1)
    a1, b1, _, _ = lax.optimization_barrier((a1, b1, g1, beside))
    m2, e2 = middle(a1), outward(b1)
    g2 = chunk_gradient(normed, a1)
    *same_core, _ = lax.optimization_barrier((*same_core, g2))
    gathered = [same_core[0], beside]
    for m in same_core[1:]:
        gathered += [m, swap(m, 1)]

    weight, codes = assembled(gathered, normed.shape[1], column_blocks)
    m2, e2, codes = lax.optimization_barrier((m2, e2, codes))
    d3 = outward(m2)
    first = first_values(place, normed, weight, parts)
    arrived = inward(first)
    codes, _ = lax.optimization_barrier((codes, first))
    partial, second = partial_values(place, normed, weight, first.shape)
    g3 = chunk_gradient(normed, b1, e2)
    codes, _, _ = lax.optimization_barrier((codes, g3, second))
    keep, send = slot_terms(codes, place, normed, (m2, d3), (g1, g2, g3), capacity, column_blocks)
    arrived, send = lax.optimization_barrier((arrived, send))

    to_middle = inward(second)
    crossing = middle(hop(lambda p: p ^ 2, place, partial, arrived))
    other = [swap(m, 1) for m in send]
    sums = [combine(keep[chip], other[chip], jnp.int16) for chip in range(1, chips)]
    own = combine(keep[0], other[0], jnp.float32)
    crossing, to_middle, _, _ = lax.optimization_barrier((crossing, to_middle, own, sums))
    terms = [swap(m, 2 * chip) for chip, m in reversed(list(enumerate(sums, 1)))]

    by_pair = pairs(hop(lambda p: p ^ 1, place, partial, crossing))
    by_middle = middle(hop(lambda p: 3 - p, place, partial, to_middle))
    grad_input = grad_inputs(place, normed.shape[1], weight, cotangent, a1, b1, e2, m2, d3)
    update = normalized_update(own, terms, tile_values.shape[1:])
    by_pair, by_middle, _ = lax.optimization_barrier((by_pair, by_middle, update))
    values = last_hop(place, partial, by_pair, by_middle)
    return values, grad_input, update[None]


def solution(mesh):
    in_specs = (
        P("fsdp", "tensor"),
        P("tensor", "fsdp", None, None),
        P("tensor", "fsdp"),
        P("tensor", "fsdp"),
        P("fsdp", "tensor"),
    )
    out_specs = (P("fsdp", "tensor"), P("fsdp", "tensor"), P("tensor", "fsdp", None, None))
    return jax.shard_map(
        functools.partial(local, mesh.shape["fsdp"], mesh.shape["tensor"]),
        mesh=mesh,
        in_specs=in_specs,
        out_specs=out_specs,
        check_vma=False,
    )
```
